32 devices in a mesh: tri: 8 (over y, x, core), vp: 4 (over z).
Axes of the slice: x: 2, y: 2, z: 4, core: 2. Of those that a mesh axis runs over, the one named last changes fastest.
Arguments:
- amplitudes: bfloat16 [2, 7680, 512], P(None, 'tri', 'vp'), may hold values from -6 to 6
- integrals: bfloat16 [7680, 512], P('tri', 'vp'), may hold values from -0.0029296875 to 0.0029296875
- ladder_blocks: bfloat16 [56, 768, 768], P('tri'), may hold values from -0.0625 to 0.0625
- slot_block: int32 [56], P('tri'), may hold values from 0 to 55, each once
Outputs:
- section_amplitudes: bfloat16 [2, 7680, 512], P(None, 'tri', 'vp')
The draws below stay inside these ranges and needn't reach their ends.
Inputs may be any that keep to these rules, and one draw needn't show every extreme that they name: `slot_block`: each value below 55 names a triangle block and stands exactly once; values of 55 or more mark empty slots.
All inputs are finite; a program needn't handle non-finite values.
Results may differ from the reference program's by a relative error of at most 0.0085.
Values may be sent and summed in bfloat16 or wider, within the bound.
No kernel may reach another device: no remote copies, remote signals or barrier semaphores. Data moves between devices by JAX's collectives and lax.ppermute only.
A program may use at most 128 MiB of HBM per device.

```python
import jax
import jax.numpy as jnp
import numpy as np
from jax import lax

NB = 10
BLOCK = 768
PAIRS = 7680
PANEL = 512
TRI_BLOCKS = 55
SLOTS = 7
TRI_SLOTS = 56
N_TRI = 8


def block_levels(rng, extent, pieces, low, top_value):
    def one(dim, blocks):
        heights = jax.random.uniform(jax.random.fold_in(jax.random.fold_in(rng, 6), dim), (blocks,), jnp.float32, low / len(pieces), top_value / len(pieces))
        return jnp.repeat(jnp.exp(heights), extent[dim] // blocks).reshape((-1,) + (1,) * (len(extent) - dim - 1))

    loudness = one(*pieces[0])
    for cut in pieces[1:]:
        loudness = loudness * one(*cut)
    return loudness


def centred(key, shape, width, most, split=(), held_as=jnp.bfloat16):
    values = width * jax.random.normal(key, shape, jnp.float32)
    if split:
        values = values * block_levels(key, shape, split, -0.22, 0.18)
    return jnp.clip(values, -most, most).astype(held_as)


def setup_inputs(seed: int = 0) -> dict:
    arg_keys = jax.random.split(jax.random.key(seed), 5)
    return {
        "amplitudes": centred(arg_keys[0], (2, PAIRS, PANEL), 1.0, 6.0, ((1, 8), (2, 4))),
        "integrals": centred(arg_keys[1], (PAIRS, PANEL), (PAIRS * PANEL) ** -0.5, 0.0029296875, ((0, 8), (1, 4))),
        "ladder_blocks": centred(arg_keys[2], (TRI_SLOTS, BLOCK, BLOCK), PAIRS ** -0.5, 0.0625, ((0, 8),)),
        "slot_block": jax.random.permutation(arg_keys[3], TRI_SLOTS).astype(jnp.int32),
    }


def triangle_tables(block_count):
    row_list = []
    column_list = []
    for row_index in range(block_count):
        for column_index in range(row_index, block_count):
            row_list.append(row_index)
            column_list.append(column_index)
    return np.array(row_list, np.int32), np.array(column_list, np.int32)


def decode(code):
    row_table, column_table = triangle_tables(NB)
    match = code == jnp.arange(TRI_BLOCKS, dtype=jnp.int32)
    row_block = jnp.sum(jnp.where(match, jnp.asarray(row_table), 0)).astype(jnp.int32)
    column_block = jnp.sum(jnp.where(match, jnp.asarray(column_table), 0)).astype(jnp.int32)
    filled = (code < TRI_BLOCKS).astype(jnp.float32)
    return row_block, column_block, filled


def symmetrize(block, row_block, column_block):
    values = block.astype(jnp.float32)
    diagonal = (row_block == column_block).astype(jnp.float32)
    return (values + diagonal * (0.5 * (values + values.T) - values)).astype(jnp.bfloat16)


def apply_block(partial_value, ladder_real, amp_row, amp_column, row_block, column_block, filled):
    def mult(weights, vectors):
        return jnp.dot(weights, vectors, preferred_element_type=jnp.float32)
    to_row = jnp.stack([mult(ladder_real, amp_column[0]), mult(ladder_real, amp_column[1])])
    to_column = jnp.stack([mult(ladder_real.T, amp_row[0]), mult(ladder_real.T, amp_row[1])])
    off_diagonal = filled * (row_block < column_block).astype(jnp.float32)
    start_row = (row_block * BLOCK).astype(jnp.int32)
    current = lax.dynamic_slice_in_dim(partial_value, start_row, BLOCK, 1)
    partial_value = lax.dynamic_update_slice_in_dim(partial_value, current + filled * to_row, start_row, 1)
    start_column = (column_block * BLOCK).astype(jnp.int32)
    current = lax.dynamic_slice_in_dim(partial_value, start_column, BLOCK, 1)
    return lax.dynamic_update_slice_in_dim(partial_value, current + off_diagonal * to_column, start_column, 1)


def reference(amplitudes, integrals, ladder_blocks, slot_block):
    def device_term(tri_index, total):
        partial_value = jnp.zeros((2, PAIRS, PANEL), jnp.float32)
        for slot_index in range(SLOTS):
            flat_index = (tri_index * SLOTS + slot_index).astype(jnp.int32)
            code = lax.dynamic_index_in_dim(slot_block, flat_index, 0, keepdims=False)
            row_block, column_block, filled = decode(code)
            start_row = (row_block * BLOCK).astype(jnp.int32)
            start_column = (column_block * BLOCK).astype(jnp.int32)
            amp_row = lax.dynamic_slice_in_dim(amplitudes, start_row, BLOCK, 1)
            amp_column = lax.dynamic_slice_in_dim(amplitudes, start_column, BLOCK, 1)
            block = lax.dynamic_index_in_dim(ladder_blocks, flat_index, 0, keepdims=False)
            symmetric = symmetrize(block, row_block, column_block)
            partial_value = apply_block(partial_value, symmetric, amp_row, amp_column,
                                  row_block, column_block, filled)
        rounded = lax.optimization_barrier(partial_value.astype(jnp.bfloat16))
        return total + rounded.astype(jnp.float32)

    ladder_term = lax.fori_loop(0, N_TRI, device_term, jnp.zeros((2, PAIRS, PANEL), jnp.float32))

    def mult(left, right):
        return jnp.dot(left, right, preferred_element_type=jnp.float32)

    contracted_real = mult(integrals.T, amplitudes[0]).astype(jnp.bfloat16)
    contracted_imag = mult(integrals.T, amplitudes[1]).astype(jnp.bfloat16)
    quad_real = 0.5 * (mult(amplitudes[0], contracted_real) - mult(amplitudes[1], contracted_imag))
    quad_imag = 0.5 * (mult(amplitudes[0], contracted_imag) + mult(amplitudes[1], contracted_real))
    ladder_term = ladder_term + jnp.stack([quad_real, quad_imag])
    start_values = amplitudes.astype(jnp.float32)
    section_real = start_values[0] + 0.5 * ladder_term[1]
    section_imag = start_values[1] - 0.5 * ladder_term[0]
    return jnp.stack([section_real, section_imag]).astype(jnp.bfloat16)
```

```python
import functools

import jax
import jax.numpy as jnp
from jax import lax
from jax.experimental import pallas as pl
from jax.experimental.pallas import tpu as pltpu
from jax.sharding import PartitionSpec as P

NB = 10
BLOCK = 768
PAIRS = NB * BLOCK
TRI_BLOCKS = NB * (NB + 1) // 2
F32 = jnp.float32
BF16 = jnp.bfloat16


def swap(value, axis_size, bit):
    pairs = [(i, i ^ (1 << bit)) for i in range(axis_size)]
    return lax.ppermute(value, "tri", pairs)


def bit_orders(bits):
    outer = list(range(1, bits))
    return outer, outer[1:] + outer[:1]


def place_index(mask, order):
    index = 0
    for bit in order:
        index = 2 * index + ((mask >> bit) & 1)
    return index


def gather_pieces(piece, axis_size, order):
    pieces = {0: piece}
    for bit in order:
        for mask in list(pieces):
            pieces[mask | (1 << bit)] = swap(pieces[mask], axis_size, bit)
    return pieces


def ladder_kernel(tri_size, orders, me_ref, code_ref, *refs):
    count = 2 * tri_size
    piece_refs = refs[:count]
    ladder_ref = refs[count]
    keep_refs = refs[count + 1:count + 3]
    send_refs = refs[count + 3:count + 5]
    amp, acc, sems = refs[count + 5:]
    rows, columns = piece_refs[0].shape
    step = pl.program_id(0)
    me = me_ref[0]

    def rows_of(mask):
        return pl.ds(pl.multiple_of((me ^ mask) * rows, rows), rows)

    @pl.when(step == 0)
    def _():
        copies = []
        for part in range(2):
            for mask in range(tri_size):
                index = part * tri_size + mask
                copy = pltpu.make_async_copy(
                    piece_refs[index],
                    amp.at[rows_of(mask), pl.ds(part * columns, columns)],
                    sems.at[index],
                )
                copy.start()
                copies.append(copy)
        acc[...] = jnp.zeros_like(acc)
        for copy in copies:
            copy.wait()

    code = code_ref[step]
    row_block = jnp.int32(0)
    start = jnp.int32(0)
    for row in range(1, NB):
        first = row * NB - row * (row - 1) // 2
        past = code >= first
        row_block = jnp.where(past, row, row_block)
        start = jnp.where(past, first, start)
    column_block = jnp.minimum(row_block + code - start, NB - 1)
    weight = jnp.where(row_block == column_block, 0.5, 1.0) * jnp.where(code < TRI_BLOCKS, 1.0, 0.0)
    at_row = pl.ds(pl.multiple_of(row_block * BLOCK, BLOCK), BLOCK)
    at_column = pl.ds(pl.multiple_of(column_block * BLOCK, BLOCK), BLOCK)
    block = ladder_ref[0]
    to_row = lax.dot_general(block, amp[at_column, :], (((1,), (0,)), ((), ())), preferred_element_type=F32)
    acc[at_row, :] += weight * to_row
    to_column = lax.dot_general(block, amp[at_row, :], (((0,), (0,)), ((), ())), preferred_element_type=F32)
    acc[at_column, :] += weight * to_column

    @pl.when(step == pl.num_programs(0) - 1)
    def _():
        for part in range(2):
            lanes = slice(part * columns, (part + 1) * columns)
            for mask in range(tri_size):
                target = send_refs[part] if mask & 1 else keep_refs[part]
                target[place_index(mask, orders[part])] = acc[rows_of(mask), lanes].astype(BF16)


def ladder(me, codes, pieces, ladder_blocks, tri_size, orders):
    slots = ladder_blocks.shape[0]
    rows, columns = pieces[0].shape
    half = jax.ShapeDtypeStruct((tri_size // 2, rows, columns), BF16)
    whole = pl.BlockSpec((tri_size // 2, rows, columns), lambda s, *_: (0, 0, 0))
    return pl.pallas_call(
        functools.partial(ladder_kernel, tri_size, orders),
        grid_spec=pltpu.PrefetchScalarGridSpec(
            num_scalar_prefetch=2,
            grid=(slots,),
            in_specs=[pl.BlockSpec(memory_space=pl.ANY)] * (2 * tri_size)
            + [pl.BlockSpec((1, BLOCK, BLOCK), lambda s, *_: (s, 0, 0))],
            out_specs=[whole] * 4,
            scratch_shapes=[
                pltpu.VMEM((PAIRS, 2 * columns), BF16),
                pltpu.VMEM((PAIRS, 2 * columns), F32),
                pltpu.SemaphoreType.DMA((2 * tri_size,)),
            ],
        ),
        out_shape=[half] * 4,
        compiler_params=pltpu.CompilerParams(
            dimension_semantics=("arbitrary",), vmem_limit_bytes=48 * 1024 * 1024
        ),
        cost_estimate=pl.CostEstimate(
            flops=slots * 8 * BLOCK * BLOCK * columns,
            bytes_accessed=slots * BLOCK * BLOCK * 2 + 8 * PAIRS * columns,
            transcendentals=0,
        ),
        name="ladder",
    )(me, codes, *pieces, ladder_blocks)


def add(*terms):
    total = terms[0].astype(F32)
    for term in terms[1:]:
        total = total + term.astype(F32)
    return total


def scatter_sum(keep, send, tri_size, order):
    terms = [keep, swap(send, tri_size, 0)]
    for bit in order:
        half = terms[0].shape[0] // 2
        outgoing = add(*[term[half:] for term in terms]).astype(BF16)
        terms = [term[:half] for term in terms] + [swap(outgoing, tri_size, bit)]
    return add(*[term[0] for term in terms])


def shards(tri_size, vp_size, amplitudes, integrals, ladder_blocks, slot_block):
    bits = tri_size.bit_length() - 1
    orders = bit_orders(bits)
    me = lax.axis_index("tri").astype(jnp.int32)

    pieces = []
    for part in range(2):
        got = gather_pieces(amplitudes[part], tri_size, orders[part] + [0])
        pieces += [got[mask] for mask in range(tri_size)]

    ring = [(i, (i + 1) % vp_size) for i in range(vp_size)]
    ints = [integrals]
    for _ in range(vp_size - 1):
        ints.append(lax.ppermute(ints[-1], "vp", ring))
    amps = [amplitudes]
    for _ in range(vp_size - 1):
        amps.append(lax.ppermute(amps[-1], "vp", ring))

    contracted = jnp.stack(
        [
            jnp.stack(
                [
                    lax.dot_general(value, amplitudes[part], (((0,), (0,)), ((), ())), preferred_element_type=F32)
                    for value in ints
                ]
            ).astype(BF16)
            for part in range(2)
        ]
    )
    summed = []
    for part in range(2):
        value = contracted[part]
        for bit in [0] + orders[part]:
            value = add(value, swap(value, tri_size, bit)).astype(BF16)
        summed.append(value)
    quad_real = jnp.zeros(amplitudes.shape[1:], F32)
    quad_imag = jnp.zeros(amplitudes.shape[1:], F32)

    def mult(left, right):
        return jnp.dot(left, right, preferred_element_type=F32)

    for step in range(vp_size):
        real, imag = amps[step][0], amps[step][1]
        c_real, c_imag = summed[0][step], summed[1][step]
        quad_real += mult(real, c_real) - mult(imag, c_imag)
        quad_imag += mult(real, c_imag) + mult(imag, c_real)

    keep_real, keep_imag, send_real, send_imag = ladder(
        me[None], slot_block, pieces, ladder_blocks, tri_size, orders
    )
    sum_real = scatter_sum(keep_real, send_real, tri_size, orders[0])
    sum_imag = scatter_sum(keep_imag, send_imag, tri_size, orders[1])
    section_real = amplitudes[0].astype(F32) + 0.5 * (sum_imag + 0.5 * quad_imag)
    section_imag = amplitudes[1].astype(F32) - 0.5 * (sum_real + 0.5 * quad_real)
    return jnp.stack([section_real, section_imag]).astype(BF16)


def solution(mesh):
    in_specs = (P(None, "tri", "vp"), P("tri", "vp"), P("tri", None, None), P("tri"))
    out_specs = P(None, "tri", "vp")
    body = functools.partial(shards, mesh.shape["tri"], mesh.shape["vp"])
    return jax.shard_map(body, mesh=mesh, in_specs=in_specs, out_specs=out_specs, check_vma=False)
```

```python
import functools

import jax
import jax.numpy as jnp
from jax import lax
from jax.experimental import pallas as pl
from jax.experimental.pallas import tpu as pltpu
from jax.sharding import PartitionSpec as P

NB = 10
BLOCK = 768
PAIRS = NB * BLOCK
TRI_BLOCKS = NB * (NB + 1) // 2
F32 = jnp.float32
BF16 = jnp.bfloat16


def swap(value, axis_size, bit):
    pairs = [(i, i ^ (1 << bit)) for i in range(axis_size)]
    return lax.ppermute(value, "tri", pairs)


def after(value, *earlier):
    return lax.optimization_barrier((value, *earlier))[0]


def gather_tri(amplitudes, axis_size):
    if axis_size != 8:
        found = {0: amplitudes}
        for bit in range(axis_size.bit_length() - 1):
            for mask in list(found):
                found[mask | (1 << bit)] = swap(found[mask], axis_size, bit)
        return [(value, mask, None) for mask, value in found.items()]
    by_x = swap(amplitudes, axis_size, 1)
    by_y = swap(amplitudes, axis_size, 2)
    own_core = swap(amplitudes, axis_size, 0)
    far_real = swap(by_y[0], axis_size, 1)
    far_imag = swap(by_x[1], axis_size, 2)
    found = [
        (amplitudes, 0, None), (by_x, 2, None), (by_y, 4, None), (far_real, 6, 0), (far_imag, 6, 1),
        (own_core, 1, None),
    ]
    for value, mask, part in found[1:5]:
        found.append((swap(value, axis_size, 0), mask | 1, part))
    return found


def ladder_kernel(labels, groups, me_ref, code_ref, *refs):
    count = len(labels)
    piece_refs = refs[:count]
    ladder_ref = refs[count]
    out_refs = refs[count + 1:-3]
    amp, acc, sems = refs[-3:]
    columns = amp.shape[1] // 2
    rows = out_refs[0].shape[-2]
    step = pl.program_id(0)
    me = me_ref[0]

    def rows_of(mask):
        return pl.ds(pl.multiple_of((me ^ mask) * rows, rows), rows)

    @pl.when(step == 0)
    def _():
        copies = []
        for index, (mask, part) in enumerate(labels):
            for which in (0, 1) if part is None else (part,):
                source = piece_refs[index].at[which] if part is None else piece_refs[index]
                lanes = pl.ds(which * columns, columns)
                copy = pltpu.make_async_copy(source, amp.at[rows_of(mask), lanes], sems.at[len(copies)])
                copy.start()
                copies.append(copy)
        acc[...] = jnp.zeros_like(acc)
        for copy in copies:
            copy.wait()

    code = code_ref[step]
    row_block = jnp.int32(0)
    start = jnp.int32(0)
    for row in range(1, NB):
        first = row * NB - row * (row - 1) // 2
        past = code >= first
        row_block = jnp.where(past, row, row_block)
        start = jnp.where(past, first, start)
    column_block = jnp.minimum(row_block + code - start, NB - 1)
    weight = jnp.where(row_block == column_block, 0.5, 1.0) * jnp.where(code < TRI_BLOCKS, 1.0, 0.0)
    at_row = pl.ds(pl.multiple_of(row_block * BLOCK, BLOCK), BLOCK)
    at_column = pl.ds(pl.multiple_of(column_block * BLOCK, BLOCK), BLOCK)
    block = ladder_ref[0]
    to_row = lax.dot_general(block, amp[at_column, :], (((1,), (0,)), ((), ())), preferred_element_type=F32)
    acc[at_row, :] += weight * to_row
    to_column = lax.dot_general(block, amp[at_row, :], (((0,), (0,)), ((), ())), preferred_element_type=F32)
    acc[at_column, :] += weight * to_column

    @pl.when(step == pl.num_programs(0) - 1)
    def _():
        for target, places in zip(out_refs, groups, strict=True):
            for place, (mask, part) in enumerate(places):
                lanes = slice(part * columns, (part + 1) * columns)
                target[place] = acc[rows_of(mask), lanes].astype(BF16)


def ladder(me, codes, pieces, ladder_blocks, groups):
    slots = ladder_blocks.shape[0]
    rows, columns = pieces[0][0].shape[-2:]
    count = sum(len(places) for places in groups)
    return pl.pallas_call(
        functools.partial(ladder_kernel, [(mask, part) for _, mask, part in pieces], groups),
        grid_spec=pltpu.PrefetchScalarGridSpec(
            num_scalar_prefetch=2,
            grid=(slots,),
            in_specs=[pl.BlockSpec(memory_space=pl.ANY)] * len(pieces)
            + [pl.BlockSpec((1, BLOCK, BLOCK), lambda s, *_: (s, 0, 0))],
            out_specs=[pl.BlockSpec((len(places), rows, columns), lambda s, *_: (0, 0, 0)) for places in groups],
            scratch_shapes=[
                pltpu.VMEM((PAIRS, 2 * columns), BF16),
                pltpu.VMEM((PAIRS, 2 * columns), F32),
                pltpu.SemaphoreType.DMA((count,)),
            ],
        ),
        out_shape=[jax.ShapeDtypeStruct((len(places), rows, columns), BF16) for places in groups],
        compiler_params=pltpu.CompilerParams(
            dimension_semantics=("arbitrary",), vmem_limit_bytes=40 * 1024 * 1024
        ),
        cost_estimate=pl.CostEstimate(flops=1, bytes_accessed=1, transcendentals=0),
        name="ladder",
    )(me, codes, *[value for value, _, _ in pieces], ladder_blocks)


def add(*terms):
    total = terms[0].astype(F32)
    for term in terms[1:]:
        total = total + term.astype(F32)
    return total


def contract_kernel(me_ref, int_ref, real_ref, imag_ref, hold_ref, give_ref):
    vp_size, _, columns = real_ref.shape
    values = int_ref[...]
    for step in range(vp_size):
        target = lax.rem(me_ref[1] + step, vp_size)
        both = jnp.concatenate([real_ref[target], imag_ref[target]], axis=1)
        product = lax.dot_general(values, both, (((0,), (0,)), ((), ())), preferred_element_type=F32)
        real = product[:, :columns].astype(BF16)
        imag = product[:, columns:].astype(BF16)
        hold_ref[step] = jnp.where(me_ref[0] == 0, real, imag)
        give_ref[step] = jnp.where(me_ref[0] == 0, imag, real)


def contract(me, integrals, wide_real, wide_imag):
    vp_size, rows, columns = wide_real.shape
    vmem = pl.BlockSpec(memory_space=pltpu.VMEM)
    return pl.pallas_call(
        contract_kernel,
        in_specs=[pl.BlockSpec(memory_space=pltpu.SMEM)] + [vmem] * 3,
        out_specs=[vmem] * 2,
        out_shape=[jax.ShapeDtypeStruct((vp_size, columns, columns), BF16)] * 2,
        compiler_params=pltpu.CompilerParams(vmem_limit_bytes=24 * 1024 * 1024),
        cost_estimate=pl.CostEstimate(
            flops=4 * vp_size * rows * columns * columns,
            bytes_accessed=4 * wide_real.size + 2 * integrals.size,
            transcendentals=0,
        ),
        name="contract",
    )(me, integrals, wide_real, wide_imag)


def quadratic_kernel(me_ref, amp_ref, real_ref, imag_ref, mine_ref, other_ref, out_ref):
    vp_size, rows, columns = real_ref.shape
    core = me_ref[0]
    total = jnp.zeros((rows, 2 * columns), F32)
    for step in range(vp_size):
        source = lax.rem(me_ref[1] + vp_size - step, vp_size)
        both = jnp.concatenate([real_ref[source], imag_ref[source]], axis=1)
        real = jnp.where(core == 0, mine_ref[step], other_ref[step])
        imag = jnp.where(core == 0, other_ref[step], mine_ref[step])
        weights = jnp.concatenate(
            [jnp.concatenate([real, imag], axis=1), jnp.concatenate([-imag, real], axis=1)], axis=0
        )
        total += jnp.dot(both, weights, preferred_element_type=F32)
    out_ref[0] = amp_ref[0].astype(F32) + 0.25 * total[:, columns:]
    out_ref[1] = amp_ref[1].astype(F32) - 0.25 * total[:, :columns]


def quadratic(me, amplitudes, wide_real, wide_imag, mine, other):
    vmem = pl.BlockSpec(memory_space=pltpu.VMEM)
    return pl.pallas_call(
        quadratic_kernel,
        in_specs=[pl.BlockSpec(memory_space=pltpu.SMEM)] + [vmem] * 5,
        out_specs=vmem,
        out_shape=jax.ShapeDtypeStruct(amplitudes.shape, F32),
        compiler_params=pltpu.CompilerParams(vmem_limit_bytes=24 * 1024 * 1024),
        cost_estimate=pl.CostEstimate(
            flops=8 * wide_real.size * amplitudes.shape[2],
            bytes_accessed=4 * wide_real.size + 4 * amplitudes.size,
            transcendentals=0,
        ),
        name="quadratic",
    )(me, amplitudes, wide_real, wide_imag, mine, other)


def finish_kernel(places, base_ref, *refs):
    sums = [0.0, 0.0]
    for ref, (_, part, place) in zip(refs, places, strict=False):
        sums[part] = sums[part] + ref[place].astype(F32)
    refs[-1][0] = (base_ref[0] + 0.5 * sums[1]).astype(BF16)
    refs[-1][1] = (base_ref[1] - 0.5 * sums[0]).astype(BF16)


def finish(base, terms):
    vmem = pl.BlockSpec(memory_space=pltpu.VMEM)
    return pl.pallas_call(
        functools.partial(finish_kernel, [(None, part, place) for _, part, place in terms]),
        in_specs=[vmem] * (1 + len(terms)),
        out_specs=vmem,
        out_shape=jax.ShapeDtypeStruct(base.shape, BF16),
        compiler_params=pltpu.CompilerParams(vmem_limit_bytes=24 * 1024 * 1024),
        name="finish",
    )(base, *[value for value, _, _ in terms])


def scatter_plain(partial, tri_size):
    terms = [partial]
    for bit in reversed(range(tri_size.bit_length() - 1)):
        half = terms[0].shape[0] // 2
        outgoing = add(*[term[half:] for term in terms]).astype(BF16)
        terms = [term[:half] for term in terms] + [swap(outgoing, tri_size, bit)]
    return [(term[0], part, part) for term in terms for part in range(2)]


def shards(tri_size, vp_size, amplitudes, integrals, ladder_blocks, slot_block):
    bits = tri_size.bit_length() - 1
    tri_me = lax.axis_index("tri").astype(jnp.int32)
    me = jnp.stack([tri_me & 1, lax.axis_index("vp").astype(jnp.int32)])
    wide_real = lax.all_gather(amplitudes[0], "vp", axis=0, tiled=False)
    wide_imag = lax.all_gather(amplitudes[1], "vp", axis=0, tiled=False)
    pieces = gather_tri(amplitudes, tri_size)
    *values, wide_real = lax.optimization_barrier((*[value for value, _, _ in pieces], wide_real))
    pieces = [(value, mask, part) for value, (_, mask, part) in zip(values, pieces, strict=True)]

    if tri_size == 8:
        real_order, imag_order = (2, 6, 4), (4, 6, 2)
        groups = [[(mask | 1, 0) for mask in real_order], [(mask | 1, 1) for mask in imag_order], [(1, 0), (1, 1)]]
        groups += [[(mask, 0) for mask in real_order], [(mask, 1) for mask in imag_order], [(0, 0), (0, 1)]]
    else:
        groups = [[(mask, part) for mask in range(tri_size) for part in range(2)]]
    partials = ladder(tri_me[None], slot_block, pieces, ladder_blocks, groups)
    *partials, wide_real, wide_imag = lax.optimization_barrier((*partials, wide_real, wide_imag))
    hold, give = contract(me, integrals, wide_real, wide_imag)

    if tri_size == 8:
        real, imag, own = partials[3:]
        real_in, imag_in, own_in = (swap(value, tri_size, 0) for value in partials[:3])
        real_in, imag_in, hold, give = lax.optimization_barrier((real_in, imag_in, hold, give))
        by_x = add(real[:2], real_in[:2]).astype(BF16)
        by_y = add(imag[:2], imag_in[:2]).astype(BF16)
        by_x, by_y, hold, give = lax.optimization_barrier((by_x, by_y, hold, give))
        by_x, by_y = swap(by_x, tri_size, 1), swap(by_y, tri_size, 2)
        mine = add(hold, swap(give, tri_size, 0)).astype(BF16)
        mine = add(mine, swap(mine, tri_size, 1)).astype(BF16)
        received = swap(mine, tri_size, 2)
        then_y = add(real[2], real_in[2], by_x[1]).astype(BF16)
        then_x = add(imag[2], imag_in[2], by_y[1]).astype(BF16)
        then_y, then_x, received = lax.optimization_barrier((then_y, then_x, received))
        then_y, then_x = swap(then_y[None], tri_size, 2), swap(then_x[None], tri_size, 1)
        mine = add(mine, received).astype(BF16)
        terms = [(own, 0, 0), (own, 1, 1), (own_in, 0, 0), (own_in, 1, 1)]
        terms += [(by_x, 0, 0), (by_y, 1, 0), (then_y, 0, 0), (then_x, 1, 0)]
    else:
        terms = scatter_plain(partials[0].reshape(tri_size, 2, *amplitudes.shape[1:]), tri_size)
        mine = add(hold, swap(give, tri_size, 0)).astype(BF16)
        for bit in range(1, bits):
            mine = add(mine, swap(mine, tri_size, bit)).astype(BF16)
    shifted = [mine[0]]
    for step in range(1, vp_size):
        shifted.append(lax.ppermute(mine[step], "vp", [(i, (i + step) % vp_size) for i in range(vp_size)]))
    mine = jnp.stack(shifted)
    base = quadratic(me, amplitudes, wide_real, wide_imag, mine, swap(mine, tri_size, 0))
    return finish(base, terms)


def solution(mesh):
    in_specs = (P(None, "tri", "vp"), P("tri", "vp"), P("tri", None, None), P("tri"))
    out_specs = P(None, "tri", "vp")
    body = functools.partial(shards, mesh.shape["tri"], mesh.shape["vp"])
    return jax.shard_map(body, mesh=mesh, in_specs=in_specs, out_specs=out_specs, check_vma=False)
```

```python
import functools

import jax
import jax.numpy as jnp
from jax import lax
from jax.experimental import pallas as pl
from jax.experimental.pallas import tpu as pltpu
from jax.sharding import PartitionSpec as P

NB = 10
BLOCK = 768
PAIRS = NB * BLOCK
TRI_BLOCKS = NB * (NB + 1) // 2
F32 = jnp.float32
BF16 = jnp.bfloat16


def swap(value, axis_size, bit):
    pairs = [(i, i ^ (1 << bit)) for i in range(axis_size)]
    return lax.ppermute(value, "tri", pairs)


def after(value, *earlier):
    return lax.optimization_barrier((value, *earlier))[0]


def gather_tri(amplitudes, axis_size):
    if axis_size != 8:
        found = {0: amplitudes}
        for bit in range(axis_size.bit_length() - 1):
            for mask in list(found):
                found[mask | (1 << bit)] = swap(found[mask], axis_size, bit)
        return [(value, mask, None) for mask, value in found.items()]
    by_x = swap(amplitudes, axis_size, 1)
    by_y = swap(amplitudes, axis_size, 2)
    own_core = swap(amplitudes, axis_size, 0)
    far_real = swap(by_y[0], axis_size, 1)
    far_imag = swap(by_x[1], axis_size, 2)
    found = [
        (amplitudes, 0, None), (by_x, 2, None), (by_y, 4, None), (far_real, 6, 0), (far_imag, 6, 1),
        (own_core, 1, None),
    ]
    for value, mask, part in found[1:5]:
        found.append((swap(value, axis_size, 0), mask | 1, part))
    return found


def ladder_kernel(labels, groups, me_ref, code_ref, *refs):
    count = len(labels)
    piece_refs = refs[:count]
    ladder_ref = refs[count]
    out_refs = refs[count + 1:-3]
    amp, acc, sems = refs[-3:]
    columns = amp.shape[1] // 2
    rows = out_refs[0].shape[-2]
    step = pl.program_id(0)
    me = me_ref[0]

    def rows_of(mask):
        return pl.ds(pl.multiple_of((me ^ mask) * rows, rows), rows)

    @pl.when(step == 0)
    def _():
        copies = []
        for index, (mask, part) in enumerate(labels):
            for which in (0, 1) if part is None else (part,):
                source = piece_refs[index].at[which] if part is None else piece_refs[index]
                lanes = pl.ds(which * columns, columns)
                copy = pltpu.make_async_copy(source, amp.at[rows_of(mask), lanes], sems.at[len(copies)])
                copy.start()
                copies.append(copy)
        acc[...] = jnp.zeros_like(acc)
        for copy in copies:
            copy.wait()

    code = code_ref[step]
    row_block = jnp.int32(0)
    start = jnp.int32(0)
    for row in range(1, NB):
        first = row * NB - row * (row - 1) // 2
        past = code >= first
        row_block = jnp.where(past, row, row_block)
        start = jnp.where(past, first, start)
    column_block = jnp.minimum(row_block + code - start, NB - 1)
    weight = jnp.where(row_block == column_block, 0.5, 1.0) * jnp.where(code < TRI_BLOCKS, 1.0, 0.0)
    at_row = pl.ds(pl.multiple_of(row_block * BLOCK, BLOCK), BLOCK)
    at_column = pl.ds(pl.multiple_of(column_block * BLOCK, BLOCK), BLOCK)
    block = ladder_ref[0]
    to_row = lax.dot_general(block, amp[at_column, :], (((1,), (0,)), ((), ())), preferred_element_type=F32)
    acc[at_row, :] += weight * to_row
    to_column = lax.dot_general(block, amp[at_row, :], (((0,), (0,)), ((), ())), preferred_element_type=F32)
    acc[at_column, :] += weight * to_column

    @pl.when(step == pl.num_programs(0) - 1)
    def _():
        for target, places in zip(out_refs, groups, strict=True):
            for place, (mask, part) in enumerate(places):
                lanes = slice(part * columns, (part + 1) * columns)
                target[place] = acc[rows_of(mask), lanes].astype(BF16)


def ladder(me, codes, pieces, ladder_blocks, groups):
    slots = ladder_blocks.shape[0]
    rows, columns = pieces[0][0].shape[-2:]
    count = sum(len(places) for places in groups)
    return pl.pallas_call(
        functools.partial(ladder_kernel, [(mask, part) for _, mask, part in pieces], groups),
        grid_spec=pltpu.PrefetchScalarGridSpec(
            num_scalar_prefetch=2,
            grid=(slots,),
            in_specs=[pl.BlockSpec(memory_space=pl.ANY)] * len(pieces)
            + [pl.BlockSpec((1, BLOCK, BLOCK), lambda s, *_: (s, 0, 0))],
            out_specs=[pl.BlockSpec((len(places), rows, columns), lambda s, *_: (0, 0, 0)) for places in groups],
            scratch_shapes=[
                pltpu.VMEM((PAIRS, 2 * columns), BF16),
                pltpu.VMEM((PAIRS, 2 * columns), F32),
                pltpu.SemaphoreType.DMA((count,)),
            ],
        ),
        out_shape=[jax.ShapeDtypeStruct((len(places), rows, columns), BF16) for places in groups],
        compiler_params=pltpu.CompilerParams(
            dimension_semantics=("arbitrary",), vmem_limit_bytes=40 * 1024 * 1024
        ),
        cost_estimate=pl.CostEstimate(flops=1, bytes_accessed=1, transcendentals=0),
        name="ladder",
    )(me, codes, *[value for value, _, _ in pieces], ladder_blocks)


def add(*terms):
    total = terms[0].astype(F32)
    for term in terms[1:]:
        total = total + term.astype(F32)
    return total


def contract_kernel(core_ref, int_ref, *refs):
    values = int_ref[...]
    columns = values.shape[1]
    hold_ref, give_ref = refs[-2:]
    for step, ref in enumerate(refs[:-2]):
        both = jnp.concatenate([ref[0], ref[1]], axis=1)
        product = lax.dot_general(values, both, (((0,), (0,)), ((), ())), preferred_element_type=F32)
        real = product[:, :columns].astype(BF16)
        imag = product[:, columns:].astype(BF16)
        hold_ref[step] = jnp.where(core_ref[0] == 0, real, imag)
        give_ref[step] = jnp.where(core_ref[0] == 0, imag, real)


def contract(core, integrals, ring):
    rows, columns = integrals.shape
    vmem = pl.BlockSpec(memory_space=pltpu.VMEM)
    return pl.pallas_call(
        contract_kernel,
        in_specs=[pl.BlockSpec(memory_space=pltpu.SMEM)] + [vmem] * (1 + len(ring)),
        out_specs=[vmem] * 2,
        out_shape=[jax.ShapeDtypeStruct((len(ring), columns, columns), BF16)] * 2,
        compiler_params=pltpu.CompilerParams(vmem_limit_bytes=20 * 1024 * 1024),
        cost_estimate=pl.CostEstimate(
            flops=4 * len(ring) * rows * columns * columns,
            bytes_accessed=(4 * len(ring) + 2) * rows * columns,
            transcendentals=0,
        ),
        name="contract",
    )(core, integrals, *ring)


def quadratic_kernel(core_ref, mine_ref, other_ref, *refs):
    amp_ref, out_ref = refs[0], refs[-1]
    _, rows, columns = amp_ref.shape
    vp_size = len(refs) - 1
    core = core_ref[0]
    total = jnp.zeros((rows, 2 * columns), F32)
    for step in range(vp_size):
        both = jnp.concatenate([refs[step][0], refs[step][1]], axis=1)
        source = (vp_size - step) % vp_size
        real = jnp.where(core == 0, mine_ref[source], other_ref[source])
        imag = jnp.where(core == 0, other_ref[source], mine_ref[source])
        weights = jnp.concatenate(
            [jnp.concatenate([real, imag], axis=1), jnp.concatenate([-imag, real], axis=1)], axis=0
        )
        total += jnp.dot(both, weights, preferred_element_type=F32)
    out_ref[0] = amp_ref[0].astype(F32) + 0.25 * total[:, columns:]
    out_ref[1] = amp_ref[1].astype(F32) - 0.25 * total[:, :columns]


def quadratic(core, ring, mine, other):
    vmem = pl.BlockSpec(memory_space=pltpu.VMEM)
    size = ring[0].size
    return pl.pallas_call(
        quadratic_kernel,
        in_specs=[pl.BlockSpec(memory_space=pltpu.SMEM)] + [vmem] * (2 + len(ring)),
        out_specs=vmem,
        out_shape=jax.ShapeDtypeStruct(ring[0].shape, F32),
        compiler_params=pltpu.CompilerParams(vmem_limit_bytes=20 * 1024 * 1024),
        cost_estimate=pl.CostEstimate(
            flops=4 * len(ring) * size * ring[0].shape[2],
            bytes_accessed=(2 * len(ring) + 4) * size,
            transcendentals=0,
        ),
        name="quadratic",
    )(core, mine, other, *ring)


def finish_kernel(places, base_ref, *refs):
    sums = [0.0, 0.0]
    for ref, (_, part, place) in zip(refs, places, strict=False):
        sums[part] = sums[part] + ref[place].astype(F32)
    refs[-1][0] = (base_ref[0] + 0.5 * sums[1]).astype(BF16)
    refs[-1][1] = (base_ref[1] - 0.5 * sums[0]).astype(BF16)


def finish(base, terms):
    vmem = pl.BlockSpec(memory_space=pltpu.VMEM)
    return pl.pallas_call(
        functools.partial(finish_kernel, [(None, part, place) for _, part, place in terms]),
        in_specs=[vmem] * (1 + len(terms)),
        out_specs=vmem,
        out_shape=jax.ShapeDtypeStruct(base.shape, BF16),
        compiler_params=pltpu.CompilerParams(vmem_limit_bytes=24 * 1024 * 1024),
        name="finish",
    )(base, *[value for value, _, _ in terms])


def scatter_plain(partial, tri_size):
    terms = [partial]
    for bit in reversed(range(tri_size.bit_length() - 1)):
        half = terms[0].shape[0] // 2
        outgoing = add(*[term[half:] for term in terms]).astype(BF16)
        terms = [term[:half] for term in terms] + [swap(outgoing, tri_size, bit)]
    return [(term[0], part, part) for term in terms for part in range(2)]


def shards(tri_size, vp_size, amplitudes, integrals, ladder_blocks, slot_block):
    bits = tri_size.bit_length() - 1
    me = lax.axis_index("tri").astype(jnp.int32)[None]
    core = me & 1

    def turn(value, distance=1):
        return lax.ppermute(value, "vp", [(i, (i + distance) % vp_size) for i in range(vp_size)])

    ring = [amplitudes]
    for _ in range(1, vp_size - 1):
        ring.append(turn(ring[-1]))
    pieces = gather_tri(amplitudes, tri_size)
    *values, ring[-1] = lax.optimization_barrier((*[value for value, _, _ in pieces], ring[-1]))
    pieces = [(value, mask, part) for value, (_, mask, part) in zip(values, pieces, strict=True)]
    ring.append(turn(ring[-1]))

    if tri_size == 8:
        real_order, imag_order = (2, 6, 4), (4, 6, 2)
        groups = [[(mask | 1, 0) for mask in real_order], [(mask | 1, 1) for mask in imag_order], [(1, 0), (1, 1)]]
        groups += [[(mask, 0) for mask in real_order], [(mask, 1) for mask in imag_order], [(0, 0), (0, 1)]]
    else:
        groups = [[(mask, part) for mask in range(tri_size) for part in range(2)]]
    partials = ladder(me, slot_block, pieces, ladder_blocks, groups)
    *partials, ring[-1] = lax.optimization_barrier((*partials, ring[-1]))
    hold, give = contract(core, integrals, ring)

    if tri_size == 8:
        real, imag, own = partials[3:]
        real_in, imag_in, own_in = (swap(value, tri_size, 0) for value in partials[:3])
        real_in, imag_in, hold, give = lax.optimization_barrier((real_in, imag_in, hold, give))
        by_x = add(real[:2], real_in[:2]).astype(BF16)
        by_y = add(imag[:2], imag_in[:2]).astype(BF16)
        by_x, by_y, hold, give = lax.optimization_barrier((by_x, by_y, hold, give))
        by_x, by_y = swap(by_x, tri_size, 1), swap(by_y, tri_size, 2)
        mine = add(hold, swap(give, tri_size, 0)).astype(BF16)
        mine = add(mine, swap(mine, tri_size, 1)).astype(BF16)
        received = swap(mine, tri_size, 2)
        then_y = add(real[2], real_in[2], by_x[1]).astype(BF16)
        then_x = add(imag[2], imag_in[2], by_y[1]).astype(BF16)
        then_y, then_x, received = lax.optimization_barrier((then_y, then_x, received))
        then_y, then_x = swap(then_y[None], tri_size, 2), swap(then_x[None], tri_size, 1)
        mine = add(mine, received).astype(BF16)
        terms = [(own, 0, 0), (own, 1, 1), (own_in, 0, 0), (own_in, 1, 1)]
        terms += [(by_x, 0, 0), (by_y, 1, 0), (then_y, 0, 0), (then_x, 1, 0)]
    else:
        terms = scatter_plain(partials[0].reshape(tri_size, 2, *amplitudes.shape[1:]), tri_size)
        mine = add(hold, swap(give, tri_size, 0)).astype(BF16)
        for bit in range(1, bits):
            mine = add(mine, swap(mine, tri_size, bit)).astype(BF16)
    mine = jnp.stack([mine[0]] + [turn(mine[step], vp_size - step) for step in range(1, vp_size)])
    base = quadratic(core, ring, mine, swap(mine, tri_size, 0))
    return finish(base, terms)


def solution(mesh):
    in_specs = (P(None, "tri", "vp"), P("tri", "vp"), P("tri", None, None), P("tri"))
    out_specs = P(None, "tri", "vp")
    body = functools.partial(shards, mesh.shape["tri"], mesh.shape["vp"])
    return jax.shard_map(body, mesh=mesh, in_specs=in_specs, out_specs=out_specs, check_vma=False)
```

```python
import functools

import jax
import jax.numpy as jnp
from jax import lax
from jax.experimental import pallas as pl
from jax.experimental.pallas import tpu as pltpu
from jax.sharding import PartitionSpec as P

NB = 10
BLOCK = 768
PAIRS = NB * BLOCK
TRI_BLOCKS = NB * (NB + 1) // 2
F32 = jnp.float32
BF16 = jnp.bfloat16


def swap(value, axis_size, bit):
    pairs = [(i, i ^ (1 << bit)) for i in range(axis_size)]
    return lax.ppermute(value, "tri", pairs)


def after(value, *earlier):
    return lax.optimization_barrier((value, *earlier))[0]


def gather_tri(amplitudes, axis_size):
    if axis_size != 8:
        found = {0: amplitudes}
        for bit in range(axis_size.bit_length() - 1):
            for mask in list(found):
                found[mask | (1 << bit)] = swap(found[mask], axis_size, bit)
        return [(value, mask, None) for mask, value in found.items()]
    by_x = swap(amplitudes, axis_size, 1)
    by_y = swap(amplitudes, axis_size, 2)
    own_core = swap(amplitudes, axis_size, 0)
    far_real = swap(by_y[0], axis_size, 1)
    far_imag = swap(by_x[1], axis_size, 2)
    found = [
        (amplitudes, 0, None), (by_x, 2, None), (by_y, 4, None), (far_real, 6, 0), (far_imag, 6, 1),
        (own_core, 1, None),
    ]
    for value, mask, part in found[1:5]:
        found.append((swap(value, axis_size, 0), mask | 1, part))
    return found


def ladder_kernel(labels, groups, me_ref, code_ref, *refs):
    count = len(labels)
    piece_refs = refs[:count]
    ladder_ref = refs[count]
    out_refs = refs[count + 1:-3]
    amp, acc, sems = refs[-3:]
    columns = amp.shape[1] // 2
    rows = out_refs[0].shape[-2]
    step = pl.program_id(0)
    me = me_ref[0]

    def rows_of(mask):
        return pl.ds(pl.multiple_of((me ^ mask) * rows, rows), rows)

    @pl.when(step == 0)
    def _():
        copies = []
        for index, (mask, part) in enumerate(labels):
            for which in (0, 1) if part is None else (part,):
                source = piece_refs[index].at[which] if part is None else piece_refs[index]
                lanes = pl.ds(which * columns, columns)
                copy = pltpu.make_async_copy(source, amp.at[rows_of(mask), lanes], sems.at[len(copies)])
                copy.start()
                copies.append(copy)
        acc[...] = jnp.zeros_like(acc)
        for copy in copies:
            copy.wait()

    code = code_ref[step]
    row_block = jnp.int32(0)
    start = jnp.int32(0)
    for row in range(1, NB):
        first = row * NB - row * (row - 1) // 2
        past = code >= first
        row_block = jnp.where(past, row, row_block)
        start = jnp.where(past, first, start)
    column_block = jnp.minimum(row_block + code - start, NB - 1)
    weight = jnp.where(row_block == column_block, 0.5, 1.0) * jnp.where(code < TRI_BLOCKS, 1.0, 0.0)
    at_row = pl.ds(pl.multiple_of(row_block * BLOCK, BLOCK), BLOCK)
    at_column = pl.ds(pl.multiple_of(column_block * BLOCK, BLOCK), BLOCK)
    block = ladder_ref[0]
    to_row = lax.dot_general(block, amp[at_column, :], (((1,), (0,)), ((), ())), preferred_element_type=F32)
    acc[at_row, :] += weight * to_row
    to_column = lax.dot_general(block, amp[at_row, :], (((0,), (0,)), ((), ())), preferred_element_type=F32)
    acc[at_column, :] += weight * to_column

    @pl.when(step == pl.num_programs(0) - 1)
    def _():
        for target, places in zip(out_refs, groups, strict=True):
            for place, (mask, part) in enumerate(places):
                lanes = slice(part * columns, (part + 1) * columns)
                target[place] = acc[rows_of(mask), lanes].astype(BF16)


def ladder(me, codes, pieces, ladder_blocks, groups):
    slots = ladder_blocks.shape[0]
    rows, columns = pieces[0][0].shape[-2:]
    count = sum(len(places) for places in groups)
    return pl.pallas_call(
        functools.partial(ladder_kernel, [(mask, part) for _, mask, part in pieces], groups),
        grid_spec=pltpu.PrefetchScalarGridSpec(
            num_scalar_prefetch=2,
            grid=(slots,),
            in_specs=[pl.BlockSpec(memory_space=pl.ANY)] * len(pieces)
            + [pl.BlockSpec((1, BLOCK, BLOCK), lambda s, *_: (s, 0, 0))],
            out_specs=[pl.BlockSpec((len(places), rows, columns), lambda s, *_: (0, 0, 0)) for places in groups],
            scratch_shapes=[
                pltpu.VMEM((PAIRS, 2 * columns), BF16),
                pltpu.VMEM((PAIRS, 2 * columns), F32),
                pltpu.SemaphoreType.DMA((count,)),
            ],
        ),
        out_shape=[jax.ShapeDtypeStruct((len(places), rows, columns), BF16) for places in groups],
        compiler_params=pltpu.CompilerParams(
            dimension_semantics=("arbitrary",), vmem_limit_bytes=40 * 1024 * 1024
        ),
        cost_estimate=pl.CostEstimate(flops=1, bytes_accessed=1, transcendentals=0),
        name="ladder",
    )(me, codes, *[value for value, _, _ in pieces], ladder_blocks)


def add(*terms):
    total = terms[0].astype(F32)
    for term in terms[1:]:
        total = total + term.astype(F32)
    return total


def contract_kernel(me_ref, int_ref, wide_ref, hold_ref, give_ref):
    vp_size, _, _, columns = wide_ref.shape
    values = int_ref[...]
    for step in range(vp_size):
        target = lax.rem(me_ref[1] + step, vp_size)
        both = jnp.concatenate([wide_ref[target, 0], wide_ref[target, 1]], axis=1)
        product = lax.dot_general(values, both, (((0,), (0,)), ((), ())), preferred_element_type=F32)
        real = product[:, :columns].astype(BF16)
        imag = product[:, columns:].astype(BF16)
        hold_ref[step] = jnp.where(me_ref[0] == 0, real, imag)
        give_ref[step] = jnp.where(me_ref[0] == 0, imag, real)


def contract(me, integrals, wide):
    vp_size, _, rows, columns = wide.shape
    vmem = pl.BlockSpec(memory_space=pltpu.VMEM)
    return pl.pallas_call(
        contract_kernel,
        in_specs=[pl.BlockSpec(memory_space=pltpu.SMEM)] + [vmem] * 2,
        out_specs=[vmem] * 2,
        out_shape=[jax.ShapeDtypeStruct((vp_size, columns, columns), BF16)] * 2,
        compiler_params=pltpu.CompilerParams(vmem_limit_bytes=20 * 1024 * 1024),
        cost_estimate=pl.CostEstimate(
            flops=2 * wide.size * columns,
            bytes_accessed=2 * (wide.size + integrals.size),
            transcendentals=0,
        ),
        name="contract",
    )(me, integrals, wide)


def quadratic_kernel(me_ref, amp_ref, wide_ref, mine_ref, other_ref, out_ref):
    vp_size, _, rows, columns = wide_ref.shape
    core = me_ref[0]
    total = jnp.zeros((rows, 2 * columns), F32)
    for step in range(vp_size):
        source = lax.rem(me_ref[1] + vp_size - step, vp_size)
        both = jnp.concatenate([wide_ref[source, 0], wide_ref[source, 1]], axis=1)
        real = jnp.where(core == 0, mine_ref[step], other_ref[step])
        imag = jnp.where(core == 0, other_ref[step], mine_ref[step])
        weights = jnp.concatenate(
            [jnp.concatenate([real, imag], axis=1), jnp.concatenate([-imag, real], axis=1)], axis=0
        )
        total += jnp.dot(both, weights, preferred_element_type=F32)
    out_ref[0] = amp_ref[0].astype(F32) + 0.25 * total[:, columns:]
    out_ref[1] = amp_ref[1].astype(F32) - 0.25 * total[:, :columns]


def quadratic(me, amplitudes, wide, mine, other):
    vmem = pl.BlockSpec(memory_space=pltpu.VMEM)
    return pl.pallas_call(
        quadratic_kernel,
        in_specs=[pl.BlockSpec(memory_space=pltpu.SMEM)] + [vmem] * 4,
        out_specs=vmem,
        out_shape=jax.ShapeDtypeStruct(amplitudes.shape, F32),
        compiler_params=pltpu.CompilerParams(vmem_limit_bytes=20 * 1024 * 1024),
        cost_estimate=pl.CostEstimate(
            flops=4 * wide.size * amplitudes.shape[2],
            bytes_accessed=2 * wide.size + 4 * amplitudes.size,
            transcendentals=0,
        ),
        name="quadratic",
    )(me, amplitudes, wide, mine, other)


def finish_kernel(places, base_ref, *refs):
    sums = [0.0, 0.0]
    for ref, (_, part, place) in zip(refs, places, strict=False):
        sums[part] = sums[part] + ref[place].astype(F32)
    refs[-1][0] = (base_ref[0] + 0.5 * sums[1]).astype(BF16)
    refs[-1][1] = (base_ref[1] - 0.5 * sums[0]).astype(BF16)


def finish(base, terms):
    vmem = pl.BlockSpec(memory_space=pltpu.VMEM)
    return pl.pallas_call(
        functools.partial(finish_kernel, [(None, part, place) for _, part, place in terms]),
        in_specs=[vmem] * (1 + len(terms)),
        out_specs=vmem,
        out_shape=jax.ShapeDtypeStruct(base.shape, BF16),
        compiler_params=pltpu.CompilerParams(vmem_limit_bytes=20 * 1024 * 1024),
        name="finish",
    )(base, *[value for value, _, _ in terms])


def scatter_plain(partial, tri_size):
    terms = [partial]
    for bit in reversed(range(tri_size.bit_length() - 1)):
        half = terms[0].shape[0] // 2
        outgoing = add(*[term[half:] for term in terms]).astype(BF16)
        terms = [term[:half] for term in terms] + [swap(outgoing, tri_size, bit)]
    return [(term[0], part, part) for term in terms for part in range(2)]


def shards(tri_size, vp_size, amplitudes, integrals, ladder_blocks, slot_block):
    bits = tri_size.bit_length() - 1
    me = lax.axis_index("tri").astype(jnp.int32)[None]
    where = jnp.stack([me[0] & 1, lax.axis_index("vp").astype(jnp.int32)])
    wide = lax.all_gather(amplitudes, "vp", axis=0, tiled=False)
    pieces = gather_tri(amplitudes, tri_size)

    if tri_size == 8:
        real_order, imag_order = (2, 6, 4), (4, 6, 2)
        groups = [[(mask | 1, 0) for mask in real_order], [(mask | 1, 1) for mask in imag_order], [(1, 0), (1, 1)]]
        groups += [[(mask, 0) for mask in real_order], [(mask, 1) for mask in imag_order], [(0, 0), (0, 1)]]
    else:
        groups = [[(mask, part) for mask in range(tri_size) for part in range(2)]]
    partials = ladder(me, slot_block, pieces, ladder_blocks, groups)
    *partials, wide = lax.optimization_barrier((*partials, wide))
    hold, give = contract(where, integrals, wide)

    def shift(value):
        moved = [value[0]]
        for step in range(1, vp_size):
            moved.append(lax.ppermute(value[step], "vp", [(i, (i + step) % vp_size) for i in range(vp_size)]))
        return jnp.stack(moved)

    if tri_size == 8:
        real, imag, own = partials[3:]
        real_in, imag_in, own_in = (swap(value, tri_size, 0) for value in partials[:3])
        real_in, imag_in, hold, give = lax.optimization_barrier((real_in, imag_in, hold, give))
        by_x = add(real[:2], real_in[:2]).astype(BF16)
        by_y = add(imag[:2], imag_in[:2]).astype(BF16)
        by_x, by_y, hold, give = lax.optimization_barrier((by_x, by_y, hold, give))
        by_x, by_y = swap(by_x, tri_size, 1), swap(by_y, tri_size, 2)
        mine = shift(add(hold, swap(give, tri_size, 0)).astype(BF16))
        received = swap(mine, tri_size, 1)
        then_y = add(real[2], real_in[2], by_x[1]).astype(BF16)
        then_x = add(imag[2], imag_in[2], by_y[1]).astype(BF16)
        then_y, then_x, received = lax.optimization_barrier((then_y, then_x, received))
        then_y, then_x = swap(then_y[None], tri_size, 2), swap(then_x[None], tri_size, 1)
        mine = add(mine, received).astype(BF16)
        mine = add(mine, swap(mine, tri_size, 2)).astype(BF16)
        terms = [(own, 0, 0), (own, 1, 1), (own_in, 0, 0), (own_in, 1, 1)]
        terms += [(by_x, 0, 0), (by_y, 1, 0), (then_y, 0, 0), (then_x, 1, 0)]
    else:
        terms = scatter_plain(partials[0].reshape(tri_size, 2, *amplitudes.shape[1:]), tri_size)
        mine = shift(add(hold, swap(give, tri_size, 0)).astype(BF16))
        for bit in range(1, bits):
            mine = add(mine, swap(mine, tri_size, bit)).astype(BF16)
    base = quadratic(where, amplitudes, wide, mine, swap(mine, tri_size, 0))
    return finish(base, terms)


def solution(mesh):
    in_specs = (P(None, "tri", "vp"), P("tri", "vp"), P("tri", None, None), P("tri"))
    out_specs = P(None, "tri", "vp")
    body = functools.partial(shards, mesh.shape["tri"], mesh.shape["vp"])
    return jax.shard_map(body, mesh=mesh, in_specs=in_specs, out_specs=out_specs, check_vma=False)
```

```python
import functools

import jax
import jax.numpy as jnp
from jax import lax
from jax.experimental import pallas as pl
from jax.experimental.pallas import tpu as pltpu
from jax.sharding import PartitionSpec as P

NB = 10
BLOCK = 768
PAIRS = NB * BLOCK
TRI_BLOCKS = NB * (NB + 1) // 2
F32 = jnp.float32
BF16 = jnp.bfloat16


def swap(value, axis_size, bit):
    pairs = [(i, i ^ (1 << bit)) for i in range(axis_size)]
    return lax.ppermute(value, "tri", pairs)


def after(value, *earlier):
    return lax.optimization_barrier((value, *earlier))[0]


def gather_tri(amplitudes, axis_size):
    if axis_size != 8:
        found = {0: amplitudes}
        for bit in range(axis_size.bit_length() - 1):
            for mask in list(found):
                found[mask | (1 << bit)] = swap(found[mask], axis_size, bit)
        return [(value, mask, None) for mask, value in found.items()]
    by_x = swap(amplitudes, axis_size, 1)
    by_y = swap(amplitudes, axis_size, 2)
    own_core = swap(amplitudes, axis_size, 0)
    far_real = swap(by_y[0], axis_size, 1)
    far_imag = swap(by_x[1], axis_size, 2)
    found = [
        (amplitudes, 0, None), (by_x, 2, None), (by_y, 4, None), (far_real, 6, 0), (far_imag, 6, 1),
        (own_core, 1, None),
    ]
    for value, mask, part in found[1:5]:
        found.append((swap(value, axis_size, 0), mask | 1, part))
    return found


def ladder_kernel(labels, groups, me_ref, code_ref, *refs):
    count = len(labels)
    piece_refs = refs[:count]
    ladder_ref = refs[count]
    out_refs = refs[count + 1:-3]
    amp, acc, sems = refs[-3:]
    columns = amp.shape[1] // 2
    rows = out_refs[0].shape[-2]
    step = pl.program_id(0)
    me = me_ref[0]

    def rows_of(mask):
        return pl.ds(pl.multiple_of((me ^ mask) * rows, rows), rows)

    @pl.when(step == 0)
    def _():
        copies = []
        for index, (mask, part) in enumerate(labels):
            for which in (0, 1) if part is None else (part,):
                source = piece_refs[index].at[which] if part is None else piece_refs[index]
                lanes = pl.ds(which * columns, columns)
                copy = pltpu.make_async_copy(source, amp.at[rows_of(mask), lanes], sems.at[len(copies)])
                copy.start()
                copies.append(copy)
        acc[...] = jnp.zeros_like(acc)
        for copy in copies:
            copy.wait()

    code = code_ref[step]
    row_block = jnp.int32(0)
    start = jnp.int32(0)
    for row in range(1, NB):
        first = row * NB - row * (row - 1) // 2
        past = code >= first
        row_block = jnp.where(past, row, row_block)
        start = jnp.where(past, first, start)
    column_block = jnp.minimum(row_block + code - start, NB - 1)
    weight = jnp.where(row_block == column_block, 0.5, 1.0) * jnp.where(code < TRI_BLOCKS, 1.0, 0.0)
    at_row = pl.ds(pl.multiple_of(row_block * BLOCK, BLOCK), BLOCK)
    at_column = pl.ds(pl.multiple_of(column_block * BLOCK, BLOCK), BLOCK)
    block = ladder_ref[0]
    to_row = lax.dot_general(block, amp[at_column, :], (((1,), (0,)), ((), ())), preferred_element_type=F32)
    acc[at_row, :] += weight * to_row
    to_column = lax.dot_general(block, amp[at_row, :], (((0,), (0,)), ((), ())), preferred_element_type=F32)
    acc[at_column, :] += weight * to_column

    @pl.when(step == pl.num_programs(0) - 1)
    def _():
        for target, places in zip(out_refs, groups, strict=True):
            for place, (mask, part) in enumerate(places):
                lanes = slice(part * columns, (part + 1) * columns)
                target[place] = acc[rows_of(mask), lanes].astype(BF16)


def ladder(me, codes, pieces, ladder_blocks, groups):
    slots = ladder_blocks.shape[0]
    rows, columns = pieces[0][0].shape[-2:]
    count = sum(len(places) for places in groups)
    return pl.pallas_call(
        functools.partial(ladder_kernel, [(mask, part) for _, mask, part in pieces], groups),
        grid_spec=pltpu.PrefetchScalarGridSpec(
            num_scalar_prefetch=2,
            grid=(slots,),
            in_specs=[pl.BlockSpec(memory_space=pl.ANY)] * len(pieces)
            + [pl.BlockSpec((1, BLOCK, BLOCK), lambda s, *_: (s, 0, 0))],
            out_specs=[pl.BlockSpec((len(places), rows, columns), lambda s, *_: (0, 0, 0)) for places in groups],
            scratch_shapes=[
                pltpu.VMEM((PAIRS, 2 * columns), BF16),
                pltpu.VMEM((PAIRS, 2 * columns), F32),
                pltpu.SemaphoreType.DMA((count,)),
            ],
        ),
        out_shape=[jax.ShapeDtypeStruct((len(places), rows, columns), BF16) for places in groups],
        compiler_params=pltpu.CompilerParams(
            dimension_semantics=("arbitrary",), vmem_limit_bytes=40 * 1024 * 1024
        ),
        cost_estimate=pl.CostEstimate(
            flops=slots * 8 * BLOCK * BLOCK * columns,
            bytes_accessed=slots * BLOCK * BLOCK * 2 + 8 * PAIRS * columns,
            transcendentals=0,
        ),
        name="ladder",
    )(me, codes, *[value for value, _, _ in pieces], ladder_blocks)


def add(*terms):
    total = terms[0].astype(F32)
    for term in terms[1:]:
        total = total + term.astype(F32)
    return total


def contract_kernel(core_ref, int_ref, last_ref, *refs):
    columns = int_ref.shape[1]
    hold_ref, give_ref = refs[-2:]
    for step in range(len(refs) - 1):
        values, ref = (int_ref, refs[step]) if step < len(refs) - 2 else (last_ref, refs[0])
        both = jnp.concatenate([ref[0], ref[1]], axis=1)
        product = lax.dot_general(values[...], both, (((0,), (0,)), ((), ())), preferred_element_type=F32)
        real = product[:, :columns].astype(BF16)
        imag = product[:, columns:].astype(BF16)
        hold_ref[step] = jnp.where(core_ref[0] == 0, real, imag)
        give_ref[step] = jnp.where(core_ref[0] == 0, imag, real)


def contract(core, integrals, back_integrals, ring):
    rows, columns = integrals.shape
    vmem = pl.BlockSpec(memory_space=pltpu.VMEM)
    count = len(ring) + 1
    return pl.pallas_call(
        contract_kernel,
        in_specs=[pl.BlockSpec(memory_space=pltpu.SMEM)] + [vmem] * (2 + len(ring)),
        out_specs=[vmem] * 2,
        out_shape=[jax.ShapeDtypeStruct((count, columns, columns), BF16)] * 2,
        compiler_params=pltpu.CompilerParams(vmem_limit_bytes=20 * 1024 * 1024),
        cost_estimate=pl.CostEstimate(
            flops=4 * count * rows * columns * columns,
            bytes_accessed=4 * count * rows * columns,
            transcendentals=0,
        ),
        name="contract",
    )(core, integrals, back_integrals, *ring)


def quadratic_kernel(core_ref, mine_ref, other_ref, *refs):
    amp_ref, out_ref = refs[0], refs[-1]
    _, rows, columns = amp_ref.shape
    vp_size = len(refs) - 1
    core = core_ref[0]
    total = jnp.zeros((rows, 2 * columns), F32)
    for step in range(vp_size):
        both = jnp.concatenate([refs[step][0], refs[step][1]], axis=1)
        source = (vp_size - step) % vp_size
        real = jnp.where(core == 0, mine_ref[source], other_ref[source])
        imag = jnp.where(core == 0, other_ref[source], mine_ref[source])
        weights = jnp.concatenate(
            [jnp.concatenate([real, imag], axis=1), jnp.concatenate([-imag, real], axis=1)], axis=0
        )
        total += jnp.dot(both, weights, preferred_element_type=F32)
    out_ref[0] = amp_ref[0].astype(F32) + 0.25 * total[:, columns:]
    out_ref[1] = amp_ref[1].astype(F32) - 0.25 * total[:, :columns]


def quadratic(core, ring, mine, other):
    vmem = pl.BlockSpec(memory_space=pltpu.VMEM)
    size = ring[0].size
    return pl.pallas_call(
        quadratic_kernel,
        in_specs=[pl.BlockSpec(memory_space=pltpu.SMEM)] + [vmem] * (2 + len(ring)),
        out_specs=vmem,
        out_shape=jax.ShapeDtypeStruct(ring[0].shape, F32),
        compiler_params=pltpu.CompilerParams(vmem_limit_bytes=20 * 1024 * 1024),
        cost_estimate=pl.CostEstimate(
            flops=4 * len(ring) * size * ring[0].shape[2],
            bytes_accessed=(2 * len(ring) + 4) * size,
            transcendentals=0,
        ),
        name="quadratic",
    )(core, mine, other, *ring)


def finish_kernel(places, base_ref, *refs):
    sums = [0.0, 0.0]
    for ref, (_, part, place) in zip(refs, places, strict=False):
        sums[part] = sums[part] + ref[place].astype(F32)
    refs[-1][0] = (base_ref[0] + 0.5 * sums[1]).astype(BF16)
    refs[-1][1] = (base_ref[1] - 0.5 * sums[0]).astype(BF16)


def finish(base, terms):
    vmem = pl.BlockSpec(memory_space=pltpu.VMEM)
    return pl.pallas_call(
        functools.partial(finish_kernel, [(None, part, place) for _, part, place in terms]),
        in_specs=[vmem] * (1 + len(terms)),
        out_specs=vmem,
        out_shape=jax.ShapeDtypeStruct(base.shape, BF16),
        compiler_params=pltpu.CompilerParams(vmem_limit_bytes=20 * 1024 * 1024),
        name="finish",
    )(base, *[value for value, _, _ in terms])


def scatter_plain(partial, tri_size):
    terms = [partial]
    for bit in reversed(range(tri_size.bit_length() - 1)):
        half = terms[0].shape[0] // 2
        outgoing = add(*[term[half:] for term in terms]).astype(BF16)
        terms = [term[:half] for term in terms] + [swap(outgoing, tri_size, bit)]
    return [(term[0], part, part) for term in terms for part in range(2)]


def shards(tri_size, vp_size, amplitudes, integrals, ladder_blocks, slot_block):
    bits = tri_size.bit_length() - 1
    me = lax.axis_index("tri").astype(jnp.int32)[None]
    core = me & 1
    order = list(range(0, vp_size, 2)) + list(range(1, vp_size, 2))[::-1]

    def turn(value, distance=1):
        return lax.ppermute(value, "vp", [(order[i], order[(i + distance) % vp_size]) for i in range(vp_size)])

    ring = [amplitudes]
    for _ in range(2, vp_size):
        ring.append(turn(ring[-1]))
    back_integrals = turn(integrals)
    pieces = gather_tri(amplitudes, tri_size)
    me = after(me, ring[1], back_integrals)

    if tri_size == 8:
        real_order, imag_order = (2, 6, 4), (4, 6, 2)
        groups = [[(mask | 1, 0) for mask in real_order], [(mask | 1, 1) for mask in imag_order], [(1, 0), (1, 1)]]
        groups += [[(mask, 0) for mask in real_order], [(mask, 1) for mask in imag_order], [(0, 0), (0, 1)]]
    else:
        groups = [[(mask, part) for mask in range(tri_size) for part in range(2)]]
    partials = ladder(me, slot_block, pieces, ladder_blocks, groups)
    *partials, ring[-1] = lax.optimization_barrier((*partials, ring[-1]))
    hold, give = contract(core, integrals, back_integrals, ring)
    last = turn(ring[-1])

    def shift(value):
        moved = [turn(value[step], vp_size - step) for step in range(1, vp_size - 1)]
        return jnp.stack([value[0], *moved, value[vp_size - 1]])

    if tri_size == 8:
        real, imag, own = partials[3:]
        real_in, imag_in, own_in = (swap(value, tri_size, 0) for value in partials[:3])
        real_in, imag_in, hold, give = lax.optimization_barrier((real_in, imag_in, hold, give))
        by_x = add(real[:2], real_in[:2]).astype(BF16)
        by_y = add(imag[:2], imag_in[:2]).astype(BF16)
        by_x, by_y, hold, give = lax.optimization_barrier((by_x, by_y, hold, give))
        by_x, by_y = swap(by_x, tri_size, 1), swap(by_y, tri_size, 2)
        mine = shift(add(hold, swap(give, tri_size, 0)).astype(BF16))
        received = swap(mine, tri_size, 1)
        then_y = add(real[2], real_in[2], by_x[1]).astype(BF16)
        then_x = add(imag[2], imag_in[2], by_y[1]).astype(BF16)
        then_y, then_x, received, last = lax.optimization_barrier((then_y, then_x, received, last))
        then_y, then_x = swap(then_y[None], tri_size, 2), swap(then_x[None], tri_size, 1)
        mine = add(mine, received).astype(BF16)
        mine = add(mine, swap(mine, tri_size, 2)).astype(BF16)
        terms = [(own, 0, 0), (own, 1, 1), (own_in, 0, 0), (own_in, 1, 1)]
        terms += [(by_x, 0, 0), (by_y, 1, 0), (then_y, 0, 0), (then_x, 1, 0)]
    else:
        terms = scatter_plain(partials[0].reshape(tri_size, 2, *amplitudes.shape[1:]), tri_size)
        mine = shift(add(hold, swap(give, tri_size, 0)).astype(BF16))
        for bit in range(1, bits):
            mine = add(mine, swap(mine, tri_size, bit)).astype(BF16)
    base = quadratic(core, [*ring, last], mine, swap(mine, tri_size, 0))
    return finish(base, terms)


def solution(mesh):
    in_specs = (P(None, "tri", "vp"), P("tri", "vp"), P("tri", None, None), P("tri"))
    out_specs = P(None, "tri", "vp")
    body = functools.partial(shards, mesh.shape["tri"], mesh.shape["vp"])
    return jax.shard_map(body, mesh=mesh, in_specs=in_specs, out_specs=out_specs, check_vma=False)
```

```python
import functools

import jax
import jax.numpy as jnp
from jax import lax
from jax.experimental import pallas as pl
from jax.experimental.pallas import tpu as pltpu
from jax.sharding import PartitionSpec as P

NB = 10
BLOCK = 768
PAIRS = NB * BLOCK
TRI_BLOCKS = NB * (NB + 1) // 2
F32 = jnp.float32
BF16 = jnp.bfloat16


def swap(value, axis_size, bit):
    pairs = [(i, i ^ (1 << bit)) for i in range(axis_size)]
    return lax.ppermute(value, "tri", pairs)


def after(value, *earlier):
    return lax.optimization_barrier((value, *earlier))[0]


def gather_tri(amplitudes, codes, ladder_blocks, axis_size):
    if axis_size != 8:
        turned, own, table = prepare(codes, ladder_blocks, amplitudes)
        found = {0: own}
        for bit in range(axis_size.bit_length() - 1):
            for mask in list(found):
                found[mask | (1 << bit)] = swap(found[mask], axis_size, bit)
        return turned, own, table, [(value, mask, None) for mask, value in found.items()]
    by_x = swap(amplitudes, axis_size, 1)
    by_y = swap(amplitudes, axis_size, 2)
    own_core = swap(amplitudes, axis_size, 0)
    turned, own, table = prepare(codes, ladder_blocks, amplitudes)
    by_x, by_y, table = lax.optimization_barrier((by_x, by_y, table))
    far_real = swap(by_y[0], axis_size, 1)
    far_imag = swap(by_x[1], axis_size, 2)
    found = [
        (own, 0, None), (by_x, 2, None), (by_y, 4, None), (far_real, 6, 0), (far_imag, 6, 1),
        (own_core, 1, None),
    ]
    for value, mask, part in found[1:5]:
        found.append((swap(value, axis_size, 0), mask | 1, part))
    return turned, own, table, found


def prepare_kernel(code_ref, ladder_ref, amp_ref, turned_ref, own_ref, table_ref):
    step = pl.program_id(0)
    turned_ref[0] = ladder_ref[0].T

    @pl.when(step == 0)
    def _():
        own_ref[...] = amp_ref[...]

    code = code_ref[step]
    row_block = jnp.int32(0)
    start = jnp.int32(0)
    for row in range(1, NB):
        first = row * NB - row * (row - 1) // 2
        past = code >= first
        row_block = jnp.where(past, row, row_block)
        start = jnp.where(past, first, start)
    column_block = jnp.minimum(row_block + code - start, NB - 1)
    table_ref[0, step] = row_block
    table_ref[1, step] = column_block
    table_ref[2, step] = jnp.where(code < TRI_BLOCKS, jnp.where(row_block == column_block, 1, 2), 0)


def prepare(codes, ladder_blocks, amplitudes):
    slots = ladder_blocks.shape[0]
    block = pl.BlockSpec((1, BLOCK, BLOCK), lambda s: (s, 0, 0))
    whole = pl.BlockSpec(amplitudes.shape, lambda s: (0, 0, 0))
    smem = pl.BlockSpec(memory_space=pltpu.SMEM)
    return pl.pallas_call(
        prepare_kernel,
        grid=(slots,),
        in_specs=[smem, block, whole],
        out_specs=[block, whole, smem],
        out_shape=[
            jax.ShapeDtypeStruct(ladder_blocks.shape, BF16),
            jax.ShapeDtypeStruct(amplitudes.shape, BF16),
            jax.ShapeDtypeStruct((3, slots), jnp.int32),
        ],
        compiler_params=pltpu.CompilerParams(
            dimension_semantics=("arbitrary",), vmem_limit_bytes=52 * 1024 * 1024
        ),
        cost_estimate=pl.CostEstimate(flops=0, bytes_accessed=4 * ladder_blocks.size, transcendentals=0),
        name="prepare",
    )(codes, ladder_blocks, amplitudes)


def ladder_kernel(labels, groups, me_ref, table_ref, *refs):
    count = len(labels)
    piece_refs = refs[:count]
    ladder_ref, turned_ref = refs[count:count + 2]
    out_refs = refs[count + 2:-3]
    amp, acc, sems = refs[-3:]
    columns = amp.shape[1] // 2
    rows = out_refs[0].shape[-2]
    step = pl.program_id(0)
    me = me_ref[0]

    def rows_of(mask):
        return pl.ds(pl.multiple_of((me ^ mask) * rows, rows), rows)

    @pl.when(step == 0)
    def _():
        copies = []
        for index, (mask, part) in enumerate(labels):
            for which in (0, 1) if part is None else (part,):
                source = piece_refs[index].at[which] if part is None else piece_refs[index]
                lanes = pl.ds(which * columns, columns)
                copy = pltpu.make_async_copy(source, amp.at[rows_of(mask), lanes], sems.at[len(copies)])
                copy.start()
                copies.append(copy)
        acc[...] = jnp.zeros_like(acc)
        for copy in copies:
            copy.wait()

    weight = 0.5 * table_ref[2, step].astype(F32)
    at_row = pl.ds(pl.multiple_of(table_ref[0, step] * BLOCK, BLOCK), BLOCK)
    at_column = pl.ds(pl.multiple_of(table_ref[1, step] * BLOCK, BLOCK), BLOCK)
    acc[at_row, :] += weight * jnp.dot(ladder_ref[0], amp[at_column, :], preferred_element_type=F32)
    acc[at_column, :] += weight * jnp.dot(turned_ref[0], amp[at_row, :], preferred_element_type=F32)

    @pl.when(step == pl.num_programs(0) - 1)
    def _():
        for target, places in zip(out_refs, groups, strict=True):
            for place, (mask, part) in enumerate(places):
                lanes = slice(part * columns, (part + 1) * columns)
                target[place] = acc[rows_of(mask), lanes].astype(BF16)


def ladder(me, table, pieces, ladder_blocks, turned, groups):
    slots = ladder_blocks.shape[0]
    rows, columns = pieces[0][0].shape[-2:]
    count = sum(len(places) for places in groups)
    block = pl.BlockSpec((1, BLOCK, BLOCK), lambda s, *_: (s, 0, 0))
    return pl.pallas_call(
        functools.partial(ladder_kernel, [(mask, part) for _, mask, part in pieces], groups),
        grid_spec=pltpu.PrefetchScalarGridSpec(
            num_scalar_prefetch=2,
            grid=(slots,),
            in_specs=[pl.BlockSpec(memory_space=pl.ANY)] * len(pieces) + [block, block],
            out_specs=[pl.BlockSpec((len(places), rows, columns), lambda s, *_: (0, 0, 0)) for places in groups],
            scratch_shapes=[
                pltpu.VMEM((PAIRS, 2 * columns), BF16),
                pltpu.VMEM((PAIRS, 2 * columns), F32),
                pltpu.SemaphoreType.DMA((count,)),
            ],
        ),
        out_shape=[jax.ShapeDtypeStruct((len(places), rows, columns), BF16) for places in groups],
        compiler_params=pltpu.CompilerParams(
            dimension_semantics=("arbitrary",), vmem_limit_bytes=40 * 1024 * 1024
        ),
        cost_estimate=pl.CostEstimate(
            flops=slots * 8 * BLOCK * BLOCK * columns,
            bytes_accessed=slots * BLOCK * BLOCK * 2 + 8 * PAIRS * columns,
            transcendentals=0,
        ),
        name="ladder",
    )(me, table, *[value for value, _, _ in pieces], ladder_blocks, turned)


def add(*terms):
    total = terms[0].astype(F32)
    for term in terms[1:]:
        total = total + term.astype(F32)
    return total


def contract_kernel(core_ref, int_ref, last_ref, *refs):
    columns = int_ref.shape[1]
    hold_ref, give_ref = refs[-2:]
    for step in range(len(refs) - 1):
        values, ref = (int_ref, refs[step]) if step < len(refs) - 2 else (last_ref, refs[0])
        both = jnp.concatenate([ref[0], ref[1]], axis=1)
        product = lax.dot_general(values[...], both, (((0,), (0,)), ((), ())), preferred_element_type=F32)
        real = product[:, :columns].astype(BF16)
        imag = product[:, columns:].astype(BF16)
        hold_ref[step] = jnp.where(core_ref[0] == 0, real, imag)
        give_ref[step] = jnp.where(core_ref[0] == 0, imag, real)


def contract(core, integrals, back_integrals, ring):
    rows, columns = integrals.shape
    vmem = pl.BlockSpec(memory_space=pltpu.VMEM)
    count = len(ring) + 1
    return pl.pallas_call(
        contract_kernel,
        in_specs=[pl.BlockSpec(memory_space=pltpu.SMEM)] + [vmem] * (2 + len(ring)),
        out_specs=[vmem] * 2,
        out_shape=[jax.ShapeDtypeStruct((count, columns, columns), BF16)] * 2,
        compiler_params=pltpu.CompilerParams(vmem_limit_bytes=20 * 1024 * 1024),
        cost_estimate=pl.CostEstimate(
            flops=4 * count * rows * columns * columns,
            bytes_accessed=4 * count * rows * columns,
            transcendentals=0,
        ),
        name="contract",
    )(core, integrals, back_integrals, *ring)


def quadratic_kernel(core_ref, mine_ref, other_ref, *refs):
    amp_ref, out_ref = refs[0], refs[-1]
    _, rows, columns = amp_ref.shape
    vp_size = len(refs) - 1
    core = core_ref[0]
    total = jnp.zeros((rows, 2 * columns), F32)
    for step in range(vp_size):
        both = jnp.concatenate([refs[step][0], refs[step][1]], axis=1)
        source = (vp_size - step) % vp_size
        real = jnp.where(core == 0, mine_ref[source], other_ref[source])
        imag = jnp.where(core == 0, other_ref[source], mine_ref[source])
        weights = jnp.concatenate(
            [jnp.concatenate([real, imag], axis=1), jnp.concatenate([-imag, real], axis=1)], axis=0
        )
        total += jnp.dot(both, weights, preferred_element_type=F32)
    out_ref[0] = amp_ref[0].astype(F32) + 0.25 * total[:, columns:]
    out_ref[1] = amp_ref[1].astype(F32) - 0.25 * total[:, :columns]


def quadratic(core, ring, mine, other):
    vmem = pl.BlockSpec(memory_space=pltpu.VMEM)
    size = ring[0].size
    return pl.pallas_call(
        quadratic_kernel,
        in_specs=[pl.BlockSpec(memory_space=pltpu.SMEM)] + [vmem] * (2 + len(ring)),
        out_specs=vmem,
        out_shape=jax.ShapeDtypeStruct(ring[0].shape, F32),
        compiler_params=pltpu.CompilerParams(vmem_limit_bytes=20 * 1024 * 1024),
        cost_estimate=pl.CostEstimate(
            flops=4 * len(ring) * size * ring[0].shape[2],
            bytes_accessed=(2 * len(ring) + 4) * size,
            transcendentals=0,
        ),
        name="quadratic",
    )(core, mine, other, *ring)


def finish_kernel(places, base_ref, *refs):
    sums = [0.0, 0.0]
    for ref, (_, part, place) in zip(refs, places, strict=False):
        sums[part] = sums[part] + ref[place].astype(F32)
    refs[-1][0] = (base_ref[0] + 0.5 * sums[1]).astype(BF16)
    refs[-1][1] = (base_ref[1] - 0.5 * sums[0]).astype(BF16)


def finish(base, terms):
    vmem = pl.BlockSpec(memory_space=pltpu.VMEM)
    return pl.pallas_call(
        functools.partial(finish_kernel, [(None, part, place) for _, part, place in terms]),
        in_specs=[vmem] * (1 + len(terms)),
        out_specs=vmem,
        out_shape=jax.ShapeDtypeStruct(base.shape, BF16),
        compiler_params=pltpu.CompilerParams(vmem_limit_bytes=20 * 1024 * 1024),
        name="finish",
    )(base, *[value for value, _, _ in terms])


def scatter_plain(partial, tri_size):
    terms = [partial]
    for bit in reversed(range(tri_size.bit_length() - 1)):
        half = terms[0].shape[0] // 2
        outgoing = add(*[term[half:] for term in terms]).astype(BF16)
        terms = [term[:half] for term in terms] + [swap(outgoing, tri_size, bit)]
    return [(term[0], part, part) for term in terms for part in range(2)]


def shards(tri_size, vp_size, amplitudes, integrals, ladder_blocks, slot_block):
    bits = tri_size.bit_length() - 1
    me = lax.axis_index("tri").astype(jnp.int32)[None]
    core = me & 1
    order = list(range(0, vp_size, 2)) + list(range(1, vp_size, 2))[::-1]

    def turn(value, distance=1):
        return lax.ppermute(value, "vp", [(order[i], order[(i + distance) % vp_size]) for i in range(vp_size)])

    ring = [amplitudes]
    for _ in range(2, vp_size):
        ring.append(turn(ring[-1]))
    back_integrals = turn(integrals)
    turned, ring[0], table, pieces = gather_tri(amplitudes, slot_block, ladder_blocks, tri_size)
    me = after(me, ring[1], back_integrals)

    if tri_size == 8:
        real_order, imag_order = (2, 6, 4), (4, 6, 2)
        groups = [[(mask | 1, 0) for mask in real_order], [(mask | 1, 1) for mask in imag_order], [(1, 0), (1, 1)]]
        groups += [[(mask, 0) for mask in real_order], [(mask, 1) for mask in imag_order], [(0, 0), (0, 1)]]
    else:
        groups = [[(mask, part) for mask in range(tri_size) for part in range(2)]]
    partials = ladder(me, table, pieces, ladder_blocks, turned, groups)
    *partials, ring[-1] = lax.optimization_barrier((*partials, ring[-1]))
    hold, give = contract(core, integrals, back_integrals, ring)
    last = turn(ring[-1])

    def shift(value):
        moved = [turn(value[step], vp_size - step) for step in range(1, vp_size - 1)]
        return jnp.stack([value[0], *moved, value[vp_size - 1]])

    if tri_size == 8:
        real, imag, own = partials[3:]
        real_in, imag_in, own_in = (swap(value, tri_size, 0) for value in partials[:3])
        mine = add(hold, swap(give, tri_size, 0)).astype(BF16)
        real_in, imag_in, mine = lax.optimization_barrier((real_in, imag_in, mine))
        by_x = add(real[:2], real_in[:2]).astype(BF16)
        by_y = add(imag[:2], imag_in[:2]).astype(BF16)
        by_x, by_y, mine = lax.optimization_barrier((by_x, by_y, mine))
        by_x, by_y = swap(by_x, tri_size, 1), swap(by_y, tri_size, 2)
        mine = add(mine, swap(mine, tri_size, 1)).astype(BF16)
        mine = shift(mine)
        then_y = add(real[2], real_in[2], by_x[1]).astype(BF16)
        then_x = add(imag[2], imag_in[2], by_y[1]).astype(BF16)
        then_y, then_x, mine, last = lax.optimization_barrier((then_y, then_x, mine, last))
        then_y, then_x = swap(then_y[None], tri_size, 2), swap(then_x[None], tri_size, 1)
        mine = add(mine, swap(mine, tri_size, 2)).astype(BF16)
        terms = [(own, 0, 0), (own, 1, 1), (own_in, 0, 0), (own_in, 1, 1)]
        terms += [(by_x, 0, 0), (by_y, 1, 0), (then_y, 0, 0), (then_x, 1, 0)]
    else:
        terms = scatter_plain(partials[0].reshape(tri_size, 2, *amplitudes.shape[1:]), tri_size)
        mine = shift(add(hold, swap(give, tri_size, 0)).astype(BF16))
        for bit in range(1, bits):
            mine = add(mine, swap(mine, tri_size, bit)).astype(BF16)
    base = quadratic(core, [*ring, last], mine, swap(mine, tri_size, 0))
    return finish(base, terms)


def solution(mesh):
    in_specs = (P(None, "tri", "vp"), P("tri", "vp"), P("tri", None, None), P("tri"))
    out_specs = P(None, "tri", "vp")
    body = functools.partial(shards, mesh.shape["tri"], mesh.shape["vp"])
    return jax.shard_map(body, mesh=mesh, in_specs=in_specs, out_specs=out_specs, check_vma=False)
```

```python
import functools

import jax
import jax.numpy as jnp
from jax import lax
from jax.experimental import pallas as pl
from jax.experimental.pallas import tpu as pltpu
from jax.sharding import PartitionSpec as P

NB = 10
BLOCK = 768
PAIRS = NB * BLOCK
TRI_BLOCKS = NB * (NB + 1) // 2
F32 = jnp.float32
BF16 = jnp.bfloat16


def swap(value, axis_size, bit):
    pairs = [(i, i ^ (1 << bit)) for i in range(axis_size)]
    return lax.ppermute(value, "tri", pairs)


def after(value, *earlier):
    return lax.optimization_barrier((value, *earlier))[0]


def stage_kernel(source_ref, target_ref, sem):
    copy = pltpu.make_async_copy(source_ref, target_ref, sem)
    copy.start()
    copy.wait()


def stage(value):
    return pl.pallas_call(
        stage_kernel,
        in_specs=[pl.BlockSpec(memory_space=pl.ANY)],
        out_specs=pl.BlockSpec(memory_space=pltpu.VMEM),
        out_shape=jax.ShapeDtypeStruct(value.shape, value.dtype),
        scratch_shapes=[pltpu.SemaphoreType.DMA],
        compiler_params=pltpu.CompilerParams(vmem_limit_bytes=16 * 1024 * 1024),
        cost_estimate=pl.CostEstimate(flops=0, bytes_accessed=4 * value.size, transcendentals=0),
        name="stage",
    )(value)


def gather_tri(amplitudes, small, axis_size):
    if axis_size != 8:
        found = {0: amplitudes}
        for bit in range(axis_size.bit_length() - 1):
            for mask in list(found):
                found[mask | (1 << bit)] = swap(found[mask], axis_size, bit)
        return [(value, mask, None) for mask, value in found.items()], small
    by_x = swap(amplitudes, axis_size, 1)
    by_y = swap(amplitudes, axis_size, 2)
    own_core = swap(amplitudes, axis_size, 0)
    own = stage(amplitudes)
    by_x, by_y, small, _ = lax.optimization_barrier((by_x, by_y, small, own))
    far_real = swap(by_y[0], axis_size, 1)
    far_imag = swap(by_x[1], axis_size, 2)
    found = [
        (own, 0, None), (by_x, 2, None), (by_y, 4, None), (far_real, 6, 0), (far_imag, 6, 1),
        (own_core, 1, None),
    ]
    for value, mask, part in found[1:5]:
        found.append((swap(value, axis_size, 0), mask | 1, part))
    return found, small


def ladder_kernel(labels, groups, small_ref, *refs):
    count = len(labels)
    piece_refs = refs[:count]
    ladder_ref = refs[count]
    out_refs = refs[count + 1:-3]
    amp, acc, sems = refs[-3:]
    columns = amp.shape[1] // 2
    rows = out_refs[0].shape[-2]
    step = pl.program_id(0)
    me = small_ref[0]

    def rows_of(mask):
        return pl.ds(pl.multiple_of((me ^ mask) * rows, rows), rows)

    @pl.when(step == 0)
    def _():
        copies = []
        for index, (mask, part) in enumerate(labels):
            for which in (0, 1) if part is None else (part,):
                source = piece_refs[index].at[which] if part is None else piece_refs[index]
                lanes = pl.ds(which * columns, columns)
                copy = pltpu.make_async_copy(source, amp.at[rows_of(mask), lanes], sems.at[len(copies)])
                copy.start()
                copies.append(copy)
        acc[...] = jnp.zeros_like(acc)
        for copy in copies:
            copy.wait()

    code = small_ref[1 + step]
    row_block = jnp.int32(0)
    start = jnp.int32(0)
    for row in range(1, NB):
        first = row * NB - row * (row - 1) // 2
        past = code >= first
        row_block = jnp.where(past, row, row_block)
        start = jnp.where(past, first, start)
    column_block = jnp.minimum(row_block + code - start, NB - 1)
    weight = jnp.where(row_block == column_block, 0.5, 1.0) * jnp.where(code < TRI_BLOCKS, 1.0, 0.0)
    at_row = pl.ds(pl.multiple_of(row_block * BLOCK, BLOCK), BLOCK)
    at_column = pl.ds(pl.multiple_of(column_block * BLOCK, BLOCK), BLOCK)
    weight = weight.astype(BF16)
    block = ladder_ref[0]
    column_amp, row_amp = weight * amp[at_column, :], weight * amp[at_row, :]
    acc[at_row, :] += lax.dot_general(block, column_amp, (((1,), (0,)), ((), ())), preferred_element_type=F32)
    acc[at_column, :] += lax.dot_general(block, row_amp, (((0,), (0,)), ((), ())), preferred_element_type=F32)

    @pl.when(step == pl.num_programs(0) - 1)
    def _():
        for target, places in zip(out_refs, groups, strict=True):
            for place, (mask, part) in enumerate(places):
                lanes = slice(part * columns, (part + 1) * columns)
                target[place] = acc[rows_of(mask), lanes].astype(BF16)


def ladder(small, pieces, ladder_blocks, groups):
    slots = ladder_blocks.shape[0]
    rows, columns = pieces[0][0].shape[-2:]
    count = sum(len(places) for places in groups)
    return pl.pallas_call(
        functools.partial(ladder_kernel, [(mask, part) for _, mask, part in pieces], groups),
        grid_spec=pltpu.PrefetchScalarGridSpec(
            num_scalar_prefetch=1,
            grid=(slots,),
            in_specs=[pl.BlockSpec(memory_space=pl.ANY)] * len(pieces)
            + [pl.BlockSpec((1, BLOCK, BLOCK), lambda s, *_: (s, 0, 0))],
            out_specs=[pl.BlockSpec((len(places), rows, columns), lambda s, *_: (0, 0, 0)) for places in groups],
            scratch_shapes=[
                pltpu.VMEM((PAIRS, 2 * columns), BF16),
                pltpu.VMEM((PAIRS, 2 * columns), F32),
                pltpu.SemaphoreType.DMA((count,)),
            ],
        ),
        out_shape=[jax.ShapeDtypeStruct((len(places), rows, columns), BF16) for places in groups],
        compiler_params=pltpu.CompilerParams(
            dimension_semantics=("arbitrary",), vmem_limit_bytes=40 * 1024 * 1024
        ),
        cost_estimate=pl.CostEstimate(
            flops=slots * 8 * BLOCK * BLOCK * columns,
            bytes_accessed=slots * BLOCK * BLOCK * 2 + 8 * PAIRS * columns,
            transcendentals=0,
        ),
        name="ladder",
    )(small, *[value for value, _, _ in pieces], ladder_blocks)


def add(*terms):
    total = terms[0].astype(F32)
    for term in terms[1:]:
        total = total + term.astype(F32)
    return total


def contract_kernel(core_ref, int_ref, last_ref, *refs):
    columns = int_ref.shape[1]
    hold_ref, give_ref = refs[-2:]
    for step in range(len(refs) - 1):
        values, ref = (int_ref, refs[step]) if step < len(refs) - 2 else (last_ref, refs[0])
        both = jnp.concatenate([ref[0], ref[1]], axis=1)
        product = lax.dot_general(values[...], both, (((0,), (0,)), ((), ())), preferred_element_type=F32)
        real = product[:, :columns].astype(BF16)
        imag = product[:, columns:].astype(BF16)
        hold_ref[step] = jnp.where(core_ref[0] == 0, real, imag)
        give_ref[step] = jnp.where(core_ref[0] == 0, imag, real)


def contract(core, integrals, back_integrals, ring):
    rows, columns = integrals.shape
    vmem = pl.BlockSpec(memory_space=pltpu.VMEM)
    count = len(ring) + 1
    return pl.pallas_call(
        contract_kernel,
        in_specs=[pl.BlockSpec(memory_space=pltpu.SMEM)] + [vmem] * (2 + len(ring)),
        out_specs=[vmem] * 2,
        out_shape=[jax.ShapeDtypeStruct((count, columns, columns), BF16)] * 2,
        compiler_params=pltpu.CompilerParams(vmem_limit_bytes=20 * 1024 * 1024),
        cost_estimate=pl.CostEstimate(
            flops=4 * count * rows * columns * columns,
            bytes_accessed=4 * count * rows * columns,
            transcendentals=0,
        ),
        name="contract",
    )(core, integrals, back_integrals, *ring)


def quadratic_kernel(core_ref, mine_ref, other_ref, *refs):
    amp_ref, out_ref = refs[0], refs[-1]
    _, rows, columns = amp_ref.shape
    vp_size = len(refs) - 1
    core = core_ref[0]
    total = jnp.zeros((rows, 2 * columns), F32)
    for step in range(vp_size):
        both = jnp.concatenate([refs[step][0], refs[step][1]], axis=1)
        source = (vp_size - step) % vp_size
        real = jnp.where(core == 0, mine_ref[source], other_ref[source])
        imag = jnp.where(core == 0, other_ref[source], mine_ref[source])
        weights = jnp.concatenate(
            [jnp.concatenate([real, imag], axis=1), jnp.concatenate([-imag, real], axis=1)], axis=0
        )
        total += jnp.dot(both, weights, preferred_element_type=F32)
    out_ref[0] = amp_ref[0].astype(F32) + 0.25 * total[:, columns:]
    out_ref[1] = amp_ref[1].astype(F32) - 0.25 * total[:, :columns]


def quadratic(core, ring, mine, other):
    vmem = pl.BlockSpec(memory_space=pltpu.VMEM)
    size = ring[0].size
    return pl.pallas_call(
        quadratic_kernel,
        in_specs=[pl.BlockSpec(memory_space=pltpu.SMEM)] + [vmem] * (2 + len(ring)),
        out_specs=vmem,
        out_shape=jax.ShapeDtypeStruct(ring[0].shape, F32),
        compiler_params=pltpu.CompilerParams(vmem_limit_bytes=20 * 1024 * 1024),
        cost_estimate=pl.CostEstimate(
            flops=4 * len(ring) * size * ring[0].shape[2],
            bytes_accessed=(2 * len(ring) + 4) * size,
            transcendentals=0,
        ),
        name="quadratic",
    )(core, mine, other, *ring)


def finish_kernel(places, base_ref, *refs):
    sums = [0.0, 0.0]
    for ref, (_, part, place) in zip(refs, places, strict=False):
        sums[part] = sums[part] + ref[place].astype(F32)
    refs[-1][0] = (base_ref[0] + 0.5 * sums[1]).astype(BF16)
    refs[-1][1] = (base_ref[1] - 0.5 * sums[0]).astype(BF16)


def finish(base, terms):
    vmem = pl.BlockSpec(memory_space=pltpu.VMEM)
    return pl.pallas_call(
        functools.partial(finish_kernel, [(None, part, place) for _, part, place in terms]),
        in_specs=[vmem] * (1 + len(terms)),
        out_specs=vmem,
        out_shape=jax.ShapeDtypeStruct(base.shape, BF16),
        compiler_params=pltpu.CompilerParams(vmem_limit_bytes=20 * 1024 * 1024),
        name="finish",
    )(base, *[value for value, _, _ in terms])


def scatter_plain(partial, tri_size):
    terms = [partial]
    for bit in reversed(range(tri_size.bit_length() - 1)):
        half = terms[0].shape[0] // 2
        outgoing = add(*[term[half:] for term in terms]).astype(BF16)
        terms = [term[:half] for term in terms] + [swap(outgoing, tri_size, bit)]
    return [(term[0], part, part) for term in terms for part in range(2)]


def shards(tri_size, vp_size, amplitudes, integrals, ladder_blocks, slot_block):
    bits = tri_size.bit_length() - 1
    me = lax.axis_index("tri").astype(jnp.int32)[None]
    core = me & 1
    order = list(range(0, vp_size, 2)) + list(range(1, vp_size, 2))[::-1]

    def turn(value, distance=1):
        return lax.ppermute(value, "vp", [(order[i], order[(i + distance) % vp_size]) for i in range(vp_size)])

    ring = [amplitudes]
    for _ in range(2, vp_size):
        ring.append(turn(ring[-1]))
    back_integrals = turn(integrals)
    pieces, small = gather_tri(amplitudes, jnp.concatenate([me, slot_block]), tri_size)
    small = after(small, ring[1], back_integrals)
    ring[0] = pieces[0][0]

    if tri_size == 8:
        real_order, imag_order = (2, 6, 4), (4, 6, 2)
        groups = [[(mask | 1, 0) for mask in real_order], [(mask | 1, 1) for mask in imag_order], [(1, 0), (1, 1)]]
        groups += [[(mask, 0) for mask in real_order], [(mask, 1) for mask in imag_order], [(0, 0), (0, 1)]]
    else:
        groups = [[(mask, part) for mask in range(tri_size) for part in range(2)]]
    partials = ladder(small, pieces, ladder_blocks, groups)
    *partials, ring[-1] = lax.optimization_barrier((*partials, ring[-1]))
    hold, give = contract(core, integrals, back_integrals, ring)

    def shift(value):
        moved = [turn(value[step], vp_size - step) for step in range(1, vp_size - 1)]
        return jnp.stack([value[0], *moved, value[vp_size - 1]])

    if tri_size == 8:
        real, imag, own = partials[3:]
        real_in, imag_in, own_in = (swap(value, tri_size, 0) for value in partials[:3])
        real_in, imag_in, hold, give = lax.optimization_barrier((real_in, imag_in, hold, give))
        by_x = add(real[:2], real_in[:2]).astype(BF16)
        by_y = add(imag[:2], imag_in[:2]).astype(BF16)
        by_x, by_y, hold, give = lax.optimization_barrier((by_x, by_y, hold, give))
        by_x, by_y = swap(by_x, tri_size, 1), swap(by_y, tri_size, 2)
        mine = shift(add(hold, swap(give, tri_size, 0)).astype(BF16))
        last = turn(after(ring[-1], mine))
        received = swap(mine, tri_size, 1)
        then_y = add(real[2], real_in[2], by_x[1]).astype(BF16)
        then_x = add(imag[2], imag_in[2], by_y[1]).astype(BF16)
        then_y, then_x, received = lax.optimization_barrier((then_y, then_x, received))
        then_y, then_x = swap(then_y[None], tri_size, 2), swap(then_x[None], tri_size, 1)
        mine = add(mine, received).astype(BF16)
        received, last = lax.optimization_barrier((swap(mine, tri_size, 2), last))
        mine = add(mine, received).astype(BF16)
        terms = [(own, 0, 0), (own, 1, 1), (own_in, 0, 0), (own_in, 1, 1)]
        terms += [(by_x, 0, 0), (by_y, 1, 0), (then_y, 0, 0), (then_x, 1, 0)]
    else:
        last = turn(ring[-1])
        terms = scatter_plain(partials[0].reshape(tri_size, 2, *amplitudes.shape[1:]), tri_size)
        mine = shift(add(hold, swap(give, tri_size, 0)).astype(BF16))
        for bit in range(1, bits):
            mine = add(mine, swap(mine, tri_size, bit)).astype(BF16)
    base = quadratic(core, [*ring, last], mine, swap(mine, tri_size, 0))
    return finish(base, terms)


def solution(mesh):
    in_specs = (P(None, "tri", "vp"), P("tri", "vp"), P("tri", None, None), P("tri"))
    out_specs = P(None, "tri", "vp")
    body = functools.partial(shards, mesh.shape["tri"], mesh.shape["vp"])
    return jax.shard_map(body, mesh=mesh, in_specs=in_specs, out_specs=out_specs, check_vma=False)
```

```python
import functools

import jax
import jax.numpy as jnp
from jax import lax
from jax.experimental import pallas as pl
from jax.experimental.pallas import tpu as pltpu
from jax.sharding import PartitionSpec as P

NB = 10
BLOCK = 768
PAIRS = NB * BLOCK
TRI_BLOCKS = NB * (NB + 1) // 2
F32 = jnp.float32
BF16 = jnp.bfloat16


def swap(value, axis_size, bit):
    pairs = [(i, i ^ (1 << bit)) for i in range(axis_size)]
    return lax.ppermute(value, "tri", pairs)


def after(value, *earlier):
    return lax.optimization_barrier((value, *earlier))[0]


def stage_kernel(source_ref, target_ref, sem):
    copy = pltpu.make_async_copy(source_ref, target_ref, sem)
    copy.start()
    copy.wait()


def stage(value):
    return pl.pallas_call(
        stage_kernel,
        in_specs=[pl.BlockSpec(memory_space=pl.ANY)],
        out_specs=pl.BlockSpec(memory_space=pltpu.VMEM),
        out_shape=jax.ShapeDtypeStruct(value.shape, value.dtype),
        scratch_shapes=[pltpu.SemaphoreType.DMA],
        compiler_params=pltpu.CompilerParams(vmem_limit_bytes=16 * 1024 * 1024),
        cost_estimate=pl.CostEstimate(flops=0, bytes_accessed=4 * value.size, transcendentals=0),
        name="stage",
    )(value)


def gather_tri(amplitudes, small, axis_size):
    if axis_size != 8:
        found = {0: amplitudes}
        for bit in range(axis_size.bit_length() - 1):
            for mask in list(found):
                found[mask | (1 << bit)] = swap(found[mask], axis_size, bit)
        return [(value, mask, None) for mask, value in found.items()], small
    by_x = swap(amplitudes, axis_size, 1)
    by_y = swap(amplitudes, axis_size, 2)
    own_core = swap(amplitudes, axis_size, 0)
    own = stage(amplitudes)
    by_x, by_y, small, _ = lax.optimization_barrier((by_x, by_y, small, own))
    far_real = swap(by_y[0], axis_size, 1)
    far_imag = swap(by_x[1], axis_size, 2)
    found = [
        (own, 0, None), (by_x, 2, None), (by_y, 4, None), (far_real, 6, 0), (far_imag, 6, 1),
        (own_core, 1, None),
    ]
    for value, mask, part in found[1:5]:
        found.append((swap(value, axis_size, 0), mask | 1, part))
    return found, small


def ladder_kernel(labels, groups, small_ref, *refs):
    count = len(labels)
    piece_refs = refs[:count]
    ladder_ref = refs[count]
    out_refs = refs[count + 1:-3]
    amp, acc, sems = refs[-3:]
    columns = amp.shape[1] // 2
    rows = out_refs[0].shape[-2]
    step = pl.program_id(0)
    me = small_ref[0]

    def rows_of(mask):
        return pl.ds(pl.multiple_of((me ^ mask) * rows, rows), rows)

    @pl.when(step == 0)
    def _():
        copies = []
        for index, (mask, part) in enumerate(labels):
            for which in (0, 1) if part is None else (part,):
                source = piece_refs[index].at[which] if part is None else piece_refs[index]
                lanes = pl.ds(which * columns, columns)
                copy = pltpu.make_async_copy(source, amp.at[rows_of(mask), lanes], sems.at[len(copies)])
                copy.start()
                copies.append(copy)
        acc[...] = jnp.zeros_like(acc)
        for copy in copies:
            copy.wait()

    code = small_ref[1 + step]
    row_block = jnp.int32(0)
    start = jnp.int32(0)
    for row in range(1, NB):
        first = row * NB - row * (row - 1) // 2
        past = code >= first
        row_block = jnp.where(past, row, row_block)
        start = jnp.where(past, first, start)
    column_block = jnp.minimum(row_block + code - start, NB - 1)
    weight = jnp.where(row_block == column_block, 0.5, 1.0) * jnp.where(code < TRI_BLOCKS, 1.0, 0.0)
    at_row = pl.ds(pl.multiple_of(row_block * BLOCK, BLOCK), BLOCK)
    at_column = pl.ds(pl.multiple_of(column_block * BLOCK, BLOCK), BLOCK)
    weight = weight.astype(BF16)
    block = ladder_ref[0]
    column_amp, row_amp = weight * amp[at_column, :], weight * amp[at_row, :]
    chunk = BLOCK // 3
    for first in range(0, BLOCK, chunk):
        span = slice(first, first + chunk)
        here = pl.ds(pl.multiple_of(row_block * BLOCK + first, chunk), chunk)
        acc[here, :] += jnp.dot(block[span], column_amp, preferred_element_type=F32)
        here = pl.ds(pl.multiple_of(column_block * BLOCK + first, chunk), chunk)
        acc[here, :] += lax.dot_general(
            block[:, span], row_amp, (((0,), (0,)), ((), ())), preferred_element_type=F32
        )

    @pl.when(step == pl.num_programs(0) - 1)
    def _():
        for target, places in zip(out_refs, groups, strict=True):
            for place, (mask, part) in enumerate(places):
                lanes = slice(part * columns, (part + 1) * columns)
                target[place] = acc[rows_of(mask), lanes].astype(BF16)


def ladder(small, pieces, ladder_blocks, groups):
    slots = ladder_blocks.shape[0]
    rows, columns = pieces[0][0].shape[-2:]
    count = sum(len(places) for places in groups)
    return pl.pallas_call(
        functools.partial(ladder_kernel, [(mask, part) for _, mask, part in pieces], groups),
        grid_spec=pltpu.PrefetchScalarGridSpec(
            num_scalar_prefetch=1,
            grid=(slots,),
            in_specs=[pl.BlockSpec(memory_space=pl.ANY)] * len(pieces)
            + [pl.BlockSpec((1, BLOCK, BLOCK), lambda s, *_: (s, 0, 0))],
            out_specs=[pl.BlockSpec((len(places), rows, columns), lambda s, *_: (0, 0, 0)) for places in groups],
            scratch_shapes=[
                pltpu.VMEM((PAIRS, 2 * columns), BF16),
                pltpu.VMEM((PAIRS, 2 * columns), F32),
                pltpu.SemaphoreType.DMA((count,)),
            ],
        ),
        out_shape=[jax.ShapeDtypeStruct((len(places), rows, columns), BF16) for places in groups],
        compiler_params=pltpu.CompilerParams(
            dimension_semantics=("arbitrary",), vmem_limit_bytes=40 * 1024 * 1024
        ),
        cost_estimate=pl.CostEstimate(
            flops=slots * 8 * BLOCK * BLOCK * columns,
            bytes_accessed=slots * BLOCK * BLOCK * 2 + 8 * PAIRS * columns,
            transcendentals=0,
        ),
        name="ladder",
    )(small, *[value for value, _, _ in pieces], ladder_blocks)


def add(*terms):
    total = terms[0].astype(F32)
    for term in terms[1:]:
        total = total + term.astype(F32)
    return total


def contract_kernel(core_ref, int_ref, last_ref, *refs):
    columns = int_ref.shape[1]
    hold_ref, give_ref = refs[-2:]
    for step in range(len(refs) - 1):
        values, ref = (int_ref, refs[step]) if step < len(refs) - 2 else (last_ref, refs[0])
        both = jnp.concatenate([ref[0], ref[1]], axis=1)
        product = lax.dot_general(values[...], both, (((0,), (0,)), ((), ())), preferred_element_type=F32)
        real = product[:, :columns].astype(BF16)
        imag = product[:, columns:].astype(BF16)
        hold_ref[step] = jnp.where(core_ref[0] == 0, real, imag)
        give_ref[step] = jnp.where(core_ref[0] == 0, imag, real)


def contract(core, integrals, back_integrals, ring):
    rows, columns = integrals.shape
    vmem = pl.BlockSpec(memory_space=pltpu.VMEM)
    count = len(ring) + 1
    return pl.pallas_call(
        contract_kernel,
        in_specs=[pl.BlockSpec(memory_space=pltpu.SMEM)] + [vmem] * (2 + len(ring)),
        out_specs=[vmem] * 2,
        out_shape=[jax.ShapeDtypeStruct((count, columns, columns), BF16)] * 2,
        compiler_params=pltpu.CompilerParams(vmem_limit_bytes=20 * 1024 * 1024),
        cost_estimate=pl.CostEstimate(
            flops=4 * count * rows * columns * columns,
            bytes_accessed=4 * count * rows * columns,
            transcendentals=0,
        ),
        name="contract",
    )(core, integrals, back_integrals, *ring)


def quadratic_kernel(core_ref, mine_ref, other_ref, *refs):
    amp_ref, out_ref = refs[0], refs[-1]
    _, rows, columns = amp_ref.shape
    vp_size = len(refs) - 1
    core = core_ref[0]
    total = jnp.zeros((rows, 2 * columns), F32)
    for step in range(vp_size):
        both = jnp.concatenate([refs[step][0], refs[step][1]], axis=1)
        source = (vp_size - step) % vp_size
        real = jnp.where(core == 0, mine_ref[source], other_ref[source])
        imag = jnp.where(core == 0, other_ref[source], mine_ref[source])
        weights = jnp.concatenate(
            [jnp.concatenate([real, imag], axis=1), jnp.concatenate([-imag, real], axis=1)], axis=0
        )
        total += jnp.dot(both, weights, preferred_element_type=F32)
    out_ref[0] = amp_ref[0].astype(F32) + 0.25 * total[:, columns:]
    out_ref[1] = amp_ref[1].astype(F32) - 0.25 * total[:, :columns]


def quadratic(core, ring, mine, other):
    vmem = pl.BlockSpec(memory_space=pltpu.VMEM)
    size = ring[0].size
    return pl.pallas_call(
        quadratic_kernel,
        in_specs=[pl.BlockSpec(memory_space=pltpu.SMEM)] + [vmem] * (2 + len(ring)),
        out_specs=vmem,
        out_shape=jax.ShapeDtypeStruct(ring[0].shape, F32),
        compiler_params=pltpu.CompilerParams(vmem_limit_bytes=20 * 1024 * 1024),
        cost_estimate=pl.CostEstimate(
            flops=4 * len(ring) * size * ring[0].shape[2],
            bytes_accessed=(2 * len(ring) + 4) * size,
            transcendentals=0,
        ),
        name="quadratic",
    )(core, mine, other, *ring)


def finish_kernel(places, base_ref, *refs):
    sums = [0.0, 0.0]
    for ref, (_, part, place) in zip(refs, places, strict=False):
        sums[part] = sums[part] + ref[place].astype(F32)
    refs[-1][0] = (base_ref[0] + 0.5 * sums[1]).astype(BF16)
    refs[-1][1] = (base_ref[1] - 0.5 * sums[0]).astype(BF16)


def finish(base, terms):
    vmem = pl.BlockSpec(memory_space=pltpu.VMEM)
    return pl.pallas_call(
        functools.partial(finish_kernel, [(None, part, place) for _, part, place in terms]),
        in_specs=[vmem] * (1 + len(terms)),
        out_specs=vmem,
        out_shape=jax.ShapeDtypeStruct(base.shape, BF16),
        compiler_params=pltpu.CompilerParams(vmem_limit_bytes=20 * 1024 * 1024),
        name="finish",
    )(base, *[value for value, _, _ in terms])


def scatter_plain(partial, tri_size):
    terms = [partial]
    for bit in reversed(range(tri_size.bit_length() - 1)):
        half = terms[0].shape[0] // 2
        outgoing = add(*[term[half:] for term in terms]).astype(BF16)
        terms = [term[:half] for term in terms] + [swap(outgoing, tri_size, bit)]
    return [(term[0], part, part) for term in terms for part in range(2)]


def shards(tri_size, vp_size, amplitudes, integrals, ladder_blocks, slot_block):
    bits = tri_size.bit_length() - 1
    me = lax.axis_index("tri").astype(jnp.int32)[None]
    core = me & 1
    order = list(range(0, vp_size, 2)) + list(range(1, vp_size, 2))[::-1]

    def turn(value, distance=1):
        return lax.ppermute(value, "vp", [(order[i], order[(i + distance) % vp_size]) for i in range(vp_size)])

    ring = [amplitudes]
    for _ in range(2, vp_size):
        ring.append(turn(ring[-1]))
    back_integrals = turn(integrals)
    pieces, small = gather_tri(amplitudes, jnp.concatenate([me, slot_block]), tri_size)
    small = after(small, ring[1], back_integrals)
    ring[0] = pieces[0][0]

    if tri_size == 8:
        real_order, imag_order = (2, 6, 4), (4, 6, 2)
        groups = [[(mask | 1, 0) for mask in real_order], [(mask | 1, 1) for mask in imag_order], [(1, 0), (1, 1)]]
        groups += [[(mask, 0) for mask in real_order], [(mask, 1) for mask in imag_order], [(0, 0), (0, 1)]]
    else:
        groups = [[(mask, part) for mask in range(tri_size) for part in range(2)]]
    partials = ladder(small, pieces, ladder_blocks, groups)
    *partials, ring[-1] = lax.optimization_barrier((*partials, ring[-1]))
    hold, give = contract(core, integrals, back_integrals, ring)

    def shift(value):
        moved = [turn(value[step], vp_size - step) for step in range(1, vp_size - 1)]
        return jnp.stack([value[0], *moved, value[vp_size - 1]])

    if tri_size == 8:
        real, imag, own = partials[3:]
        real_in, imag_in, own_in = (swap(value, tri_size, 0) for value in partials[:3])
        real_in, imag_in, hold, give = lax.optimization_barrier((real_in, imag_in, hold, give))
        far_x, far_y, near_x, near_y = (
            add(kept[i], came[i]).astype(BF16)[None]
            for i, kept, came in ((1, real, real_in), (1, imag, imag_in), (0, real, real_in), (0, imag, imag_in))
        )
        far_x, far_y, near_x, near_y, hold, give = lax.optimization_barrier(
            (far_x, far_y, near_x, near_y, hold, give)
        )
        far_x, far_y = swap(far_x, tri_size, 1), swap(far_y, tri_size, 2)
        near_x, near_y = swap(near_x, tri_size, 1), swap(near_y, tri_size, 2)
        mine = shift(add(hold, swap(give, tri_size, 0)).astype(BF16))
        mine, far_x, far_y = lax.optimization_barrier((mine, far_x, far_y))
        last = turn(after(ring[-1], mine))
        then_y = swap(add(real[2], real_in[2], far_x[0]).astype(BF16)[None], tri_size, 2)
        then_x = swap(add(imag[2], imag_in[2], far_y[0]).astype(BF16)[None], tri_size, 1)
        mine = add(mine, swap(mine, tri_size, 1)).astype(BF16)
        received, last, then_y, then_x, near_x, near_y = lax.optimization_barrier(
            (swap(mine, tri_size, 2), last, then_y, then_x, near_x, near_y)
        )
        mine = add(mine, received).astype(BF16)
        terms = [(own, 0, 0), (own, 1, 1), (own_in, 0, 0), (own_in, 1, 1)]
        terms += [(near_x, 0, 0), (near_y, 1, 0), (then_y, 0, 0), (then_x, 1, 0)]
    else:
        last = turn(ring[-1])
        terms = scatter_plain(partials[0].reshape(tri_size, 2, *amplitudes.shape[1:]), tri_size)
        mine = shift(add(hold, swap(give, tri_size, 0)).astype(BF16))
        for bit in range(1, bits):
            mine = add(mine, swap(mine, tri_size, bit)).astype(BF16)
    base = quadratic(core, [*ring, last], mine, swap(mine, tri_size, 0))
    return finish(base, terms)


def solution(mesh):
    in_specs = (P(None, "tri", "vp"), P("tri", "vp"), P("tri", None, None), P("tri"))
    out_specs = P(None, "tri", "vp")
    body = functools.partial(shards, mesh.shape["tri"], mesh.shape["vp"])
    return jax.shard_map(body, mesh=mesh, in_specs=in_specs, out_specs=out_specs, check_vma=False)
```

```python
import functools

import jax
import jax.numpy as jnp
from jax import lax
from jax.experimental import pallas as pl
from jax.experimental.pallas import tpu as pltpu
from jax.sharding import PartitionSpec as P

NB = 10
BLOCK = 768
PAIRS = NB * BLOCK
TRI_BLOCKS = NB * (NB + 1) // 2
F32 = jnp.float32
BF16 = jnp.bfloat16


def swap(value, axis_size, bit):
    pairs = [(i, i ^ (1 << bit)) for i in range(axis_size)]
    return lax.ppermute(value, "tri", pairs)


def after(value, *earlier):
    return lax.optimization_barrier((value, *earlier))[0]


def stage_kernel(source_ref, target_ref, sem):
    copy = pltpu.make_async_copy(source_ref, target_ref, sem)
    copy.start()
    copy.wait()


def stage(value):
    return pl.pallas_call(
        stage_kernel,
        in_specs=[pl.BlockSpec(memory_space=pl.ANY)],
        out_specs=pl.BlockSpec(memory_space=pltpu.VMEM),
        out_shape=jax.ShapeDtypeStruct(value.shape, value.dtype),
        scratch_shapes=[pltpu.SemaphoreType.DMA],
        compiler_params=pltpu.CompilerParams(vmem_limit_bytes=16 * 1024 * 1024),
        cost_estimate=pl.CostEstimate(flops=0, bytes_accessed=4 * value.size, transcendentals=0),
        name="stage",
    )(value)


def gather_tri(amplitudes, small, axis_size):
    if axis_size != 8:
        found = {0: amplitudes}
        for bit in range(axis_size.bit_length() - 1):
            for mask in list(found):
                found[mask | (1 << bit)] = swap(found[mask], axis_size, bit)
        return [(value, mask, None) for mask, value in found.items()], small
    by_x = swap(amplitudes, axis_size, 1)
    by_y = swap(amplitudes, axis_size, 2)
    own_core = swap(amplitudes, axis_size, 0)
    own = stage(amplitudes)
    by_x, by_y, small, _ = lax.optimization_barrier((by_x, by_y, small, own))
    far_real = swap(by_y[0], axis_size, 1)
    far_imag = swap(by_x[1], axis_size, 2)
    found = [
        (own, 0, None), (by_x, 2, None), (by_y, 4, None), (far_real, 6, 0), (far_imag, 6, 1),
        (own_core, 1, None),
    ]
    for value, mask, part in found[1:5]:
        found.append((swap(value, axis_size, 0), mask | 1, part))
    return found, small


def ladder_kernel(labels, groups, small_ref, *refs):
    count = len(labels)
    piece_refs = refs[:count]
    ladder_ref = refs[count]
    out_refs = refs[count + 1:-2]
    amp, acc = refs[-2:]
    columns = amp.shape[1] // 2
    rows = out_refs[0].shape[-2]
    step = pl.program_id(0)
    me = small_ref[0]

    def rows_of(mask):
        return pl.ds(pl.multiple_of((me ^ mask) * rows, rows), rows)

    @pl.when(step == 0)
    def _():
        for ref, (mask, part) in zip(piece_refs, labels, strict=True):
            for which in (0, 1) if part is None else (part,):
                value = ref[which] if part is None else ref[...]
                amp[rows_of(mask), which * columns:(which + 1) * columns] = value
        acc[...] = jnp.zeros_like(acc)

    code = small_ref[1 + step]
    row_block = jnp.int32(0)
    start = jnp.int32(0)
    for row in range(1, NB):
        first = row * NB - row * (row - 1) // 2
        past = code >= first
        row_block = jnp.where(past, row, row_block)
        start = jnp.where(past, first, start)
    column_block = jnp.minimum(row_block + code - start, NB - 1)
    weight = jnp.where(row_block == column_block, 0.5, 1.0) * jnp.where(code < TRI_BLOCKS, 1.0, 0.0)
    at_row = pl.ds(pl.multiple_of(row_block * BLOCK, BLOCK), BLOCK)
    at_column = pl.ds(pl.multiple_of(column_block * BLOCK, BLOCK), BLOCK)
    weight = weight.astype(BF16)
    block = ladder_ref[0]
    column_amp, row_amp = weight * amp[at_column, :], weight * amp[at_row, :]
    chunk = BLOCK // 3
    for first in range(0, BLOCK, chunk):
        span = slice(first, first + chunk)
        here = pl.ds(pl.multiple_of(row_block * BLOCK + first, chunk), chunk)
        acc[here, :] += jnp.dot(block[span], column_amp, preferred_element_type=F32)
        here = pl.ds(pl.multiple_of(column_block * BLOCK + first, chunk), chunk)
        acc[here, :] += lax.dot_general(
            block[:, span], row_amp, (((0,), (0,)), ((), ())), preferred_element_type=F32
        )

    @pl.when(step == pl.num_programs(0) - 1)
    def _():
        for target, places in zip(out_refs, groups, strict=True):
            for place, (mask, part) in enumerate(places):
                lanes = slice(part * columns, (part + 1) * columns)
                target[place] = acc[rows_of(mask), lanes].astype(BF16)


def ladder(small, pieces, ladder_blocks, groups):
    slots = ladder_blocks.shape[0]
    rows, columns = pieces[0][0].shape[-2:]
    return pl.pallas_call(
        functools.partial(ladder_kernel, [(mask, part) for _, mask, part in pieces], groups),
        grid_spec=pltpu.PrefetchScalarGridSpec(
            num_scalar_prefetch=1,
            grid=(slots,),
            in_specs=[pl.BlockSpec(memory_space=pltpu.VMEM)] * len(pieces)
            + [pl.BlockSpec((1, BLOCK, BLOCK), lambda s, *_: (s, 0, 0))],
            out_specs=[pl.BlockSpec((len(places), rows, columns), lambda s, *_: (0, 0, 0)) for places in groups],
            scratch_shapes=[
                pltpu.VMEM((PAIRS, 2 * columns), BF16),
                pltpu.VMEM((PAIRS, 2 * columns), F32),
            ],
        ),
        out_shape=[jax.ShapeDtypeStruct((len(places), rows, columns), BF16) for places in groups],
        compiler_params=pltpu.CompilerParams(
            dimension_semantics=("arbitrary",), vmem_limit_bytes=40 * 1024 * 1024
        ),
        cost_estimate=pl.CostEstimate(
            flops=slots * 8 * BLOCK * BLOCK * columns,
            bytes_accessed=slots * BLOCK * BLOCK * 2 + 8 * PAIRS * columns,
            transcendentals=0,
        ),
        name="ladder",
    )(small, *[value for value, _, _ in pieces], ladder_blocks)


def add(*terms):
    total = terms[0].astype(F32)
    for term in terms[1:]:
        total = total + term.astype(F32)
    return total


def contract_kernel(core_ref, int_ref, last_ref, *refs):
    columns = int_ref.shape[1]
    hold_ref, give_ref = refs[-2:]
    for step in range(len(refs) - 1):
        values, ref = (int_ref, refs[step]) if step < len(refs) - 2 else (last_ref, refs[0])
        both = jnp.concatenate([ref[0], ref[1]], axis=1)
        product = lax.dot_general(values[...], both, (((0,), (0,)), ((), ())), preferred_element_type=F32)
        real = product[:, :columns].astype(BF16)
        imag = product[:, columns:].astype(BF16)
        hold_ref[step] = jnp.where(core_ref[0] == 0, real, imag)
        give_ref[step] = jnp.where(core_ref[0] == 0, imag, real)


def contract(core, integrals, back_integrals, ring):
    rows, columns = integrals.shape
    vmem = pl.BlockSpec(memory_space=pltpu.VMEM)
    count = len(ring) + 1
    return pl.pallas_call(
        contract_kernel,
        in_specs=[pl.BlockSpec(memory_space=pltpu.SMEM)] + [vmem] * (2 + len(ring)),
        out_specs=[vmem] * 2,
        out_shape=[jax.ShapeDtypeStruct((count, columns, columns), BF16)] * 2,
        compiler_params=pltpu.CompilerParams(vmem_limit_bytes=20 * 1024 * 1024),
        cost_estimate=pl.CostEstimate(
            flops=4 * count * rows * columns * columns,
            bytes_accessed=4 * count * rows * columns,
            transcendentals=0,
        ),
        name="contract",
    )(core, integrals, back_integrals, *ring)


def quadratic_kernel(core_ref, mine_ref, other_ref, *refs):
    amp_ref, out_ref = refs[0], refs[-1]
    _, rows, columns = amp_ref.shape
    vp_size = len(refs) - 1
    core = core_ref[0]
    total = jnp.zeros((rows, 2 * columns), F32)
    for step in range(vp_size):
        both = jnp.concatenate([refs[step][0], refs[step][1]], axis=1)
        source = (vp_size - step) % vp_size
        real = jnp.where(core == 0, mine_ref[source], other_ref[source])
        imag = jnp.where(core == 0, other_ref[source], mine_ref[source])
        weights = jnp.concatenate(
            [jnp.concatenate([real, imag], axis=1), jnp.concatenate([-imag, real], axis=1)], axis=0
        )
        total += jnp.dot(both, weights, preferred_element_type=F32)
    out_ref[0] = amp_ref[0].astype(F32) + 0.25 * total[:, columns:]
    out_ref[1] = amp_ref[1].astype(F32) - 0.25 * total[:, :columns]


def quadratic(core, ring, mine, other):
    vmem = pl.BlockSpec(memory_space=pltpu.VMEM)
    size = ring[0].size
    return pl.pallas_call(
        quadratic_kernel,
        in_specs=[pl.BlockSpec(memory_space=pltpu.SMEM)] + [vmem] * (2 + len(ring)),
        out_specs=vmem,
        out_shape=jax.ShapeDtypeStruct(ring[0].shape, F32),
        compiler_params=pltpu.CompilerParams(vmem_limit_bytes=20 * 1024 * 1024),
        cost_estimate=pl.CostEstimate(
            flops=4 * len(ring) * size * ring[0].shape[2],
            bytes_accessed=(2 * len(ring) + 4) * size,
            transcendentals=0,
        ),
        name="quadratic",
    )(core, mine, other, *ring)


def finish_kernel(places, base_ref, *refs):
    sums = [0.0, 0.0]
    for ref, (_, part, place) in zip(refs, places, strict=False):
        sums[part] = sums[part] + ref[place].astype(F32)
    refs[-1][0] = (base_ref[0] + 0.5 * sums[1]).astype(BF16)
    refs[-1][1] = (base_ref[1] - 0.5 * sums[0]).astype(BF16)


def finish(base, terms):
    vmem = pl.BlockSpec(memory_space=pltpu.VMEM)
    return pl.pallas_call(
        functools.partial(finish_kernel, [(None, part, place) for _, part, place in terms]),
        in_specs=[vmem] * (1 + len(terms)),
        out_specs=vmem,
        out_shape=jax.ShapeDtypeStruct(base.shape, BF16),
        compiler_params=pltpu.CompilerParams(vmem_limit_bytes=20 * 1024 * 1024),
        name="finish",
    )(base, *[value for value, _, _ in terms])


def scatter_plain(partial, tri_size):
    terms = [partial]
    for bit in reversed(range(tri_size.bit_length() - 1)):
        half = terms[0].shape[0] // 2
        outgoing = add(*[term[half:] for term in terms]).astype(BF16)
        terms = [term[:half] for term in terms] + [swap(outgoing, tri_size, bit)]
    return [(term[0], part, part) for term in terms for part in range(2)]


def shards(tri_size, vp_size, amplitudes, integrals, ladder_blocks, slot_block):
    bits = tri_size.bit_length() - 1
    me = lax.axis_index("tri").astype(jnp.int32)[None]
    core = me & 1
    order = list(range(0, vp_size, 2)) + list(range(1, vp_size, 2))[::-1]

    def turn(value, distance=1):
        return lax.ppermute(value, "vp", [(order[i], order[(i + distance) % vp_size]) for i in range(vp_size)])

    ring = [amplitudes]
    for _ in range(2, vp_size):
        ring.append(turn(ring[-1]))
    back_integrals = turn(integrals)
    pieces, small = gather_tri(amplitudes, jnp.concatenate([me, slot_block]), tri_size)
    small = after(small, ring[1], back_integrals)
    ring[0] = pieces[0][0]

    if tri_size == 8:
        real_order, imag_order = (2, 6, 4), (4, 6, 2)
        groups = [[(mask | 1, 0) for mask in real_order], [(mask | 1, 1) for mask in imag_order], [(1, 0), (1, 1)]]
        groups += [[(mask, 0) for mask in real_order], [(mask, 1) for mask in imag_order], [(0, 0), (0, 1)]]
    else:
        groups = [[(mask, part) for mask in range(tri_size) for part in range(2)]]
    partials = ladder(small, pieces, ladder_blocks, groups)
    *partials, ring[-1] = lax.optimization_barrier((*partials, ring[-1]))
    hold, give = contract(core, integrals, back_integrals, ring)

    def shift(value):
        moved = [turn(value[step], vp_size - step) for step in range(1, vp_size - 1)]
        return jnp.stack([value[0], *moved, value[vp_size - 1]])

    if tri_size == 8:
        real, imag, own = partials[3:]
        real_in, imag_in, own_in = (swap(value, tri_size, 0) for value in partials[:3])
        real_in, imag_in, hold, give = lax.optimization_barrier((real_in, imag_in, hold, give))
        far_x, far_y, near_x, near_y = (
            add(kept[i], came[i]).astype(BF16)[None]
            for i, kept, came in ((1, real, real_in), (1, imag, imag_in), (0, real, real_in), (0, imag, imag_in))
        )
        far_x, far_y, near_x, near_y, hold, give = lax.optimization_barrier(
            (far_x, far_y, near_x, near_y, hold, give)
        )
        far_x, far_y = swap(far_x, tri_size, 1), swap(far_y, tri_size, 2)
        near_x, near_y = swap(near_x, tri_size, 1), swap(near_y, tri_size, 2)
        mine = shift(add(hold, swap(give, tri_size, 0)).astype(BF16))
        mine, far_x, far_y = lax.optimization_barrier((mine, far_x, far_y))
        last = turn(after(ring[-1], mine))
        then_y = swap(add(real[2], real_in[2], far_x[0]).astype(BF16)[None], tri_size, 2)
        then_x = swap(add(imag[2], imag_in[2], far_y[0]).astype(BF16)[None], tri_size, 1)
        mine = add(mine, swap(mine, tri_size, 1)).astype(BF16)
        received, last, then_y, then_x, near_x, near_y = lax.optimization_barrier(
            (swap(mine, tri_size, 2), last, then_y, then_x, near_x, near_y)
        )
        mine = add(mine, received).astype(BF16)
        terms = [(own, 0, 0), (own, 1, 1), (own_in, 0, 0), (own_in, 1, 1)]
        terms += [(near_x, 0, 0), (near_y, 1, 0), (then_y, 0, 0), (then_x, 1, 0)]
    else:
        last = turn(ring[-1])
        terms = scatter_plain(partials[0].reshape(tri_size, 2, *amplitudes.shape[1:]), tri_size)
        mine = shift(add(hold, swap(give, tri_size, 0)).astype(BF16))
        for bit in range(1, bits):
            mine = add(mine, swap(mine, tri_size, bit)).astype(BF16)
    base = quadratic(core, [*ring, last], mine, swap(mine, tri_size, 0))
    return finish(base, terms)


def solution(mesh):
    in_specs = (P(None, "tri", "vp"), P("tri", "vp"), P("tri", None, None), P("tri"))
    out_specs = P(None, "tri", "vp")
    body = functools.partial(shards, mesh.shape["tri"], mesh.shape["vp"])
    return jax.shard_map(body, mesh=mesh, in_specs=in_specs, out_specs=out_specs, check_vma=False)
```

```python
import functools

import jax
import jax.numpy as jnp
from jax import lax
from jax.experimental import pallas as pl
from jax.experimental.pallas import tpu as pltpu
from jax.sharding import PartitionSpec as P

NB = 10
BLOCK = 768
PAIRS = NB * BLOCK
TRI_BLOCKS = NB * (NB + 1) // 2
F32 = jnp.float32
BF16 = jnp.bfloat16


def swap(value, axis_size, bit):
    pairs = [(i, i ^ (1 << bit)) for i in range(axis_size)]
    return lax.ppermute(value, "tri", pairs)


def after(value, *earlier):
    return lax.optimization_barrier((value, *earlier))[0]


def stage_kernel(source_ref, target_ref, sem):
    copy = pltpu.make_async_copy(source_ref, target_ref, sem)
    copy.start()
    copy.wait()


def stage(value):
    return pl.pallas_call(
        stage_kernel,
        in_specs=[pl.BlockSpec(memory_space=pl.ANY)],
        out_specs=pl.BlockSpec(memory_space=pltpu.VMEM),
        out_shape=jax.ShapeDtypeStruct(value.shape, value.dtype),
        scratch_shapes=[pltpu.SemaphoreType.DMA],
        compiler_params=pltpu.CompilerParams(vmem_limit_bytes=16 * 1024 * 1024),
        cost_estimate=pl.CostEstimate(flops=0, bytes_accessed=4 * value.size, transcendentals=0),
        name="stage",
    )(value)


def gather_tri(amplitudes, small, axis_size):
    if axis_size != 8:
        found = {0: amplitudes}
        for bit in range(axis_size.bit_length() - 1):
            for mask in list(found):
                found[mask | (1 << bit)] = swap(found[mask], axis_size, bit)
        return [(value, mask, None) for mask, value in found.items()], small
    by_x = swap(amplitudes, axis_size, 1)
    by_y = swap(amplitudes, axis_size, 2)
    own_core = swap(amplitudes, axis_size, 0)
    own = stage(amplitudes)
    by_x, by_y, small, _ = lax.optimization_barrier((by_x, by_y, small, own))
    far_real = swap(by_y[0], axis_size, 1)
    far_imag = swap(by_x[1], axis_size, 2)
    found = [
        (own, 0, None), (by_x, 2, None), (by_y, 4, None), (far_real, 6, 0), (far_imag, 6, 1),
        (own_core, 1, None),
    ]
    for value, mask, part in found[1:5]:
        found.append((swap(value, axis_size, 0), mask | 1, part))
    return found, small


def ladder_kernel(labels, groups, small_ref, *refs):
    count = len(labels)
    piece_refs = refs[:count]
    ladder_ref = refs[count]
    out_refs = refs[count + 1:-4]
    amp, acc, blocks, sems = refs[-4:]
    columns = amp.shape[1] // 2
    rows = out_refs[0].shape[-2]
    step = pl.program_id(0)
    me = small_ref[0]

    def rows_of(mask):
        return pl.ds(pl.multiple_of((me ^ mask) * rows, rows), rows)

    halves = BLOCK // 2

    def fetch(slot, side):
        span = pl.ds(side * halves, halves)
        return pltpu.make_async_copy(ladder_ref.at[slot, span], blocks.at[slot, span], sems.at[slot, side])

    @pl.when(step == 0)
    def _():
        for slot in range(blocks.shape[0]):
            for side in range(2):
                fetch(slot, side).start()
        for ref, (mask, part) in zip(piece_refs, labels, strict=True):
            for which in (0, 1) if part is None else (part,):
                value = ref[which] if part is None else ref[...]
                amp[rows_of(mask), which * columns:(which + 1) * columns] = value
        acc[...] = jnp.zeros_like(acc)

    code = small_ref[1 + step]
    row_block = jnp.int32(0)
    start = jnp.int32(0)
    for row in range(1, NB):
        first = row * NB - row * (row - 1) // 2
        past = code >= first
        row_block = jnp.where(past, row, row_block)
        start = jnp.where(past, first, start)
    column_block = jnp.minimum(row_block + code - start, NB - 1)
    weight = jnp.where(row_block == column_block, 0.5, 1.0) * jnp.where(code < TRI_BLOCKS, 1.0, 0.0)
    at_row = pl.ds(pl.multiple_of(row_block * BLOCK, BLOCK), BLOCK)
    at_column = pl.ds(pl.multiple_of(column_block * BLOCK, BLOCK), BLOCK)
    weight = weight.astype(BF16)
    for side in range(2):
        fetch(step, side).wait()
    block = blocks[step]
    column_amp, row_amp = weight * amp[at_column, :], weight * amp[at_row, :]
    chunk = BLOCK // 3
    for first in range(0, BLOCK, chunk):
        span = slice(first, first + chunk)
        here = pl.ds(pl.multiple_of(row_block * BLOCK + first, chunk), chunk)
        acc[here, :] += jnp.dot(block[span], column_amp, preferred_element_type=F32)
        here = pl.ds(pl.multiple_of(column_block * BLOCK + first, chunk), chunk)
        acc[here, :] += lax.dot_general(
            block[:, span], row_amp, (((0,), (0,)), ((), ())), preferred_element_type=F32
        )

    @pl.when(step == pl.num_programs(0) - 1)
    def _():
        for target, places in zip(out_refs, groups, strict=True):
            for place, (mask, part) in enumerate(places):
                lanes = slice(part * columns, (part + 1) * columns)
                target[place] = acc[rows_of(mask), lanes].astype(BF16)


def ladder(small, pieces, ladder_blocks, groups):
    slots = ladder_blocks.shape[0]
    rows, columns = pieces[0][0].shape[-2:]
    return pl.pallas_call(
        functools.partial(ladder_kernel, [(mask, part) for _, mask, part in pieces], groups),
        grid_spec=pltpu.PrefetchScalarGridSpec(
            num_scalar_prefetch=1,
            grid=(slots,),
            in_specs=[pl.BlockSpec(memory_space=pltpu.VMEM)] * len(pieces) + [pl.BlockSpec(memory_space=pl.ANY)],
            out_specs=[pl.BlockSpec((len(places), rows, columns), lambda s, *_: (0, 0, 0)) for places in groups],
            scratch_shapes=[
                pltpu.VMEM((PAIRS, 2 * columns), BF16),
                pltpu.VMEM((PAIRS, 2 * columns), F32),
                pltpu.VMEM(ladder_blocks.shape, BF16),
                pltpu.SemaphoreType.DMA((slots, 2)),
            ],
        ),
        out_shape=[jax.ShapeDtypeStruct((len(places), rows, columns), BF16) for places in groups],
        compiler_params=pltpu.CompilerParams(
            dimension_semantics=("arbitrary",), vmem_limit_bytes=48 * 1024 * 1024
        ),
        cost_estimate=pl.CostEstimate(
            flops=slots * 8 * BLOCK * BLOCK * columns,
            bytes_accessed=slots * BLOCK * BLOCK * 2 + 8 * PAIRS * columns,
            transcendentals=0,
        ),
        name="ladder",
    )(small, *[value for value, _, _ in pieces], ladder_blocks)


def add(*terms):
    total = terms[0].astype(F32)
    for term in terms[1:]:
        total = total + term.astype(F32)
    return total


def contract_kernel(core_ref, int_ref, last_ref, *refs):
    columns = int_ref.shape[1]
    hold_ref, give_ref = refs[-2:]
    for step in range(len(refs) - 1):
        values, ref = (int_ref, refs[step]) if step < len(refs) - 2 else (last_ref, refs[0])
        both = jnp.concatenate([ref[0], ref[1]], axis=1)
        product = lax.dot_general(values[...], both, (((0,), (0,)), ((), ())), preferred_element_type=F32)
        real = product[:, :columns].astype(BF16)
        imag = product[:, columns:].astype(BF16)
        hold_ref[step] = jnp.where(core_ref[0] == 0, real, imag)
        give_ref[step] = jnp.where(core_ref[0] == 0, imag, real)


def contract(core, integrals, back_integrals, ring):
    rows, columns = integrals.shape
    vmem = pl.BlockSpec(memory_space=pltpu.VMEM)
    count = len(ring) + 1
    return pl.pallas_call(
        contract_kernel,
        in_specs=[pl.BlockSpec(memory_space=pltpu.SMEM)] + [vmem] * (2 + len(ring)),
        out_specs=[vmem] * 2,
        out_shape=[jax.ShapeDtypeStruct((count, columns, columns), BF16)] * 2,
        compiler_params=pltpu.CompilerParams(vmem_limit_bytes=20 * 1024 * 1024),
        cost_estimate=pl.CostEstimate(
            flops=4 * count * rows * columns * columns,
            bytes_accessed=4 * count * rows * columns,
            transcendentals=0,
        ),
        name="contract",
    )(core, integrals, back_integrals, *ring)


def quadratic_kernel(core_ref, mine_ref, other_ref, *refs):
    amp_ref, out_ref = refs[0], refs[-1]
    _, rows, columns = amp_ref.shape
    vp_size = len(refs) - 1
    core = core_ref[0]
    total = jnp.zeros((rows, 2 * columns), F32)
    for step in range(vp_size):
        both = jnp.concatenate([refs[step][0], refs[step][1]], axis=1)
        source = (vp_size - step) % vp_size
        real = jnp.where(core == 0, mine_ref[source], other_ref[source])
        imag = jnp.where(core == 0, other_ref[source], mine_ref[source])
        weights = jnp.concatenate(
            [jnp.concatenate([real, imag], axis=1), jnp.concatenate([-imag, real], axis=1)], axis=0
        )
        total += jnp.dot(both, weights, preferred_element_type=F32)
    out_ref[0] = amp_ref[0].astype(F32) + 0.25 * total[:, columns:]
    out_ref[1] = amp_ref[1].astype(F32) - 0.25 * total[:, :columns]


def quadratic(core, ring, mine, other):
    vmem = pl.BlockSpec(memory_space=pltpu.VMEM)
    size = ring[0].size
    return pl.pallas_call(
        quadratic_kernel,
        in_specs=[pl.BlockSpec(memory_space=pltpu.SMEM)] + [vmem] * (2 + len(ring)),
        out_specs=vmem,
        out_shape=jax.ShapeDtypeStruct(ring[0].shape, F32),
        compiler_params=pltpu.CompilerParams(vmem_limit_bytes=20 * 1024 * 1024),
        cost_estimate=pl.CostEstimate(
            flops=4 * len(ring) * size * ring[0].shape[2],
            bytes_accessed=(2 * len(ring) + 4) * size,
            transcendentals=0,
        ),
        name="quadratic",
    )(core, mine, other, *ring)


def finish_kernel(places, base_ref, *refs):
    sums = [0.0, 0.0]
    for ref, (_, part, place) in zip(refs, places, strict=False):
        sums[part] = sums[part] + ref[place].astype(F32)
    refs[-1][0] = (base_ref[0] + 0.5 * sums[1]).astype(BF16)
    refs[-1][1] = (base_ref[1] - 0.5 * sums[0]).astype(BF16)


def finish(base, terms):
    vmem = pl.BlockSpec(memory_space=pltpu.VMEM)
    return pl.pallas_call(
        functools.partial(finish_kernel, [(None, part, place) for _, part, place in terms]),
        in_specs=[vmem] * (1 + len(terms)),
        out_specs=vmem,
        out_shape=jax.ShapeDtypeStruct(base.shape, BF16),
        compiler_params=pltpu.CompilerParams(vmem_limit_bytes=20 * 1024 * 1024),
        name="finish",
    )(base, *[value for value, _, _ in terms])


def scatter_plain(partial, tri_size):
    terms = [partial]
    for bit in reversed(range(tri_size.bit_length() - 1)):
        half = terms[0].shape[0] // 2
        outgoing = add(*[term[half:] for term in terms]).astype(BF16)
        terms = [term[:half] for term in terms] + [swap(outgoing, tri_size, bit)]
    return [(term[0], part, part) for term in terms for part in range(2)]


def shards(tri_size, vp_size, amplitudes, integrals, ladder_blocks, slot_block):
    bits = tri_size.bit_length() - 1
    me = lax.axis_index("tri").astype(jnp.int32)[None]
    core = me & 1
    order = list(range(0, vp_size, 2)) + list(range(1, vp_size, 2))[::-1]

    def turn(value, distance=1):
        return lax.ppermute(value, "vp", [(order[i], order[(i + distance) % vp_size]) for i in range(vp_size)])

    ring = [amplitudes]
    for _ in range(2, vp_size):
        ring.append(turn(ring[-1]))
    back_integrals = turn(integrals)
    pieces, small = gather_tri(amplitudes, jnp.concatenate([me, slot_block]), tri_size)
    small = after(small, ring[1], back_integrals)
    ring[0] = pieces[0][0]

    if tri_size == 8:
        real_order, imag_order = (2, 6, 4), (4, 6, 2)
        groups = [[(mask | 1, 0) for mask in real_order], [(mask | 1, 1) for mask in imag_order], [(1, 0), (1, 1)]]
        groups += [[(mask, 0) for mask in real_order], [(mask, 1) for mask in imag_order], [(0, 0), (0, 1)]]
    else:
        groups = [[(mask, part) for mask in range(tri_size) for part in range(2)]]
    partials = ladder(small, pieces, ladder_blocks, groups)
    *partials, ring[-1] = lax.optimization_barrier((*partials, ring[-1]))
    hold, give = contract(core, integrals, back_integrals, ring)

    def shift(value):
        moved = [turn(value[step], vp_size - step) for step in range(1, vp_size - 1)]
        return jnp.stack([value[0], *moved, value[vp_size - 1]])

    if tri_size == 8:
        real, imag, own = partials[3:]
        real_in, imag_in, own_in = (swap(value, tri_size, 0) for value in partials[:3])
        real_in, imag_in, hold, give = lax.optimization_barrier((real_in, imag_in, hold, give))
        far_x, far_y, near_x, near_y = (
            add(kept[i], came[i]).astype(BF16)[None]
            for i, kept, came in ((1, real, real_in), (1, imag, imag_in), (0, real, real_in), (0, imag, imag_in))
        )
        far_x, far_y, near_x, near_y, hold, give = lax.optimization_barrier(
            (far_x, far_y, near_x, near_y, hold, give)
        )
        far_x, far_y = swap(far_x, tri_size, 1), swap(far_y, tri_size, 2)
        near_x, near_y = swap(near_x, tri_size, 1), swap(near_y, tri_size, 2)
        mine = shift(add(hold, swap(give, tri_size, 0)).astype(BF16))
        mine, far_x, far_y = lax.optimization_barrier((mine, far_x, far_y))
        last = turn(after(ring[-1], mine))
        then_y = swap(add(real[2], real_in[2], far_x[0]).astype(BF16)[None], tri_size, 2)
        then_x = swap(add(imag[2], imag_in[2], far_y[0]).astype(BF16)[None], tri_size, 1)
        mine = add(mine, swap(mine, tri_size, 1)).astype(BF16)
        received, last, then_y, then_x, near_x, near_y = lax.optimization_barrier(
            (swap(mine, tri_size, 2), last, then_y, then_x, near_x, near_y)
        )
        mine = add(mine, received).astype(BF16)
        terms = [(own, 0, 0), (own, 1, 1), (own_in, 0, 0), (own_in, 1, 1)]
        terms += [(near_x, 0, 0), (near_y, 1, 0), (then_y, 0, 0), (then_x, 1, 0)]
    else:
        last = turn(ring[-1])
        terms = scatter_plain(partials[0].reshape(tri_size, 2, *amplitudes.shape[1:]), tri_size)
        mine = shift(add(hold, swap(give, tri_size, 0)).astype(BF16))
        for bit in range(1, bits):
            mine = add(mine, swap(mine, tri_size, bit)).astype(BF16)
    base = quadratic(core, [*ring, last], mine, swap(mine, tri_size, 0))
    return finish(base, terms)


def solution(mesh):
    in_specs = (P(None, "tri", "vp"), P("tri", "vp"), P("tri", None, None), P("tri"))
    out_specs = P(None, "tri", "vp")
    body = functools.partial(shards, mesh.shape["tri"], mesh.shape["vp"])
    return jax.shard_map(body, mesh=mesh, in_specs=in_specs, out_specs=out_specs, check_vma=False)
```

```python
import functools

import jax
import jax.numpy as jnp
from jax import lax
from jax.experimental import pallas as pl
from jax.experimental.pallas import tpu as pltpu
from jax.sharding import PartitionSpec as P

NB = 10
BLOCK = 768
PAIRS = NB * BLOCK
TRI_BLOCKS = NB * (NB + 1) // 2
F32 = jnp.float32
BF16 = jnp.bfloat16


def swap(value, axis_size, bit):
    pairs = [(i, i ^ (1 << bit)) for i in range(axis_size)]
    return lax.ppermute(value, "tri", pairs)


def after(value, *earlier):
    return lax.optimization_barrier((value, *earlier))[0]


def stage_kernel(source_ref, target_ref, sem):
    copy = pltpu.make_async_copy(source_ref, target_ref, sem)
    copy.start()
    copy.wait()


def stage(value):
    return pl.pallas_call(
        stage_kernel,
        in_specs=[pl.BlockSpec(memory_space=pl.ANY)],
        out_specs=pl.BlockSpec(memory_space=pltpu.VMEM),
        out_shape=jax.ShapeDtypeStruct(value.shape, value.dtype),
        scratch_shapes=[pltpu.SemaphoreType.DMA],
        compiler_params=pltpu.CompilerParams(vmem_limit_bytes=16 * 1024 * 1024),
        cost_estimate=pl.CostEstimate(flops=0, bytes_accessed=4 * value.size, transcendentals=0),
        name="stage",
    )(value)


def gather_tri(amplitudes, small, axis_size):
    if axis_size != 8:
        found = {0: amplitudes}
        for bit in range(axis_size.bit_length() - 1):
            for mask in list(found):
                found[mask | (1 << bit)] = swap(found[mask], axis_size, bit)
        return [(value, mask, None) for mask, value in found.items()], small
    by_x = swap(amplitudes, axis_size, 1)
    by_y = swap(amplitudes, axis_size, 2)
    own_core = swap(amplitudes, axis_size, 0)
    own = stage(amplitudes)
    by_x, by_y, small, _ = lax.optimization_barrier((by_x, by_y, small, own))
    far_real = swap(by_y[0], axis_size, 1)
    far_imag = swap(by_x[1], axis_size, 2)
    found = [
        (own, 0, None), (by_x, 2, None), (by_y, 4, None), (far_real, 6, 0), (far_imag, 6, 1),
        (own_core, 1, None),
    ]
    for value, mask, part in found[1:5]:
        found.append((swap(value, axis_size, 0), mask | 1, part))
    return found, small


def ladder_kernel(labels, groups, small_ref, *refs):
    count = len(labels)
    piece_refs = refs[:count]
    ladder_ref = refs[count]
    out_refs = refs[count + 1:-4]
    amp, acc, blocks, sems = refs[-4:]
    columns = amp.shape[1] // 2
    rows = out_refs[0].shape[-2]
    step = pl.program_id(0)
    me = small_ref[0]

    def rows_of(mask):
        return pl.ds(pl.multiple_of((me ^ mask) * rows, rows), rows)

    halves = BLOCK // 2

    def fetch(slot, side):
        span = pl.ds(side * halves, halves)
        return pltpu.make_async_copy(ladder_ref.at[slot, span], blocks.at[slot, span], sems.at[slot, side])

    @pl.when(step == 0)
    def _():
        for slot in range(blocks.shape[0]):
            for side in range(2):
                fetch(slot, side).start()
        for ref, (mask, part) in zip(piece_refs, labels, strict=True):
            for which in (0, 1) if part is None else (part,):
                value = ref[which] if part is None else ref[...]
                amp[rows_of(mask), which * columns:(which + 1) * columns] = value
        acc[...] = jnp.zeros_like(acc)

    code = small_ref[1 + step]
    row_block = jnp.int32(0)
    start = jnp.int32(0)
    for row in range(1, NB):
        first = row * NB - row * (row - 1) // 2
        past = code >= first
        row_block = jnp.where(past, row, row_block)
        start = jnp.where(past, first, start)
    column_block = jnp.minimum(row_block + code - start, NB - 1)
    weight = jnp.where(row_block == column_block, 0.5, 1.0) * jnp.where(code < TRI_BLOCKS, 1.0, 0.0)
    at_row = pl.ds(pl.multiple_of(row_block * BLOCK, BLOCK), BLOCK)
    at_column = pl.ds(pl.multiple_of(column_block * BLOCK, BLOCK), BLOCK)
    weight = weight.astype(BF16)
    for side in range(2):
        fetch(step, side).wait()
    block = blocks[step]
    column_amp, row_amp = weight * amp[at_column, :], weight * amp[at_row, :]
    chunk = BLOCK // 3
    for first in range(0, BLOCK, chunk):
        span = slice(first, first + chunk)
        here = pl.ds(pl.multiple_of(row_block * BLOCK + first, chunk), chunk)
        acc[here, :] += jnp.dot(block[span], column_amp, preferred_element_type=F32)
        here = pl.ds(pl.multiple_of(column_block * BLOCK + first, chunk), chunk)
        acc[here, :] += lax.dot_general(
            block[:, span], row_amp, (((0,), (0,)), ((), ())), preferred_element_type=F32
        )

    @pl.when(step == pl.num_programs(0) - 1)
    def _():
        for target, places in zip(out_refs, groups, strict=True):
            for place, (mask, part) in enumerate(places):
                lanes = slice(part * columns, (part + 1) * columns)
                target[place] = acc[rows_of(mask), lanes].astype(BF16)


def ladder(small, pieces, ladder_blocks, groups):
    slots = ladder_blocks.shape[0]
    rows, columns = pieces[0][0].shape[-2:]
    return pl.pallas_call(
        functools.partial(ladder_kernel, [(mask, part) for _, mask, part in pieces], groups),
        grid_spec=pltpu.PrefetchScalarGridSpec(
            num_scalar_prefetch=1,
            grid=(slots,),
            in_specs=[pl.BlockSpec(memory_space=pltpu.VMEM)] * len(pieces) + [pl.BlockSpec(memory_space=pl.ANY)],
            out_specs=[pl.BlockSpec((len(places), rows, columns), lambda s, *_: (0, 0, 0)) for places in groups],
            scratch_shapes=[
                pltpu.VMEM((PAIRS, 2 * columns), BF16),
                pltpu.VMEM((PAIRS, 2 * columns), F32),
                pltpu.VMEM(ladder_blocks.shape, BF16),
                pltpu.SemaphoreType.DMA((slots, 2)),
            ],
        ),
        out_shape=[jax.ShapeDtypeStruct((len(places), rows, columns), BF16) for places in groups],
        compiler_params=pltpu.CompilerParams(
            dimension_semantics=("arbitrary",), vmem_limit_bytes=40 * 1024 * 1024
        ),
        cost_estimate=pl.CostEstimate(
            flops=slots * 8 * BLOCK * BLOCK * columns,
            bytes_accessed=slots * BLOCK * BLOCK * 2 + 8 * PAIRS * columns,
            transcendentals=0,
        ),
        name="ladder",
    )(small, *[value for value, _, _ in pieces], ladder_blocks)


def add(*terms):
    total = terms[0].astype(F32)
    for term in terms[1:]:
        total = total + term.astype(F32)
    return total


def contract_kernel(core_ref, int_ref, last_ref, *refs):
    columns = int_ref.shape[1]
    hold_ref, give_ref = refs[-2:]
    for step in range(len(refs) - 1):
        values, ref = (int_ref, refs[step]) if step < len(refs) - 2 else (last_ref, refs[0])
        both = jnp.concatenate([ref[0], ref[1]], axis=1)
        product = lax.dot_general(values[...], both, (((0,), (0,)), ((), ())), preferred_element_type=F32)
        real = product[:, :columns].astype(BF16)
        imag = product[:, columns:].astype(BF16)
        hold_ref[step] = jnp.where(core_ref[0] == 0, real, imag)
        give_ref[step] = jnp.where(core_ref[0] == 0, imag, real)


def contract(core, integrals, back_integrals, ring):
    rows, columns = integrals.shape
    vmem = pl.BlockSpec(memory_space=pltpu.VMEM)
    count = len(ring) + 1
    return pl.pallas_call(
        contract_kernel,
        in_specs=[pl.BlockSpec(memory_space=pltpu.SMEM)] + [vmem] * (2 + len(ring)),
        out_specs=[vmem] * 2,
        out_shape=[jax.ShapeDtypeStruct((count, columns, columns), BF16)] * 2,
        compiler_params=pltpu.CompilerParams(vmem_limit_bytes=20 * 1024 * 1024),
        cost_estimate=pl.CostEstimate(
            flops=4 * count * rows * columns * columns,
            bytes_accessed=4 * count * rows * columns,
            transcendentals=0,
        ),
        name="contract",
    )(core, integrals, back_integrals, *ring)


def quadratic_kernel(core_ref, mine_ref, other_ref, base_ref, *refs):
    out_ref = refs[-1]
    _, rows, columns = base_ref.shape
    vp_size = len(refs) - 1
    core = core_ref[0]
    total = jnp.zeros((rows, 2 * columns), F32)
    for step in range(vp_size):
        both = jnp.concatenate([refs[step][0], refs[step][1]], axis=1)
        source = (vp_size - step) % vp_size
        real = jnp.where(core == 0, mine_ref[source], other_ref[source])
        imag = jnp.where(core == 0, other_ref[source], mine_ref[source])
        weights = jnp.concatenate(
            [jnp.concatenate([real, imag], axis=1), jnp.concatenate([-imag, real], axis=1)], axis=0
        )
        total += jnp.dot(both, weights, preferred_element_type=F32)
    out_ref[0] = (base_ref[0] + 0.25 * total[:, columns:]).astype(BF16)
    out_ref[1] = (base_ref[1] - 0.25 * total[:, :columns]).astype(BF16)


def quadratic(core, ring, mine, other, base):
    vmem = pl.BlockSpec(memory_space=pltpu.VMEM)
    size = ring[0].size
    return pl.pallas_call(
        quadratic_kernel,
        in_specs=[pl.BlockSpec(memory_space=pltpu.SMEM)] + [vmem] * (3 + len(ring)),
        out_specs=vmem,
        out_shape=jax.ShapeDtypeStruct(base.shape, BF16),
        compiler_params=pltpu.CompilerParams(vmem_limit_bytes=20 * 1024 * 1024),
        cost_estimate=pl.CostEstimate(
            flops=4 * len(ring) * size * base.shape[2],
            bytes_accessed=(2 * len(ring) + 6) * size,
            transcendentals=0,
        ),
        name="quadratic",
    )(core, mine, other, base, *ring)


def combine_kernel(places, amp_ref, *refs):
    sums = [0.0, 0.0]
    for ref, (part, place) in zip(refs, places, strict=False):
        sums[part] = sums[part] + ref[place].astype(F32)
    refs[-1][0] = amp_ref[0].astype(F32) + 0.5 * sums[1]
    refs[-1][1] = amp_ref[1].astype(F32) - 0.5 * sums[0]


def combine(amplitudes, terms):
    vmem = pl.BlockSpec(memory_space=pltpu.VMEM)
    return pl.pallas_call(
        functools.partial(combine_kernel, [(part, place) for _, part, place in terms]),
        in_specs=[vmem] * (1 + len(terms)),
        out_specs=vmem,
        out_shape=jax.ShapeDtypeStruct(amplitudes.shape, F32),
        compiler_params=pltpu.CompilerParams(vmem_limit_bytes=20 * 1024 * 1024),
        name="combine",
    )(amplitudes, *[value for value, _, _ in terms])


def scatter_plain(partial, tri_size):
    terms = [partial]
    for bit in reversed(range(tri_size.bit_length() - 1)):
        half = terms[0].shape[0] // 2
        outgoing = add(*[term[half:] for term in terms]).astype(BF16)
        terms = [term[:half] for term in terms] + [swap(outgoing, tri_size, bit)]
    return [(term[0], part, part) for term in terms for part in range(2)]


def shards(tri_size, vp_size, amplitudes, integrals, ladder_blocks, slot_block):
    bits = tri_size.bit_length() - 1
    me = lax.axis_index("tri").astype(jnp.int32)[None]
    core = me & 1
    order = list(range(0, vp_size, 2)) + list(range(1, vp_size, 2))[::-1]

    def turn(value, distance=1):
        return lax.ppermute(value, "vp", [(order[i], order[(i + distance) % vp_size]) for i in range(vp_size)])

    ring = [amplitudes]
    for _ in range(2, vp_size):
        ring.append(turn(ring[-1]))
    back_integrals = turn(integrals)
    pieces, small = gather_tri(amplitudes, jnp.concatenate([me, slot_block]), tri_size)
    small = after(small, ring[1], back_integrals)
    ring[0] = pieces[0][0]

    if tri_size == 8:
        real_order, imag_order = (2, 6, 4), (4, 6, 2)
        groups = [[(mask | 1, 0) for mask in real_order], [(mask | 1, 1) for mask in imag_order], [(1, 0), (1, 1)]]
        groups += [[(mask, 0) for mask in real_order], [(mask, 1) for mask in imag_order], [(0, 0), (0, 1)]]
    else:
        groups = [[(mask, part) for mask in range(tri_size) for part in range(2)]]
    partials = ladder(small, pieces, ladder_blocks, groups)
    *partials, ring[-1] = lax.optimization_barrier((*partials, ring[-1]))
    hold, give = contract(core, integrals, back_integrals, ring)

    def shift(value):
        moved = [turn(value[step], vp_size - step) for step in range(1, vp_size - 1)]
        return jnp.stack([value[0], *moved, value[vp_size - 1]])

    if tri_size == 8:
        real, imag, own = partials[3:]
        real_in, imag_in, own_in = (swap(value, tri_size, 0) for value in partials[:3])
        real_in, imag_in, hold, give = lax.optimization_barrier((real_in, imag_in, hold, give))
        far_x, far_y, near_x, near_y = (
            add(kept[i], came[i]).astype(BF16)[None]
            for i, kept, came in ((1, real, real_in), (1, imag, imag_in), (0, real, real_in), (0, imag, imag_in))
        )
        far_x, far_y, near_x, near_y, hold, give = lax.optimization_barrier(
            (far_x, far_y, near_x, near_y, hold, give)
        )
        far_x, far_y = swap(far_x, tri_size, 1), swap(far_y, tri_size, 2)
        near_x, near_y = swap(near_x, tri_size, 1), swap(near_y, tri_size, 2)
        mine = shift(add(hold, swap(give, tri_size, 0)).astype(BF16))
        mine, far_x, far_y, last = lax.optimization_barrier((mine, far_x, far_y, turn(ring[-1])))
        then_y = swap(add(real[2], real_in[2], far_x[0]).astype(BF16)[None], tri_size, 2)
        then_x = swap(add(imag[2], imag_in[2], far_y[0]).astype(BF16)[None], tri_size, 1)
        mine = add(mine, swap(mine, tri_size, 1)).astype(BF16)
        received, then_y, then_x, near_x, near_y = lax.optimization_barrier(
            (swap(mine, tri_size, 2), then_y, then_x, near_x, near_y)
        )
        mine = add(mine, received).astype(BF16)
        terms = [(own, 0, 0), (own, 1, 1), (own_in, 0, 0), (own_in, 1, 1)]
        terms += [(near_x, 0, 0), (near_y, 1, 0), (then_y, 0, 0), (then_x, 1, 0)]
    else:
        last = turn(ring[-1])
        terms = scatter_plain(partials[0].reshape(tri_size, 2, *amplitudes.shape[1:]), tri_size)
        mine = shift(add(hold, swap(give, tri_size, 0)).astype(BF16))
        for bit in range(1, bits):
            mine = add(mine, swap(mine, tri_size, bit)).astype(BF16)
    base = combine(ring[0], terms)
    return quadratic(core, [*ring, last], mine, swap(mine, tri_size, 0), base)


def solution(mesh):
    in_specs = (P(None, "tri", "vp"), P("tri", "vp"), P("tri", None, None), P("tri"))
    out_specs = P(None, "tri", "vp")
    body = functools.partial(shards, mesh.shape["tri"], mesh.shape["vp"])
    return jax.shard_map(body, mesh=mesh, in_specs=in_specs, out_specs=out_specs, check_vma=False)
```

```python
import functools

import jax
import jax.numpy as jnp
from jax import lax
from jax.experimental import pallas as pl
from jax.experimental.pallas import tpu as pltpu
from jax.sharding import PartitionSpec as P

NB = 10
BLOCK = 768
PAIRS = NB * BLOCK
TRI_BLOCKS = NB * (NB + 1) // 2
F32 = jnp.float32
BF16 = jnp.bfloat16


def swap(value, axis_size, bit):
    pairs = [(i, i ^ (1 << bit)) for i in range(axis_size)]
    return lax.ppermute(value, "tri", pairs)


def after(value, *earlier):
    return lax.optimization_barrier((value, *earlier))[0]


def stage_kernel(source_ref, target_ref, sem):
    copy = pltpu.make_async_copy(source_ref, target_ref, sem)
    copy.start()
    copy.wait()


def stage(value):
    return pl.pallas_call(
        stage_kernel,
        in_specs=[pl.BlockSpec(memory_space=pl.ANY)],
        out_specs=pl.BlockSpec(memory_space=pltpu.VMEM),
        out_shape=jax.ShapeDtypeStruct(value.shape, value.dtype),
        scratch_shapes=[pltpu.SemaphoreType.DMA],
        compiler_params=pltpu.CompilerParams(vmem_limit_bytes=16 * 1024 * 1024),
        cost_estimate=pl.CostEstimate(flops=0, bytes_accessed=4 * value.size, transcendentals=0),
        name="stage",
    )(value)


def gather_tri(amplitudes, small, axis_size):
    if axis_size != 8:
        found = {0: amplitudes}
        for bit in range(axis_size.bit_length() - 1):
            for mask in list(found):
                found[mask | (1 << bit)] = swap(found[mask], axis_size, bit)
        return [(value, mask, None) for mask, value in found.items()], small
    by_x = swap(amplitudes, axis_size, 1)
    by_y = swap(amplitudes, axis_size, 2)
    own_core = swap(amplitudes, axis_size, 0)
    own = stage(amplitudes)
    by_x, by_y, small, _ = lax.optimization_barrier((by_x, by_y, small, own))
    far_real = swap(by_y[0], axis_size, 1)
    far_imag = swap(by_x[1], axis_size, 2)
    found = [
        (own, 0, None), (by_x, 2, None), (by_y, 4, None), (far_real, 6, 0), (far_imag, 6, 1),
        (own_core, 1, None),
    ]
    for value, mask, part in found[1:5]:
        found.append((swap(value, axis_size, 0), mask | 1, part))
    return found, small


def ladder_kernel(labels, groups, small_ref, *refs):
    count = len(labels)
    piece_refs = refs[:count]
    ladder_ref = refs[count]
    out_refs = refs[count + 1:-4]
    amp, acc, blocks, sems = refs[-4:]
    columns = amp.shape[1] // 2
    rows = out_refs[0].shape[-2]
    step = pl.program_id(0)
    me = small_ref[0]

    def rows_of(mask):
        return pl.ds(pl.multiple_of((me ^ mask) * rows, rows), rows)

    halves = BLOCK // 2

    def fetch(slot, side):
        span = pl.ds(side * halves, halves)
        return pltpu.make_async_copy(ladder_ref.at[slot, span], blocks.at[slot, span], sems.at[slot, side])

    @pl.when(step == 0)
    def _():
        for slot in range(blocks.shape[0]):
            for side in range(2):
                fetch(slot, side).start()
        for ref, (mask, part) in zip(piece_refs, labels, strict=True):
            for which in (0, 1) if part is None else (part,):
                value = ref[which] if part is None else ref[...]
                amp[rows_of(mask), which * columns:(which + 1) * columns] = value
        acc[...] = jnp.zeros_like(acc)

    code = small_ref[1 + step]
    row_block = jnp.int32(0)
    start = jnp.int32(0)
    for row in range(1, NB):
        first = row * NB - row * (row - 1) // 2
        past = code >= first
        row_block = jnp.where(past, row, row_block)
        start = jnp.where(past, first, start)
    column_block = jnp.minimum(row_block + code - start, NB - 1)
    weight = jnp.where(row_block == column_block, 0.5, 1.0) * jnp.where(code < TRI_BLOCKS, 1.0, 0.0)
    at_row = pl.ds(pl.multiple_of(row_block * BLOCK, BLOCK), BLOCK)
    at_column = pl.ds(pl.multiple_of(column_block * BLOCK, BLOCK), BLOCK)
    weight = weight.astype(BF16)
    for side in range(2):
        fetch(step, side).wait()
    block = blocks[step]
    column_amp, row_amp = weight * amp[at_column, :], weight * amp[at_row, :]
    chunk = BLOCK // 3
    for first in range(0, BLOCK, chunk):
        span = slice(first, first + chunk)
        here = pl.ds(pl.multiple_of(row_block * BLOCK + first, chunk), chunk)
        acc[here, :] += jnp.dot(block[span], column_amp, preferred_element_type=F32)
        here = pl.ds(pl.multiple_of(column_block * BLOCK + first, chunk), chunk)
        acc[here, :] += lax.dot_general(
            block[:, span], row_amp, (((0,), (0,)), ((), ())), preferred_element_type=F32
        )

    @pl.when(step == pl.num_programs(0) - 1)
    def _():
        for target, places in zip(out_refs, groups, strict=True):
            for place, (mask, part) in enumerate(places):
                lanes = slice(part * columns, (part + 1) * columns)
                target[place] = acc[rows_of(mask), lanes].astype(BF16)


def ladder(small, pieces, ladder_blocks, groups):
    slots = ladder_blocks.shape[0]
    rows, columns = pieces[0][0].shape[-2:]
    return pl.pallas_call(
        functools.partial(ladder_kernel, [(mask, part) for _, mask, part in pieces], groups),
        grid_spec=pltpu.PrefetchScalarGridSpec(
            num_scalar_prefetch=1,
            grid=(slots,),
            in_specs=[pl.BlockSpec(memory_space=pltpu.VMEM)] * len(pieces) + [pl.BlockSpec(memory_space=pl.ANY)],
            out_specs=[pl.BlockSpec((len(places), rows, columns), lambda s, *_: (0, 0, 0)) for places in groups],
            scratch_shapes=[
                pltpu.VMEM((PAIRS, 2 * columns), BF16),
                pltpu.VMEM((PAIRS, 2 * columns), F32),
                pltpu.VMEM(ladder_blocks.shape, BF16),
                pltpu.SemaphoreType.DMA((slots, 2)),
            ],
        ),
        out_shape=[jax.ShapeDtypeStruct((len(places), rows, columns), BF16) for places in groups],
        compiler_params=pltpu.CompilerParams(
            dimension_semantics=("arbitrary",), vmem_limit_bytes=40 * 1024 * 1024
        ),
        cost_estimate=pl.CostEstimate(
            flops=slots * BLOCK * BLOCK * columns,
            bytes_accessed=2 * PAIRS * columns,
            transcendentals=0,
        ),
        name="ladder",
    )(small, *[value for value, _, _ in pieces], ladder_blocks)


def add(*terms):
    total = terms[0].astype(F32)
    for term in terms[1:]:
        total = total + term.astype(F32)
    return total


def contract_kernel(core_ref, int_ref, last_ref, *refs):
    columns = int_ref.shape[1]
    hold_ref, give_ref = refs[-2:]
    for step in range(len(refs) - 1):
        values, ref = (int_ref, refs[step]) if step < len(refs) - 2 else (last_ref, refs[0])
        both = jnp.concatenate([ref[0], ref[1]], axis=1)
        product = lax.dot_general(values[...], both, (((0,), (0,)), ((), ())), preferred_element_type=F32)
        real = product[:, :columns].astype(BF16)
        imag = product[:, columns:].astype(BF16)
        hold_ref[step] = jnp.where(core_ref[0] == 0, real, imag)
        give_ref[step] = jnp.where(core_ref[0] == 0, imag, real)


def contract(core, integrals, back_integrals, ring):
    rows, columns = integrals.shape
    vmem = pl.BlockSpec(memory_space=pltpu.VMEM)
    count = len(ring) + 1
    return pl.pallas_call(
        contract_kernel,
        in_specs=[pl.BlockSpec(memory_space=pltpu.SMEM)] + [vmem] * (2 + len(ring)),
        out_specs=[vmem] * 2,
        out_shape=[jax.ShapeDtypeStruct((count, columns, columns), BF16)] * 2,
        compiler_params=pltpu.CompilerParams(vmem_limit_bytes=20 * 1024 * 1024),
        cost_estimate=pl.CostEstimate(
            flops=4 * count * rows * columns * columns,
            bytes_accessed=4 * count * rows * columns,
            transcendentals=0,
        ),
        name="contract",
    )(core, integrals, back_integrals, *ring)


def quadratic_kernel(core_ref, mine_ref, other_ref, base_ref, *refs):
    out_ref = refs[-1]
    _, rows, columns = base_ref.shape
    vp_size = len(refs) - 1
    core = core_ref[0]
    total = jnp.zeros((rows, 2 * columns), F32)
    for step in range(vp_size):
        both = jnp.concatenate([refs[step][0], refs[step][1]], axis=1)
        source = (vp_size - step) % vp_size
        real = jnp.where(core == 0, mine_ref[source], other_ref[source])
        imag = jnp.where(core == 0, other_ref[source], mine_ref[source])
        weights = jnp.concatenate(
            [jnp.concatenate([real, imag], axis=1), jnp.concatenate([-imag, real], axis=1)], axis=0
        )
        total += jnp.dot(both, weights, preferred_element_type=F32)
    out_ref[0] = (base_ref[0] + 0.25 * total[:, columns:]).astype(BF16)
    out_ref[1] = (base_ref[1] - 0.25 * total[:, :columns]).astype(BF16)


def quadratic(core, ring, mine, other, base):
    vmem = pl.BlockSpec(memory_space=pltpu.VMEM)
    size = ring[0].size
    return pl.pallas_call(
        quadratic_kernel,
        in_specs=[pl.BlockSpec(memory_space=pltpu.SMEM)] + [vmem] * (3 + len(ring)),
        out_specs=vmem,
        out_shape=jax.ShapeDtypeStruct(base.shape, BF16),
        compiler_params=pltpu.CompilerParams(vmem_limit_bytes=20 * 1024 * 1024),
        cost_estimate=pl.CostEstimate(
            flops=4 * len(ring) * size * base.shape[2],
            bytes_accessed=(2 * len(ring) + 6) * size,
            transcendentals=0,
        ),
        name="quadratic",
    )(core, mine, other, base, *ring)


def combine_kernel(places, amp_ref, *refs):
    sums = [0.0, 0.0]
    for ref, (part, place) in zip(refs, places, strict=False):
        sums[part] = sums[part] + ref[place].astype(F32)
    refs[-1][0] = amp_ref[0].astype(F32) + 0.5 * sums[1]
    refs[-1][1] = amp_ref[1].astype(F32) - 0.5 * sums[0]


def combine(amplitudes, terms):
    vmem = pl.BlockSpec(memory_space=pltpu.VMEM)
    return pl.pallas_call(
        functools.partial(combine_kernel, [(part, place) for _, part, place in terms]),
        in_specs=[vmem] * (1 + len(terms)),
        out_specs=vmem,
        out_shape=jax.ShapeDtypeStruct(amplitudes.shape, F32),
        compiler_params=pltpu.CompilerParams(vmem_limit_bytes=20 * 1024 * 1024),
        name="combine",
    )(amplitudes, *[value for value, _, _ in terms])


def scatter_plain(partial, tri_size):
    terms = [partial]
    for bit in reversed(range(tri_size.bit_length() - 1)):
        half = terms[0].shape[0] // 2
        outgoing = add(*[term[half:] for term in terms]).astype(BF16)
        terms = [term[:half] for term in terms] + [swap(outgoing, tri_size, bit)]
    return [(term[0], part, part) for term in terms for part in range(2)]


def shards(tri_size, vp_size, amplitudes, integrals, ladder_blocks, slot_block):
    bits = tri_size.bit_length() - 1
    me = lax.axis_index("tri").astype(jnp.int32)[None]
    core = me & 1
    order = list(range(0, vp_size, 2)) + list(range(1, vp_size, 2))[::-1]

    def turn(value, distance=1):
        return lax.ppermute(value, "vp", [(order[i], order[(i + distance) % vp_size]) for i in range(vp_size)])

    ring = [amplitudes]
    for _ in range(2, vp_size):
        ring.append(turn(ring[-1]))
    back_integrals = turn(after(integrals, ring[1]))
    pieces, small = gather_tri(amplitudes, jnp.concatenate([me, slot_block]), tri_size)
    small = after(small, ring[1])
    ring[0] = pieces[0][0]

    if tri_size == 8:
        real_order, imag_order = (2, 6, 4), (4, 6, 2)
        groups = [[(mask | 1, 0) for mask in real_order], [(mask | 1, 1) for mask in imag_order], [(1, 0), (1, 1)]]
        groups += [[(mask, 0) for mask in real_order], [(mask, 1) for mask in imag_order], [(0, 0), (0, 1)]]
    else:
        groups = [[(mask, part) for mask in range(tri_size) for part in range(2)]]
    partials = ladder(small, pieces, ladder_blocks, groups)
    *partials, ring[-1], back_integrals = lax.optimization_barrier((*partials, ring[-1], back_integrals))
    hold, give = contract(core, integrals, back_integrals, ring)

    def shift(value):
        moved = [turn(value[step], vp_size - step) for step in range(1, vp_size - 1)]
        return jnp.stack([value[0], *moved, value[vp_size - 1]])

    if tri_size == 8:
        real, imag, own = partials[3:]
        real_in, imag_in, own_in = (swap(value, tri_size, 0) for value in partials[:3])
        real_in, imag_in, hold, give = lax.optimization_barrier((real_in, imag_in, hold, give))
        far_x, far_y, near_x, near_y = (
            add(kept[i], came[i]).astype(BF16)[None]
            for i, kept, came in ((1, real, real_in), (1, imag, imag_in), (0, real, real_in), (0, imag, imag_in))
        )
        far_x, far_y, near_x, near_y, hold, give = lax.optimization_barrier(
            (far_x, far_y, near_x, near_y, hold, give)
        )
        far_x, far_y = swap(far_x, tri_size, 1), swap(far_y, tri_size, 2)
        near_x, near_y = swap(near_x, tri_size, 1), swap(near_y, tri_size, 2)
        mine = shift(add(hold, swap(give, tri_size, 0)).astype(BF16))
        mine, far_x, far_y = lax.optimization_barrier((mine, far_x, far_y))
        last = turn(after(ring[-1], mine))
        then_y = swap(add(real[2], real_in[2], far_x[0]).astype(BF16)[None], tri_size, 2)
        then_x = swap(add(imag[2], imag_in[2], far_y[0]).astype(BF16)[None], tri_size, 1)
        mine = add(mine, swap(mine, tri_size, 1)).astype(BF16)
        received, last, then_y, then_x, near_x, near_y = lax.optimization_barrier(
            (swap(mine, tri_size, 2), last, then_y, then_x, near_x, near_y)
        )
        mine = add(mine, received).astype(BF16)
        terms = [(own, 0, 0), (own, 1, 1), (own_in, 0, 0), (own_in, 1, 1)]
        terms += [(near_x, 0, 0), (near_y, 1, 0), (then_y, 0, 0), (then_x, 1, 0)]
    else:
        last = turn(ring[-1])
        terms = scatter_plain(partials[0].reshape(tri_size, 2, *amplitudes.shape[1:]), tri_size)
        mine = shift(add(hold, swap(give, tri_size, 0)).astype(BF16))
        for bit in range(1, bits):
            mine = add(mine, swap(mine, tri_size, bit)).astype(BF16)
    base = combine(ring[0], terms)
    return quadratic(core, [*ring, last], mine, swap(mine, tri_size, 0), base)


def solution(mesh):
    in_specs = (P(None, "tri", "vp"), P("tri", "vp"), P("tri", None, None), P("tri"))
    out_specs = P(None, "tri", "vp")
    body = functools.partial(shards, mesh.shape["tri"], mesh.shape["vp"])
    return jax.shard_map(body, mesh=mesh, in_specs=in_specs, out_specs=out_specs, check_vma=False)
```

```python
import functools

import jax
import jax.numpy as jnp
from jax import lax
from jax.experimental import pallas as pl
from jax.experimental.pallas import tpu as pltpu
from jax.sharding import PartitionSpec as P

NB = 10
BLOCK = 768
PAIRS = NB * BLOCK
TRI_BLOCKS = NB * (NB + 1) // 2
F32 = jnp.float32
BF16 = jnp.bfloat16


def swap(value, axis_size, bit):
    pairs = [(i, i ^ (1 << bit)) for i in range(axis_size)]
    return lax.ppermute(value, "tri", pairs)


def after(value, *earlier):
    return lax.optimization_barrier((value, *earlier))[0]


def stage_kernel(source_ref, target_ref, sem):
    copy = pltpu.make_async_copy(source_ref, target_ref, sem)
    copy.start()
    copy.wait()


def stage(value):
    return pl.pallas_call(
        stage_kernel,
        in_specs=[pl.BlockSpec(memory_space=pl.ANY)],
        out_specs=pl.BlockSpec(memory_space=pltpu.VMEM),
        out_shape=jax.ShapeDtypeStruct(value.shape, value.dtype),
        scratch_shapes=[pltpu.SemaphoreType.DMA],
        compiler_params=pltpu.CompilerParams(vmem_limit_bytes=16 * 1024 * 1024),
        cost_estimate=pl.CostEstimate(flops=0, bytes_accessed=4 * value.size, transcendentals=0),
        name="stage",
    )(value)


def gather_tri(amplitudes, small, axis_size):
    if axis_size != 8:
        found = {0: amplitudes}
        for bit in range(axis_size.bit_length() - 1):
            for mask in list(found):
                found[mask | (1 << bit)] = swap(found[mask], axis_size, bit)
        return [(value, mask, None) for mask, value in found.items()], small
    by_x = swap(amplitudes, axis_size, 1)
    by_y = swap(amplitudes, axis_size, 2)
    own_core = swap(amplitudes, axis_size, 0)
    own = stage(amplitudes)
    by_x, by_y, small, _ = lax.optimization_barrier((by_x, by_y, small, own))
    far_real = swap(by_y[0], axis_size, 1)
    far_imag = swap(by_x[1], axis_size, 2)
    found = [
        (own, 0, None), (by_x, 2, None), (by_y, 4, None), (far_real, 6, 0), (far_imag, 6, 1),
        (own_core, 1, None),
    ]
    for value, mask, part in found[1:5]:
        found.append((swap(value, axis_size, 0), mask | 1, part))
    return found, small


def ladder_kernel(labels, groups, small_ref, *refs):
    count = len(labels)
    piece_refs = refs[:count]
    ladder_ref = refs[count]
    out_refs = refs[count + 1:-4]
    amp, acc, blocks, sems = refs[-4:]
    columns = amp.shape[1] // 2
    rows = out_refs[0].shape[-2]
    step = pl.program_id(0)
    me = small_ref[0]

    def rows_of(mask):
        return pl.ds(pl.multiple_of((me ^ mask) * rows, rows), rows)

    halves = BLOCK // 2

    def fetch(slot, side):
        span = pl.ds(side * halves, halves)
        return pltpu.make_async_copy(ladder_ref.at[slot, span], blocks.at[slot, span], sems.at[slot, side])

    @pl.when(step == 0)
    def _():
        for slot in range(blocks.shape[0]):
            for side in range(2):
                fetch(slot, side).start()
        for ref, (mask, part) in zip(piece_refs, labels, strict=True):
            for which in (0, 1) if part is None else (part,):
                value = ref[which] if part is None else ref[...]
                amp[rows_of(mask), which * columns:(which + 1) * columns] = value
        acc[...] = jnp.zeros_like(acc)

    code = small_ref[1 + step]
    row_block = jnp.int32(0)
    start = jnp.int32(0)
    for row in range(1, NB):
        first = row * NB - row * (row - 1) // 2
        past = code >= first
        row_block = jnp.where(past, row, row_block)
        start = jnp.where(past, first, start)
    column_block = jnp.minimum(row_block + code - start, NB - 1)
    weight = jnp.where(row_block == column_block, 0.5, 1.0) * jnp.where(code < TRI_BLOCKS, 1.0, 0.0)
    at_row = pl.ds(pl.multiple_of(row_block * BLOCK, BLOCK), BLOCK)
    at_column = pl.ds(pl.multiple_of(column_block * BLOCK, BLOCK), BLOCK)
    weight = weight.astype(BF16)
    for side in range(2):
        fetch(step, side).wait()
    block = blocks[step]
    column_amp, row_amp = weight * amp[at_column, :], weight * amp[at_row, :]
    chunk = BLOCK // 3
    for first in range(0, BLOCK, chunk):
        span = slice(first, first + chunk)
        here = pl.ds(pl.multiple_of(row_block * BLOCK + first, chunk), chunk)
        acc[here, :] += jnp.dot(block[span], column_amp, preferred_element_type=F32)
        here = pl.ds(pl.multiple_of(column_block * BLOCK + first, chunk), chunk)
        acc[here, :] += lax.dot_general(
            block[:, span], row_amp, (((0,), (0,)), ((), ())), preferred_element_type=F32
        )

    @pl.when(step == pl.num_programs(0) - 1)
    def _():
        for target, places in zip(out_refs, groups, strict=True):
            for place, (mask, part) in enumerate(places):
                lanes = slice(part * columns, (part + 1) * columns)
                target[place] = acc[rows_of(mask), lanes].astype(BF16)


def ladder(small, pieces, ladder_blocks, groups):
    slots = ladder_blocks.shape[0]
    rows, columns = pieces[0][0].shape[-2:]
    return pl.pallas_call(
        functools.partial(ladder_kernel, [(mask, part) for _, mask, part in pieces], groups),
        grid_spec=pltpu.PrefetchScalarGridSpec(
            num_scalar_prefetch=1,
            grid=(slots,),
            in_specs=[pl.BlockSpec(memory_space=pltpu.VMEM)] * len(pieces) + [pl.BlockSpec(memory_space=pl.ANY)],
            out_specs=[pl.BlockSpec((len(places), rows, columns), lambda s, *_: (0, 0, 0)) for places in groups],
            scratch_shapes=[
                pltpu.VMEM((PAIRS, 2 * columns), BF16),
                pltpu.VMEM((PAIRS, 2 * columns), F32),
                pltpu.VMEM(ladder_blocks.shape, BF16),
                pltpu.SemaphoreType.DMA((slots, 2)),
            ],
        ),
        out_shape=[jax.ShapeDtypeStruct((len(places), rows, columns), BF16) for places in groups],
        compiler_params=pltpu.CompilerParams(
            dimension_semantics=("arbitrary",), vmem_limit_bytes=40 * 1024 * 1024
        ),
        cost_estimate=pl.CostEstimate(
            flops=slots * BLOCK * BLOCK * columns,
            bytes_accessed=2 * PAIRS * columns,
            transcendentals=0,
        ),
        name="ladder",
    )(small, *[value for value, _, _ in pieces], ladder_blocks)


def add(*terms):
    total = terms[0].astype(F32)
    for term in terms[1:]:
        total = total + term.astype(F32)
    return total


def contract_kernel(core_ref, int_ref, last_ref, *refs):
    columns = int_ref.shape[1]
    hold_ref, give_ref = refs[-2:]
    for step in range(len(refs) - 1):
        values, ref = (int_ref, refs[step]) if step < len(refs) - 2 else (last_ref, refs[0])
        both = jnp.concatenate([ref[0], ref[1]], axis=1)
        product = lax.dot_general(values[...], both, (((0,), (0,)), ((), ())), preferred_element_type=F32)
        real = product[:, :columns].astype(BF16)
        imag = product[:, columns:].astype(BF16)
        hold_ref[step] = jnp.where(core_ref[0] == 0, real, imag)
        give_ref[step] = jnp.where(core_ref[0] == 0, imag, real)


def contract(core, integrals, back_integrals, ring):
    rows, columns = integrals.shape
    vmem = pl.BlockSpec(memory_space=pltpu.VMEM)
    count = len(ring) + 1
    return pl.pallas_call(
        contract_kernel,
        in_specs=[pl.BlockSpec(memory_space=pltpu.SMEM)] + [vmem] * (2 + len(ring)),
        out_specs=[vmem] * 2,
        out_shape=[jax.ShapeDtypeStruct((count, columns, columns), BF16)] * 2,
        compiler_params=pltpu.CompilerParams(vmem_limit_bytes=20 * 1024 * 1024),
        cost_estimate=pl.CostEstimate(
            flops=4 * count * rows * columns * columns,
            bytes_accessed=4 * count * rows * columns,
            transcendentals=0,
        ),
        name="contract",
    )(core, integrals, back_integrals, *ring)


def quadratic_kernel(core_ref, mine_ref, other_ref, base_ref, *refs):
    out_ref = refs[-1]
    _, rows, columns = base_ref.shape
    vp_size = len(refs) - 1
    core = core_ref[0]
    total = jnp.zeros((rows, 2 * columns), F32)
    for step in range(vp_size):
        both = jnp.concatenate([refs[step][0], refs[step][1]], axis=1)
        source = (vp_size - step) % vp_size
        real = jnp.where(core == 0, mine_ref[source], other_ref[source])
        imag = jnp.where(core == 0, other_ref[source], mine_ref[source])
        weights = jnp.concatenate(
            [jnp.concatenate([real, imag], axis=1), jnp.concatenate([-imag, real], axis=1)], axis=0
        )
        total += jnp.dot(both, weights, preferred_element_type=F32)
    out_ref[0] = (base_ref[0] + 0.25 * total[:, columns:]).astype(BF16)
    out_ref[1] = (base_ref[1] - 0.25 * total[:, :columns]).astype(BF16)


def quadratic(core, ring, mine, other, base):
    vmem = pl.BlockSpec(memory_space=pltpu.VMEM)
    size = ring[0].size
    return pl.pallas_call(
        quadratic_kernel,
        in_specs=[pl.BlockSpec(memory_space=pltpu.SMEM)] + [vmem] * (3 + len(ring)),
        out_specs=vmem,
        out_shape=jax.ShapeDtypeStruct(base.shape, BF16),
        compiler_params=pltpu.CompilerParams(vmem_limit_bytes=20 * 1024 * 1024),
        cost_estimate=pl.CostEstimate(
            flops=4 * len(ring) * size * base.shape[2],
            bytes_accessed=(2 * len(ring) + 6) * size,
            transcendentals=0,
        ),
        name="quadratic",
    )(core, mine, other, base, *ring)


def combine_kernel(places, amp_ref, *refs):
    sums = [0.0, 0.0]
    for ref, (part, place) in zip(refs, places, strict=False):
        sums[part] = sums[part] + ref[place].astype(F32)
    refs[-1][0] = amp_ref[0].astype(F32) + 0.5 * sums[1]
    refs[-1][1] = amp_ref[1].astype(F32) - 0.5 * sums[0]


def combine(amplitudes, terms):
    vmem = pl.BlockSpec(memory_space=pltpu.VMEM)
    return pl.pallas_call(
        functools.partial(combine_kernel, [(part, place) for _, part, place in terms]),
        in_specs=[vmem] * (1 + len(terms)),
        out_specs=vmem,
        out_shape=jax.ShapeDtypeStruct(amplitudes.shape, F32),
        compiler_params=pltpu.CompilerParams(vmem_limit_bytes=20 * 1024 * 1024),
        name="combine",
    )(amplitudes, *[value for value, _, _ in terms])


def scatter_plain(partial, tri_size):
    terms = [partial]
    for bit in reversed(range(tri_size.bit_length() - 1)):
        half = terms[0].shape[0] // 2
        outgoing = add(*[term[half:] for term in terms]).astype(BF16)
        terms = [term[:half] for term in terms] + [swap(outgoing, tri_size, bit)]
    return [(term[0], part, part) for term in terms for part in range(2)]


def shards(tri_size, vp_size, amplitudes, integrals, ladder_blocks, slot_block):
    bits = tri_size.bit_length() - 1
    me = lax.axis_index("tri").astype(jnp.int32)[None]
    core = me & 1
    order = list(range(0, vp_size, 2)) + list(range(1, vp_size, 2))[::-1]

    def turn(value, distance=1):
        return lax.ppermute(value, "vp", [(order[i], order[(i + distance) % vp_size]) for i in range(vp_size)])

    ring = [amplitudes]
    for _ in range(2, vp_size):
        ring.append(turn(ring[-1]))
    back_integrals = turn(integrals)
    pieces, small = gather_tri(amplitudes, jnp.concatenate([me, slot_block]), tri_size)
    small = after(small, ring[1], back_integrals)
    ring[0] = pieces[0][0]

    if tri_size == 8:
        real_order, imag_order = (2, 6, 4), (4, 6, 2)
        groups = [[(mask | 1, 0) for mask in real_order], [(mask | 1, 1) for mask in imag_order], [(1, 0), (1, 1)]]
        groups += [[(mask, 0) for mask in real_order], [(mask, 1) for mask in imag_order], [(0, 0), (0, 1)]]
    else:
        groups = [[(mask, part) for mask in range(tri_size) for part in range(2)]]
    partials = ladder(small, pieces, ladder_blocks, groups)
    *partials, ring[-1] = lax.optimization_barrier((*partials, ring[-1]))
    hold, give = contract(core, integrals, back_integrals, ring)

    def shift(value):
        moved = [turn(value[step], vp_size - step) for step in range(1, vp_size - 1)]
        return jnp.stack([value[0], *moved, value[vp_size - 1]])

    if tri_size == 8:
        real, imag, own = partials[3:]
        real_in, imag_in, own_in = (swap(value, tri_size, 0) for value in partials[:3])
        real_in, imag_in, hold, give = lax.optimization_barrier((real_in, imag_in, hold, give))
        far_x, far_y, near_x, near_y = (
            add(kept[i], came[i]).astype(BF16)[None]
            for i, kept, came in ((1, real, real_in), (1, imag, imag_in), (0, real, real_in), (0, imag, imag_in))
        )
        far_x, far_y, near_x, near_y, hold, give = lax.optimization_barrier(
            (far_x, far_y, near_x, near_y, hold, give)
        )
        far_x, far_y = swap(far_x, tri_size, 1), swap(far_y, tri_size, 2)
        near_x, near_y = swap(near_x, tri_size, 1), swap(near_y, tri_size, 2)
        mine = shift(add(hold, swap(give, tri_size, 0)).astype(BF16))
        mine, far_x, far_y = lax.optimization_barrier((mine, far_x, far_y))
        last = turn(after(ring[-1], mine))
        then_y = swap(add(real[2], real_in[2], far_x[0]).astype(BF16)[None], tri_size, 2)
        then_x = swap(add(imag[2], imag_in[2], far_y[0]).astype(BF16)[None], tri_size, 1)
        mine = add(mine, swap(mine, tri_size, 1)).astype(BF16)
        received, last, then_y, then_x, near_x, near_y = lax.optimization_barrier(
            (swap(mine, tri_size, 2), last, then_y, then_x, near_x, near_y)
        )
        mine = add(mine, received).astype(BF16)
        terms = [(own, 0, 0), (own, 1, 1), (own_in, 0, 0), (own_in, 1, 1)]
        terms += [(near_x, 0, 0), (near_y, 1, 0), (then_y, 0, 0), (then_x, 1, 0)]
    else:
        last = turn(ring[-1])
        terms = scatter_plain(partials[0].reshape(tri_size, 2, *amplitudes.shape[1:]), tri_size)
        mine = shift(add(hold, swap(give, tri_size, 0)).astype(BF16))
        for bit in range(1, bits):
            mine = add(mine, swap(mine, tri_size, bit)).astype(BF16)
    base = combine(ring[0], terms)
    return quadratic(core, [*ring, last], mine, swap(mine, tri_size, 0), base)


def solution(mesh):
    in_specs = (P(None, "tri", "vp"), P("tri", "vp"), P("tri", None, None), P("tri"))
    out_specs = P(None, "tri", "vp")
    body = functools.partial(shards, mesh.shape["tri"], mesh.shape["vp"])
    return jax.shard_map(body, mesh=mesh, in_specs=in_specs, out_specs=out_specs, check_vma=False)
```

```python
import functools

import jax
import jax.numpy as jnp
from jax import lax
from jax.experimental import pallas as pl
from jax.experimental.pallas import tpu as pltpu
from jax.sharding import PartitionSpec as P

NB = 10
BLOCK = 768
PAIRS = NB * BLOCK
TRI_BLOCKS = NB * (NB + 1) // 2
F32 = jnp.float32
BF16 = jnp.bfloat16


def swap(value, axis_size, bit):
    pairs = [(i, i ^ (1 << bit)) for i in range(axis_size)]
    return lax.ppermute(value, "tri", pairs)


def after(value, *earlier):
    return lax.optimization_barrier((value, *earlier))[0]


def stage_kernel(source_ref, target_ref, sem):
    copy = pltpu.make_async_copy(source_ref, target_ref, sem)
    copy.start()
    copy.wait()


def stage(value):
    return pl.pallas_call(
        stage_kernel,
        in_specs=[pl.BlockSpec(memory_space=pl.ANY)],
        out_specs=pl.BlockSpec(memory_space=pltpu.VMEM),
        out_shape=jax.ShapeDtypeStruct(value.shape, value.dtype),
        scratch_shapes=[pltpu.SemaphoreType.DMA],
        compiler_params=pltpu.CompilerParams(vmem_limit_bytes=16 * 1024 * 1024),
        cost_estimate=pl.CostEstimate(flops=0, bytes_accessed=4 * value.size, transcendentals=0),
        name="stage",
    )(value)


def gather_tri(amplitudes, small, axis_size):
    if axis_size != 8:
        found = {0: amplitudes}
        for bit in range(axis_size.bit_length() - 1):
            for mask in list(found):
                found[mask | (1 << bit)] = swap(found[mask], axis_size, bit)
        return [(value, mask, None) for mask, value in found.items()], small
    by_x = swap(amplitudes, axis_size, 1)
    by_y = swap(amplitudes, axis_size, 2)
    own_core = swap(amplitudes, axis_size, 0)
    own = stage(amplitudes)
    by_x, by_y, small, _ = lax.optimization_barrier((by_x, by_y, small, own))
    far_real = swap(by_y[0], axis_size, 1)
    far_imag = swap(by_x[1], axis_size, 2)
    found = [
        (own, 0, None), (by_x, 2, None), (by_y, 4, None), (far_real, 6, 0), (far_imag, 6, 1),
        (own_core, 1, None),
    ]
    for value, mask, part in found[1:5]:
        found.append((swap(value, axis_size, 0), mask | 1, part))
    return found, small


def ladder_kernel(labels, groups, small_ref, *refs):
    count = len(labels)
    piece_refs = refs[:count]
    ladder_ref = refs[count]
    out_refs = refs[count + 1:-4]
    amp, acc, blocks, sems = refs[-4:]
    columns = amp.shape[1] // 2
    rows = out_refs[0].shape[-2]
    step = pl.program_id(0)
    me = small_ref[0]

    def rows_of(mask):
        return pl.ds(pl.multiple_of((me ^ mask) * rows, rows), rows)

    halves = BLOCK // 2

    def fetch(slot, side):
        span = pl.ds(side * halves, halves)
        return pltpu.make_async_copy(ladder_ref.at[slot, span], blocks.at[slot, span], sems.at[slot, side])

    @pl.when(step == 0)
    def _():
        for slot in range(blocks.shape[0]):
            for side in range(2):
                fetch(slot, side).start()
        for ref, (mask, part) in zip(piece_refs, labels, strict=True):
            for which in (0, 1) if part is None else (part,):
                value = ref[which] if part is None else ref[...]
                amp[rows_of(mask), which * columns:(which + 1) * columns] = value
        acc[...] = jnp.zeros_like(acc)

    code = small_ref[1 + step]
    row_block = jnp.int32(0)
    start = jnp.int32(0)
    for row in range(1, NB):
        first = row * NB - row * (row - 1) // 2
        past = code >= first
        row_block = jnp.where(past, row, row_block)
        start = jnp.where(past, first, start)
    column_block = jnp.minimum(row_block + code - start, NB - 1)
    weight = jnp.where(row_block == column_block, 0.5, 1.0) * jnp.where(code < TRI_BLOCKS, 1.0, 0.0)
    at_row = pl.ds(pl.multiple_of(row_block * BLOCK, BLOCK), BLOCK)
    at_column = pl.ds(pl.multiple_of(column_block * BLOCK, BLOCK), BLOCK)
    weight = weight.astype(BF16)
    for side in range(2):
        fetch(step, side).wait()
    block = blocks[step]
    column_amp, row_amp = weight * amp[at_column, :], weight * amp[at_row, :]
    chunk = BLOCK // 3
    for first in range(0, BLOCK, chunk):
        span = slice(first, first + chunk)
        here = pl.ds(pl.multiple_of(row_block * BLOCK + first, chunk), chunk)
        acc[here, :] += jnp.dot(block[span], column_amp, preferred_element_type=F32)
        here = pl.ds(pl.multiple_of(column_block * BLOCK + first, chunk), chunk)
        acc[here, :] += lax.dot_general(
            block[:, span], row_amp, (((0,), (0,)), ((), ())), preferred_element_type=F32
        )

    @pl.when(step == pl.num_programs(0) - 1)
    def _():
        for target, places in zip(out_refs, groups, strict=True):
            for place, (mask, part) in enumerate(places):
                lanes = slice(part * columns, (part + 1) * columns)
                target[place] = acc[rows_of(mask), lanes].astype(BF16)


def ladder(small, pieces, ladder_blocks, groups):
    slots = ladder_blocks.shape[0]
    rows, columns = pieces[0][0].shape[-2:]
    return pl.pallas_call(
        functools.partial(ladder_kernel, [(mask, part) for _, mask, part in pieces], groups),
        grid_spec=pltpu.PrefetchScalarGridSpec(
            num_scalar_prefetch=1,
            grid=(slots,),
            in_specs=[pl.BlockSpec(memory_space=pltpu.VMEM)] * len(pieces) + [pl.BlockSpec(memory_space=pl.ANY)],
            out_specs=[pl.BlockSpec((len(places), rows, columns), lambda s, *_: (0, 0, 0)) for places in groups],
            scratch_shapes=[
                pltpu.VMEM((PAIRS, 2 * columns), BF16),
                pltpu.VMEM((PAIRS, 2 * columns), F32),
                pltpu.VMEM(ladder_blocks.shape, BF16),
                pltpu.SemaphoreType.DMA((slots, 2)),
            ],
        ),
        out_shape=[jax.ShapeDtypeStruct((len(places), rows, columns), BF16) for places in groups],
        compiler_params=pltpu.CompilerParams(
            dimension_semantics=("arbitrary",), vmem_limit_bytes=40 * 1024 * 1024
        ),
        cost_estimate=pl.CostEstimate(
            flops=slots * BLOCK * BLOCK * columns,
            bytes_accessed=2 * PAIRS * columns,
            transcendentals=0,
        ),
        name="ladder",
    )(small, *[value for value, _, _ in pieces], ladder_blocks)


def add(*terms):
    total = terms[0].astype(F32)
    for term in terms[1:]:
        total = total + term.astype(F32)
    return total


def contract_kernel(core_ref, int_ref, last_ref, *refs):
    columns = int_ref.shape[1]
    hold_ref, give_ref = refs[-2:]
    for step in range(len(refs) - 1):
        values, ref = (int_ref, refs[step]) if step < len(refs) - 2 else (last_ref, refs[0])
        both = jnp.concatenate([ref[0], ref[1]], axis=1)
        product = lax.dot_general(values[...], both, (((0,), (0,)), ((), ())), preferred_element_type=F32)
        real = product[:, :columns].astype(BF16)
        imag = product[:, columns:].astype(BF16)
        hold_ref[step] = jnp.where(core_ref[0] == 0, real, imag)
        give_ref[step] = jnp.where(core_ref[0] == 0, imag, real)


def contract(core, integrals, back_integrals, ring):
    rows, columns = integrals.shape
    vmem = pl.BlockSpec(memory_space=pltpu.VMEM)
    count = len(ring) + 1
    return pl.pallas_call(
        contract_kernel,
        in_specs=[pl.BlockSpec(memory_space=pltpu.SMEM)] + [vmem] * (2 + len(ring)),
        out_specs=[vmem] * 2,
        out_shape=[jax.ShapeDtypeStruct((count, columns, columns), BF16)] * 2,
        compiler_params=pltpu.CompilerParams(vmem_limit_bytes=20 * 1024 * 1024),
        cost_estimate=pl.CostEstimate(
            flops=4 * count * rows * columns * columns,
            bytes_accessed=4 * count * rows * columns,
            transcendentals=0,
        ),
        name="contract",
    )(core, integrals, back_integrals, *ring)


def quadratic_kernel(core_ref, mine_ref, other_ref, base_ref, *refs):
    out_ref = refs[-1]
    _, rows, columns = base_ref.shape
    vp_size = len(refs) - 1
    core = core_ref[0]
    total = jnp.zeros((rows, 2 * columns), F32)
    for step in range(vp_size):
        both = jnp.concatenate([refs[step][0], refs[step][1]], axis=1)
        source = (vp_size - step) % vp_size
        real = jnp.where(core == 0, mine_ref[source], other_ref[source])
        imag = jnp.where(core == 0, other_ref[source], mine_ref[source])
        weights = jnp.concatenate(
            [jnp.concatenate([real, imag], axis=1), jnp.concatenate([-imag, real], axis=1)], axis=0
        )
        total += jnp.dot(both, weights, preferred_element_type=F32)
    out_ref[0] = (base_ref[0] + 0.25 * total[:, columns:]).astype(BF16)
    out_ref[1] = (base_ref[1] - 0.25 * total[:, :columns]).astype(BF16)


def quadratic(core, ring, mine, other, base):
    vmem = pl.BlockSpec(memory_space=pltpu.VMEM)
    size = ring[0].size
    return pl.pallas_call(
        quadratic_kernel,
        in_specs=[pl.BlockSpec(memory_space=pltpu.SMEM)] + [vmem] * (3 + len(ring)),
        out_specs=vmem,
        out_shape=jax.ShapeDtypeStruct(base.shape, BF16),
        compiler_params=pltpu.CompilerParams(vmem_limit_bytes=20 * 1024 * 1024),
        cost_estimate=pl.CostEstimate(
            flops=4 * len(ring) * size * base.shape[2],
            bytes_accessed=(2 * len(ring) + 6) * size,
            transcendentals=0,
        ),
        name="quadratic",
    )(core, mine, other, base, *ring)


def combine_kernel(places, amp_ref, *refs):
    sums = [0.0, 0.0]
    for ref, (part, place) in zip(refs, places, strict=False):
        sums[part] = sums[part] + ref[place].astype(F32)
    refs[-1][0] = amp_ref[0].astype(F32) + 0.5 * sums[1]
    refs[-1][1] = amp_ref[1].astype(F32) - 0.5 * sums[0]


def combine(amplitudes, terms):
    vmem = pl.BlockSpec(memory_space=pltpu.VMEM)
    return pl.pallas_call(
        functools.partial(combine_kernel, [(part, place) for _, part, place in terms]),
        in_specs=[vmem] * (1 + len(terms)),
        out_specs=vmem,
        out_shape=jax.ShapeDtypeStruct(amplitudes.shape, F32),
        compiler_params=pltpu.CompilerParams(vmem_limit_bytes=20 * 1024 * 1024),
        name="combine",
    )(amplitudes, *[value for value, _, _ in terms])


def scatter_plain(partial, tri_size):
    terms = [partial]
    for bit in reversed(range(tri_size.bit_length() - 1)):
        half = terms[0].shape[0] // 2
        outgoing = add(*[term[half:] for term in terms]).astype(BF16)
        terms = [term[:half] for term in terms] + [swap(outgoing, tri_size, bit)]
    return [(term[0], part, part) for term in terms for part in range(2)]


def shards(tri_size, vp_size, amplitudes, integrals, ladder_blocks, slot_block):
    bits = tri_size.bit_length() - 1
    me = lax.axis_index("tri").astype(jnp.int32)[None]
    core = me & 1
    order = list(range(0, vp_size, 2)) + list(range(1, vp_size, 2))[::-1]

    def turn(value, distance=1):
        return lax.ppermute(value, "vp", [(order[i], order[(i + distance) % vp_size]) for i in range(vp_size)])

    ring = [amplitudes]
    for _ in range(2, vp_size):
        ring.append(turn(ring[-1]))
    back_integrals = turn(integrals)
    pieces, small = gather_tri(amplitudes, jnp.concatenate([me, slot_block]), tri_size)
    small = after(small, ring[1], back_integrals)
    ring[0] = pieces[0][0]

    if tri_size == 8:
        far, rest, mine = [(6, 0), (6, 1)], [(2, 0), (4, 1), (4, 0), (2, 1)], [(0, 0), (0, 1)]
        groups = [[(mask | 1, part) for mask, part in places] for places in (far, rest, mine)] + [far, rest, mine]
    else:
        groups = [[(mask, part) for mask in range(tri_size) for part in range(2)]]
    partials = ladder(small, pieces, ladder_blocks, groups)
    *partials, ring[-1] = lax.optimization_barrier((*partials, ring[-1]))
    hold, give = contract(core, integrals, back_integrals, ring)

    def shift(value):
        moved = [turn(value[step], vp_size - step) for step in range(1, vp_size - 1)]
        return jnp.stack([value[0], *moved, value[vp_size - 1]])

    if tri_size == 8:
        far, rest, own = partials[3:]
        far_in, rest_in, own_in = (swap(value, tri_size, 0) for value in partials[:3])
        far_in, hold, give = lax.optimization_barrier((far_in, hold, give))
        far_x, far_y = (add(far[i], far_in[i]).astype(BF16)[None] for i in range(2))
        far_x, far_y, hold, give = lax.optimization_barrier((far_x, far_y, hold, give))
        near_x, near_y = (add(rest[i], rest_in[i]).astype(BF16)[None] for i in range(2))
        far_x, far_y = swap(far_x, tri_size, 1), swap(far_y, tri_size, 2)
        mine = add(hold, swap(give, tri_size, 0)).astype(BF16)
        near_x, near_y, mine = lax.optimization_barrier((near_x, near_y, mine))
        near_x, near_y = swap(near_x, tri_size, 1), swap(near_y, tri_size, 2)
        mine = shift(mine)
        mine, far_x, far_y = lax.optimization_barrier((mine, far_x, far_y))
        last = turn(after(ring[-1], mine))
        then_y = swap(add(rest[2], rest_in[2], far_x[0]).astype(BF16)[None], tri_size, 2)
        then_x = swap(add(rest[3], rest_in[3], far_y[0]).astype(BF16)[None], tri_size, 1)
        mine = add(mine, swap(mine, tri_size, 1)).astype(BF16)
        received, last, then_y, then_x, near_x, near_y = lax.optimization_barrier(
            (swap(mine, tri_size, 2), last, then_y, then_x, near_x, near_y)
        )
        mine = add(mine, received).astype(BF16)
        terms = [(own, 0, 0), (own, 1, 1), (own_in, 0, 0), (own_in, 1, 1)]
        terms += [(near_x, 0, 0), (near_y, 1, 0), (then_y, 0, 0), (then_x, 1, 0)]
    else:
        last = turn(ring[-1])
        terms = scatter_plain(partials[0].reshape(tri_size, 2, *amplitudes.shape[1:]), tri_size)
        mine = shift(add(hold, swap(give, tri_size, 0)).astype(BF16))
        for bit in range(1, bits):
            mine = add(mine, swap(mine, tri_size, bit)).astype(BF16)
    base = combine(ring[0], terms)
    return quadratic(core, [*ring, last], mine, swap(mine, tri_size, 0), base)


def solution(mesh):
    in_specs = (P(None, "tri", "vp"), P("tri", "vp"), P("tri", None, None), P("tri"))
    out_specs = P(None, "tri", "vp")
    body = functools.partial(shards, mesh.shape["tri"], mesh.shape["vp"])
    return jax.shard_map(body, mesh=mesh, in_specs=in_specs, out_specs=out_specs, check_vma=False)
```
